32 devices in a mesh: seq: 16 (over z, x, core), mp: 2 (over y).
Axes of the slice: x: 2, y: 2, z: 4, core: 2. Of those that a mesh axis runs over, the one named last changes fastest.
Arguments:
- queries: bfloat16 [8192, 4096], P(('seq', 'mp')), may hold values from -6 to 6
- memory_keys: bfloat16 [128, 4096], P('seq', 'mp'), may hold values from -6 to 6
- memory_values: bfloat16 [128, 4096], P('seq', 'mp'), may hold values from -48 to 48
- output_grad: bfloat16 [8192, 4096], P(('seq', 'mp')), may hold values from -24 to 24
Outputs:
- attended: bfloat16 [8192, 4096], P(('seq', 'mp'))
- query_grad: bfloat16 [8192, 4096], P(('seq', 'mp'))
- key_grad: bfloat16 [128, 4096], P('seq', 'mp')
- value_grad: bfloat16 [128, 4096], P('seq', 'mp')
The draws below stay inside these ranges and needn't reach their ends.
All inputs are finite; a program needn't handle non-finite values.
Results may differ from the reference program's by a relative error of at most 0.012.
The reference program's roundings to bfloat16 on the way (of `attention_weights` and `score_grad`) count: a program that leaves them out, or rounds other values in their place, can miss the bound.
Values may be sent and summed in bfloat16 or wider, within the bound.
No kernel may reach another device: no remote copies, remote signals or barrier semaphores. Data moves between devices by JAX's collectives and lax.ppermute only.
A program may use at most 64 MiB of HBM per device.

```python
import math
import jax
import jax.numpy as jnp
from jax import lax

DH = 128
FEATURES = 4096
LENGTH = 8192
MEMORY = 128


def draw_memory_keys(key, part):
    key = jax.random.fold_in(key, 7)
    base = jnp.clip(jax.random.normal(key, (MEMORY, FEATURES), jnp.float32), -4.0, 4.0)
    return base.astype(jnp.bfloat16)


def draw_queries(key, part):
    key = jax.random.fold_in(key, 5)
    base = jnp.clip(jax.random.normal(key, (LENGTH, FEATURES), jnp.float32), -4.0, 4.0)
    return base.astype(jnp.bfloat16)


def block_scale(key, extent, shards, least, top_value):
    level, own = 1.0, jax.random.fold_in(key, 6)
    for dim, blocks in shards:
        steps = jnp.exp(jax.random.uniform(jax.random.fold_in(own, dim), (blocks,), jnp.float32, least / len(shards), top_value / len(shards)))
        level = level * jnp.repeat(steps, extent[dim] // blocks).reshape([-1 if axis == dim else 1 for axis in range(len(extent))])
    return level


def noise(own_key, dims, spread, limit, split=(), dtype=jnp.bfloat16):
    level = block_scale(own_key, dims, split, -0.22, 0.18) if split else 1.0
    array = jax.random.normal(own_key, dims, jnp.float32) * spread * level
    return jnp.minimum(jnp.maximum(array, -limit), limit).astype(dtype)


def setup_inputs(seed: int = 0) -> dict:
    arg_keys = jax.random.split(jax.random.key(seed), 5)
    queries = draw_queries(jax.random.fold_in(arg_keys[4], 71), 0)
    memory_keys = draw_memory_keys(jax.random.fold_in(arg_keys[4], 71), 0)
    memory_values = noise(arg_keys[2], (MEMORY, FEATURES), 8.0, 48.0, ((0, 16), (1, 2)))
    output_grad = noise(arg_keys[3], (LENGTH, FEATURES), 4.0, 24.0, ((0, 32),))
    return dict(queries=queries, memory_keys=memory_keys, memory_values=memory_values, output_grad=output_grad)


def split_heads(matrix, head_width):
    row_count = matrix.shape[0]
    return matrix.reshape(row_count, -1, head_width).transpose(1, 0, 2)

def join_heads(stacked):
    head_count, row_count, head_width = stacked.shape
    return stacked.transpose(1, 0, 2).reshape(row_count, head_count * head_width)

def forward_head(query_rows, key_rows, value_rows):
    temper = 1.0 / math.sqrt(query_rows.shape[1])
    scores = jnp.dot(query_rows, key_rows.T, preferred_element_type=jnp.float32) * temper
    peak_score = lax.optimization_barrier(jnp.max(scores, axis=1, keepdims=True))
    log_total = peak_score + jnp.log(lax.optimization_barrier(jnp.sum(jnp.exp(scores - peak_score), axis=1, keepdims=True)))
    attention_weights = jnp.exp(scores - log_total).astype(jnp.bfloat16)
    attended = jnp.dot(attention_weights, value_rows, preferred_element_type=jnp.float32).astype(jnp.bfloat16)
    return (attended, log_total)

def backward_head(query_rows, key_rows, value_rows, grad_rows, attended, log_total):
    temper = 1.0 / math.sqrt(query_rows.shape[1])
    scores = jnp.dot(query_rows, key_rows.T, preferred_element_type=jnp.float32) * temper
    exact_weights = jnp.exp(scores - log_total)
    attention_weights = exact_weights.astype(jnp.bfloat16)
    row_delta = lax.optimization_barrier(jnp.sum(grad_rows.astype(jnp.float32) * attended.astype(jnp.float32), axis=1, keepdims=True))
    prob_grad = jnp.dot(grad_rows, value_rows.T, preferred_element_type=jnp.float32)
    score_grad = (exact_weights * (prob_grad - row_delta) * temper).astype(jnp.bfloat16)
    query_grad = jnp.dot(score_grad, key_rows, preferred_element_type=jnp.float32).astype(jnp.bfloat16)
    key_grad = jnp.dot(score_grad.T, query_rows, preferred_element_type=jnp.float32)
    value_grad = jnp.dot(attention_weights.T, grad_rows, preferred_element_type=jnp.float32)
    return (query_grad, key_grad, value_grad)

def one_head(operands):
    query_rows, key_rows, value_rows, grad_rows = operands
    attended, log_total = forward_head(query_rows, key_rows, value_rows)
    query_grad, key_grad, value_grad = backward_head(query_rows, key_rows, value_rows, grad_rows, attended, log_total)
    return (attended, query_grad, key_grad.astype(jnp.bfloat16), value_grad.astype(jnp.bfloat16))

def reference(queries, memory_keys, memory_values, output_grad):
    stacked = (split_heads(queries, DH), split_heads(memory_keys, DH), split_heads(memory_values, DH), split_heads(output_grad, DH))
    attended, query_grad, key_grad, value_grad = lax.map(one_head, stacked)
    return (join_heads(attended), join_heads(query_grad), join_heads(key_grad), join_heads(value_grad))
```

```python
import functools
import math

import jax
import jax.numpy as jnp
from jax import lax
from jax.experimental import pallas as pl
from jax.experimental.pallas import tpu as pltpu
from jax.sharding import PartitionSpec as P

DH = 128

NT = (((1,), (1,)), ((), ()))
NN = (((1,), (0,)), ((), ()))

bf16, f32 = jnp.bfloat16, jnp.float32


def dot(a, b, dims):
    return lax.dot_general(a, b, dims, preferred_element_type=f32)


def softmax_part(raw, prob_grad):
    temper = 1.0 / math.sqrt(DH)
    peak = jnp.max(raw, axis=0, keepdims=True)
    powers = jnp.exp2((raw - peak) * (temper * math.log2(math.e)))
    inverse = 1.0 / jnp.sum(powers, axis=0, keepdims=True)
    delta = jnp.sum(powers * prob_grad, axis=0, keepdims=True) * inverse
    weights = (powers * inverse).astype(bf16)
    score_grad = (powers * (inverse * temper) * (prob_grad - delta)).astype(bf16)
    return score_grad, weights


def columns(n_mp, blocks, block, width, of_sibling):
    core, my = lax.axis_index("seq") & 1, lax.axis_index("mp")
    core = 1 - core if of_sibling else core
    return lambda r: pl.multiple_of((((my ^ r) * 2 + core) * blocks + block) * width, width)


def attention_kernel(n_mp, blocks, block, rs, n_memory, q_ref, g_ref, sq_ref, sg_ref, *refs):
    memory_refs, refs = refs[:n_memory], refs[-10 - n_memory :]
    (attended_ref, query_grad_ref, sibling_ref), term_refs = refs[:3], refs[3:-7]
    token_buf, result_buf, raw_ref, prob_ref, grad_ref, weight_ref, sems = refs[-7:]
    count, width = q_ref.shape[0], term_refs[0].shape[1] // 2
    heads, group = width // DH, min(2 * DH, width)
    parts = width // group
    size = memory_refs[0].shape[0] // len(rs)
    column = columns(n_mp, blocks, block, width, False)
    step = min(DH, 2 * count)
    cols = [slice(n * DH, (n + 1) * DH) for n in range(heads)]
    targets = [[slice(m * width + n * DH, m * width + (n + 1) * DH) for n in range(heads)] for m in (0, 1)]

    def inputs(k, part):
        begin = part * group
        where = pl.ds(pl.multiple_of(column(rs[0] + k) + begin, group), group)
        return [
            pltpu.make_async_copy(
                array.at[:, where],
                token_buf.at[k, m, pl.ds(n * count, count), pl.ds(begin, group)],
                sems.at[0, k, part, m, n],
            )
            for m, pair in enumerate(((q_ref, sq_ref), (g_ref, sg_ref)))
            for n, array in enumerate(pair)
        ]

    def outputs(k, part):
        begin = part * group
        copies = []
        for m, own in enumerate((query_grad_ref, attended_ref)):
            starts = (column(rs[0] + k), (2 * (rs[0] + k) + m) * width)
            for n, (array, start) in enumerate(zip((own, sibling_ref), starts)):
                copies.append(
                    pltpu.make_async_copy(
                        result_buf.at[k, m, pl.ds(n * count, count), pl.ds(begin, group)],
                        array.at[:, pl.ds(pl.multiple_of(start + begin, group), group)],
                        sems.at[1, k, part, m, n],
                    )
                )
        return copies

    def every(action):
        def at(k, _):
            for part in range(parts):
                for copy in action(k, part):
                    copy()

        repeat(at)

    def repeat(body):
        if len(rs) == 1:
            body(0, None)
        else:
            lax.fori_loop(0, len(rs), body, None)

    def work(k, _):
        rows = pl.ds(pl.multiple_of(k * size, size), size)
        memory = [[jnp.concatenate([ref[rows, t] for ref in memory_refs], axis=0) for t in row] for row in targets]
        for n in range(heads):
            if n * DH % group == 0:
                for copy in inputs(k, n * DH // group):
                    copy.wait()
            raw_ref[n] = dot(memory[0][n], token_buf[k, 0, :, cols[n]], NT)
            prob_ref[n] = dot(memory[1][n], token_buf[k, 1, :, cols[n]], NT)
        for n in range(heads):
            for begin in range(0, 2 * count, step):
                part = slice(begin, begin + step)
                grad_ref[n, :, part], weight_ref[n, :, part] = softmax_part(raw_ref[n, :, part], prob_ref[n, :, part])
        for n in range(heads):
            for m, pair_ref in enumerate((grad_ref, weight_ref)):
                result_buf[k, m, :, cols[n]] = dot(memory[m][n].T, pair_ref[n], NN).astype(bf16).T
            if (n + 1) * DH % group == 0:
                for copy in outputs(k, n * DH // group):
                    copy.start()
        for n in range(heads):
            for m, pair_ref in enumerate((grad_ref, weight_ref)):
                term = dot(pair_ref[n], token_buf[k, m, :, cols[n]], NN)
                for i, term_ref in enumerate(term_refs):
                    term_ref[rows, targets[m][n]] = term[i * size : (i + 1) * size].astype(term_ref.dtype)

    every(lambda k, part: [copy.start for copy in inputs(k, part)])
    repeat(work)
    every(lambda k, part: [copy.wait for copy in outputs(k, part)])


def pinned(space, *arrays):
    return [pltpu.with_memory_space_constraint(array, space) for array in arrays]


HBM, VMEM = pl.BlockSpec(memory_space=pltpu.HBM), pl.BlockSpec(memory_space=pltpu.VMEM)


def attention(n_mp, blocks, block, rs, tokens, memory, types, outputs, sent):
    rows, whole = tokens[0].shape
    width = memory[0].shape[1] // 2
    count = sum(m.shape[0] for m in memory) // len(rs)
    group = min(2 * DH, width)
    scratch = (width // DH, count, 2 * rows)
    earlier = [*outputs] + ([] if sent is None else [sent])
    first = 4 + len(memory)
    return pl.pallas_call(
        functools.partial(attention_kernel, n_mp, blocks, block, rs, len(memory)),
        in_specs=[HBM] * 4 + [VMEM] * len(memory) + [HBM] * len(earlier),
        out_specs=[HBM] * 3 + [VMEM] * len(memory),
        out_shape=[jax.ShapeDtypeStruct((rows, whole), bf16)] * 2
        + [jax.ShapeDtypeStruct((rows, whole // blocks), bf16)]
        + [pltpu.VMEM(m.shape, t) for m, t in zip(memory, types)],
        scratch_shapes=[pltpu.VMEM((len(rs), 2, 2 * rows, width), bf16)] * 2
        + [pltpu.VMEM(scratch, t) for t in (f32, f32, bf16, bf16)]
        + [pltpu.SemaphoreType.DMA((2, len(rs), width // group, 2, 2))],
        input_output_aliases={first + n: n for n in range(len(earlier))},
        compiler_params=pltpu.CompilerParams(vmem_limit_bytes=32 * 1024 * 1024),
        cost_estimate=pl.CostEstimate(
            flops=24 * rows * count * width * len(rs),
            bytes_accessed=16 * rows * width * len(rs),
            transcendentals=2 * rows * count * width * len(rs) // DH,
        ),
    )(*pinned(pltpu.HBM, *tokens[:2]), *tokens[2:], *pinned(pltpu.VMEM, *memory), *earlier)


def placing_kernel(n_mp, blocks, *refs):
    returned_refs, (attended_ref, query_grad_ref, sems) = refs[:blocks], refs[-3:]
    width = returned_refs[0].shape[1] // (2 * n_mp)
    copies = []
    for block, returned_ref in enumerate(returned_refs):
        column = columns(n_mp, blocks, block, width, True)
        for r in range(n_mp):
            for m, target in enumerate((query_grad_ref, attended_ref)):
                start = (2 * r + m) * width
                copies.append(
                    pltpu.make_async_copy(
                        returned_ref.at[:, start : start + width],
                        target.at[:, pl.ds(column(r), width)],
                        sems.at[len(copies)],
                    )
                )
    for copy in copies:
        copy.start()
    for copy in copies:
        copy.wait()


def placing(n_mp, returned, attended, query_grad):
    blocks = len(returned)
    return pl.pallas_call(
        functools.partial(placing_kernel, n_mp, blocks),
        in_specs=[VMEM] * blocks + [HBM] * 2,
        out_specs=[HBM] * 2,
        out_shape=[jax.ShapeDtypeStruct(attended.shape, bf16)] * 2,
        scratch_shapes=[pltpu.SemaphoreType.DMA((2 * blocks * n_mp,))],
        input_output_aliases={blocks: 0, blocks + 1: 1},
    )(*pinned(pltpu.VMEM, *returned), attended, query_grad)


def together(*values):
    return lax.optimization_barrier(values)


def shards(n_seq, n_mp, queries, memory_keys, memory_values, output_grad):
    def swap(array, axis, bits):
        size = n_seq if axis == "seq" else n_mp
        return lax.ppermute(array, axis, [(i, i ^ bits) for i in range(size)])

    core_bit, x_bit = 1, 2
    z_bits = range(4, n_seq, 4)
    y_bits = [1 << b for b in range(n_mp.bit_length() - 1)]
    rows, part = memory_keys.shape
    share, blocks = part // 2, 2
    block = share // blocks
    core = lax.axis_index("seq") & 1

    def packed(c):
        both = [lax.dynamic_slice_in_dim(array, c * share, share, axis=1) for array in (memory_keys, memory_values)]
        return jnp.concatenate([b[:, n * block : (n + 1) * block] for n in range(blocks) for b in both], axis=1)

    base = jnp.concatenate([packed(core), swap(packed(1 - core), "seq", core_bit)])
    base, queries_out, grad_out = together(base, queries, output_grad)
    sibling_queries, sibling_grad = swap(queries_out, "seq", core_bit), swap(grad_out, "seq", core_bit)
    tokens = (queries, output_grad, sibling_queries, sibling_grad)

    got = [base] + [swap(base, "seq", bits) for bits in z_bits]
    first, second = (jnp.concatenate([g[:, n * 2 * block : (n + 1) * 2 * block] for g in got]) for n in (0, 1))

    def wider(held, got):
        return jnp.concatenate([held, got])

    first_got, second_got = together(swap(first, "seq", x_bit), swap(second, "mp", y_bits[0]))
    first, second = wider(first, first_got), wider(second, second_got)
    for bits in y_bits[:-1]:
        first = wider(first, swap(first, "mp", bits))
    for bits in y_bits[1:]:
        second = wider(second, swap(second, "mp", bits))
    first_got, second_got = swap(first, "mp", y_bits[-1]), swap(second, "seq", x_bit)

    half = n_mp // 2
    *outputs, out, first_keep = attention(n_mp, blocks, 0, range(half), tokens, [first], [f32], [], None)
    *outputs, out_first, give = attention(
        n_mp, blocks, 0, range(half, n_mp), tokens, [first_got], [bf16], outputs, out
    )
    first_got = swap(give, "mp", y_bits[-1])
    *outputs, out_second, second_keep, give = attention(
        n_mp, blocks, 1, range(n_mp), tokens, [second, second_got], [f32, bf16], outputs, None
    )
    second_got = swap(give, "seq", x_bit)
    first, second = together(first_keep + first_got.astype(f32), second_keep + second_got.astype(f32))

    def fold(total, axis, bits):
        middle = total.shape[0] // 2
        return total[:middle] + swap(total[middle:].astype(bf16), axis, bits).astype(f32)

    for bits in y_bits[-2::-1]:
        first = fold(first, "mp", bits)
    for bits in y_bits[:0:-1]:
        second = fold(second, "mp", bits)
    first, second = fold(first, "seq", x_bit), fold(second, "mp", y_bits[0])
    returned = [swap(out, "seq", core_bit) for out in (out_first, out_second)]
    first, second, returned = together(first, second, returned)
    total = jnp.concatenate([first, second], axis=1)
    outputs = placing(n_mp, returned, *outputs)
    count, give = 2 * rows, total.astype(bf16)
    got = [swap(give[n * count : (n + 1) * count], "seq", bits) for n, bits in enumerate(z_bits, 1)]
    got, outputs = together(got, outputs)
    total = (total[:count] + sum(g.astype(f32) for g in got)).astype(bf16)
    mine, other = total[:rows], swap(total[rows:], "seq", core_bit)

    def joined(m):
        a, b = (
            jnp.concatenate([t[:, (2 * n + m) * block : (2 * n + m + 1) * block] for n in range(blocks)], axis=1)
            for t in (mine, other)
        )
        whole = lax.dynamic_update_slice_in_dim(jnp.zeros((rows, part), bf16), a, core * share, axis=1)
        return lax.dynamic_update_slice_in_dim(whole, b, (1 - core) * share, axis=1)

    return (*outputs, joined(0), joined(1))


def solution(mesh):
    body = functools.partial(shards, mesh.shape["seq"], mesh.shape["mp"])
    return jax.shard_map(
        body,
        mesh=mesh,
        in_specs=(P(("seq", "mp"), None), P("seq", "mp"), P("seq", "mp"), P(("seq", "mp"), None)),
        out_specs=(P(("seq", "mp"), None), P(("seq", "mp"), None), P("seq", "mp"), P("seq", "mp")),
        check_vma=False,
    )
```

```python
import functools
import math

import jax
import jax.numpy as jnp
from jax import lax
from jax.experimental import pallas as pl
from jax.experimental.pallas import tpu as pltpu
from jax.sharding import PartitionSpec as P

DH = 128

NT = (((1,), (1,)), ((), ()))
NN = (((1,), (0,)), ((), ()))

bf16, f32 = jnp.bfloat16, jnp.float32


def dot(a, b, dims):
    return lax.dot_general(a, b, dims, preferred_element_type=f32)


def softmax_part(raw, prob_grad):
    temper = 1.0 / math.sqrt(DH)
    peak = jnp.max(raw, axis=0, keepdims=True)
    powers = jnp.exp2((raw - peak) * (temper * math.log2(math.e)))
    inverse = 1.0 / jnp.sum(powers, axis=0, keepdims=True)
    delta = jnp.sum(powers * prob_grad, axis=0, keepdims=True) * inverse
    weights = (powers * inverse).astype(bf16)
    score_grad = (powers * (inverse * temper) * (prob_grad - delta)).astype(bf16)
    return score_grad, weights


def columns(n_mp, blocks, block, width, of_sibling):
    core, my = lax.axis_index("seq") & 1, lax.axis_index("mp")
    core = 1 - core if of_sibling else core
    return lambda r: pl.multiple_of((((my ^ r) * 2 + core) * blocks + block) * width, width)


def attention_kernel(n_mp, blocks, block, rs, n_memory, q_ref, g_ref, sq_ref, sg_ref, *refs):
    memory_refs, refs = refs[:n_memory], refs[-10 - n_memory :]
    (attended_ref, query_grad_ref, sibling_ref), term_refs = refs[:3], refs[3:-7]
    token_buf, result_buf, raw_ref, prob_ref, grad_ref, weight_ref, sems = refs[-7:]
    count, width = q_ref.shape[0], term_refs[0].shape[1] // 2
    heads, group = width // DH, min(2 * DH, width)
    parts = width // group
    size = memory_refs[0].shape[0] // len(rs)
    column = columns(n_mp, blocks, block, width, False)
    step = min(DH, 2 * count)
    cols = [slice(n * DH, (n + 1) * DH) for n in range(heads)]
    targets = [[slice(m * width + n * DH, m * width + (n + 1) * DH) for n in range(heads)] for m in (0, 1)]

    def inputs(k, part):
        begin = part * group
        starts = (column(rs[0] + k) + begin, (block * n_mp + rs[0] + k) * width + begin)
        return [
            pltpu.make_async_copy(
                array.at[:, pl.ds(pl.multiple_of(starts[n], group), group)],
                token_buf.at[k, m, pl.ds(n * count, count), pl.ds(begin, group)],
                sems.at[0, k, part, m, n],
            )
            for m, pair in enumerate(((q_ref, sq_ref), (g_ref, sg_ref)))
            for n, array in enumerate(pair)
        ]

    def outputs(k, part):
        begin = part * group
        copies = []
        for m, own in enumerate((query_grad_ref, attended_ref)):
            starts = (column(rs[0] + k), (2 * (rs[0] + k) + m) * width)
            for n, (array, start) in enumerate(zip((own, sibling_ref), starts)):
                copies.append(
                    pltpu.make_async_copy(
                        result_buf.at[k, m, pl.ds(n * count, count), pl.ds(begin, group)],
                        array.at[:, pl.ds(pl.multiple_of(start + begin, group), group)],
                        sems.at[1, k, part, m, n],
                    )
                )
        return copies

    def every(action):
        def at(k, _):
            for part in range(parts):
                for copy in action(k, part):
                    copy()

        repeat(at)

    def repeat(body):
        if len(rs) == 1:
            body(0, None)
        else:
            lax.fori_loop(0, len(rs), body, None)

    def work(k, _):
        rows = pl.ds(pl.multiple_of(k * size, size), size)
        memory = [[jnp.concatenate([ref[rows, t] for ref in memory_refs], axis=0) for t in row] for row in targets]
        for n in range(heads):
            if n * DH % group == 0:
                for copy in inputs(k, n * DH // group):
                    copy.wait()
            raw_ref[n] = dot(memory[0][n], token_buf[k, 0, :, cols[n]], NT)
            prob_ref[n] = dot(memory[1][n], token_buf[k, 1, :, cols[n]], NT)
        for n in range(heads):
            for begin in range(0, 2 * count, step):
                part = slice(begin, begin + step)
                grad_ref[n, :, part], weight_ref[n, :, part] = softmax_part(raw_ref[n, :, part], prob_ref[n, :, part])
        for n in range(heads):
            for m, pair_ref in enumerate((grad_ref, weight_ref)):
                result_buf[k, m, :, cols[n]] = dot(memory[m][n].T, pair_ref[n], NN).astype(bf16).T
            if (n + 1) * DH % group == 0:
                for copy in outputs(k, n * DH // group):
                    copy.start()
        for n in range(heads):
            for m, pair_ref in enumerate((grad_ref, weight_ref)):
                term = dot(pair_ref[n], token_buf[k, m, :, cols[n]], NN)
                for i, term_ref in enumerate(term_refs):
                    term_ref[rows, targets[m][n]] = term[i * size : (i + 1) * size].astype(term_ref.dtype)

    every(lambda k, part: [copy.start for copy in inputs(k, part)])
    repeat(work)
    every(lambda k, part: [copy.wait for copy in outputs(k, part)])


def pinned(space, *arrays):
    return [pltpu.with_memory_space_constraint(array, space) for array in arrays]


HBM, VMEM = pl.BlockSpec(memory_space=pltpu.HBM), pl.BlockSpec(memory_space=pltpu.VMEM)


def attention(n_mp, blocks, block, rs, tokens, memory, types, outputs, sent):
    rows, whole = tokens[0].shape
    width = memory[0].shape[1] // 2
    count = sum(m.shape[0] for m in memory) // len(rs)
    group = min(2 * DH, width)
    scratch = (width // DH, count, 2 * rows)
    earlier = [*outputs] + ([] if sent is None else [sent])
    first = 4 + len(memory)
    return pl.pallas_call(
        functools.partial(attention_kernel, n_mp, blocks, block, rs, len(memory)),
        in_specs=[HBM] * 4 + [VMEM] * len(memory) + [HBM] * len(earlier),
        out_specs=[HBM] * 3 + [VMEM] * len(memory),
        out_shape=[jax.ShapeDtypeStruct((rows, whole), bf16)] * 2
        + [jax.ShapeDtypeStruct((rows, whole // blocks), bf16)]
        + [pltpu.VMEM(m.shape, t) for m, t in zip(memory, types)],
        scratch_shapes=[pltpu.VMEM((len(rs), 2, 2 * rows, width), bf16)] * 2
        + [pltpu.VMEM(scratch, t) for t in (f32, f32, bf16, bf16)]
        + [pltpu.SemaphoreType.DMA((2, len(rs), width // group, 2, 2))],
        input_output_aliases={first + n: n for n in range(len(earlier))},
        compiler_params=pltpu.CompilerParams(vmem_limit_bytes=32 * 1024 * 1024),
        cost_estimate=pl.CostEstimate(
            flops=24 * rows * count * width * len(rs),
            bytes_accessed=16 * rows * width * len(rs),
            transcendentals=2 * rows * count * width * len(rs) // DH,
        ),
    )(*pinned(pltpu.HBM, *tokens[:2]), *tokens[2:], *pinned(pltpu.VMEM, *memory), *earlier)


def packing_kernel(n_mp, blocks, q_ref, g_ref, packed_q_ref, packed_g_ref, sems):
    width = packed_q_ref.shape[1] // (blocks * n_mp)
    copies = []
    for block in range(blocks):
        column = columns(n_mp, blocks, block, width, True)
        for r in range(n_mp):
            where = pl.ds((block * n_mp + r) * width, width)
            for array, packed in ((q_ref, packed_q_ref), (g_ref, packed_g_ref)):
                copies.append(
                    pltpu.make_async_copy(
                        array.at[:, pl.ds(column(r), width)], packed.at[:, where], sems.at[len(copies)]
                    )
                )
    for copy in copies:
        copy.start()
    for copy in copies:
        copy.wait()


def packing(n_mp, blocks, queries, grad):
    rows, whole = queries.shape
    return pl.pallas_call(
        functools.partial(packing_kernel, n_mp, blocks),
        in_specs=[HBM] * 2,
        out_specs=[VMEM] * 2,
        out_shape=[pltpu.VMEM((rows, whole // 2), bf16)] * 2,
        scratch_shapes=[pltpu.SemaphoreType.DMA((2 * blocks * n_mp,))],
        cost_estimate=pl.CostEstimate(flops=0, bytes_accessed=4 * rows * whole, transcendentals=0),
    )(*pinned(pltpu.HBM, queries, grad))


def placing_kernel(n_mp, blocks, *refs):
    returned_refs, (attended_ref, query_grad_ref, sems) = refs[:blocks], refs[-3:]
    width = returned_refs[0].shape[1] // (2 * n_mp)
    copies = []
    for block, returned_ref in enumerate(returned_refs):
        column = columns(n_mp, blocks, block, width, True)
        for r in range(n_mp):
            for m, target in enumerate((query_grad_ref, attended_ref)):
                start = (2 * r + m) * width
                copies.append(
                    pltpu.make_async_copy(
                        returned_ref.at[:, start : start + width],
                        target.at[:, pl.ds(column(r), width)],
                        sems.at[len(copies)],
                    )
                )
    for copy in copies:
        copy.start()
    for copy in copies:
        copy.wait()


def placing(n_mp, returned, attended, query_grad):
    blocks = len(returned)
    return pl.pallas_call(
        functools.partial(placing_kernel, n_mp, blocks),
        in_specs=[VMEM] * blocks + [HBM] * 2,
        out_specs=[HBM] * 2,
        out_shape=[jax.ShapeDtypeStruct(attended.shape, bf16)] * 2,
        scratch_shapes=[pltpu.SemaphoreType.DMA((2 * blocks * n_mp,))],
        input_output_aliases={blocks: 0, blocks + 1: 1},
    )(*pinned(pltpu.VMEM, *returned), attended, query_grad)


def together(*values):
    return lax.optimization_barrier(values)


def shards(n_seq, n_mp, queries, memory_keys, memory_values, output_grad):
    def swap(array, axis, bits):
        size = n_seq if axis == "seq" else n_mp
        return lax.ppermute(array, axis, [(i, i ^ bits) for i in range(size)])

    core_bit, x_bit = 1, 2
    z_bits = range(4, n_seq, 4)
    y_bits = [1 << b for b in range(n_mp.bit_length() - 1)]
    rows, part = memory_keys.shape
    share, blocks = part // 2, 2
    block = share // blocks
    core = lax.axis_index("seq") & 1

    def packed(c):
        both = [lax.dynamic_slice_in_dim(array, c * share, share, axis=1) for array in (memory_keys, memory_values)]
        return jnp.concatenate([b[:, n * block : (n + 1) * block] for n in range(blocks) for b in both], axis=1)

    base = jnp.concatenate([packed(core), swap(packed(1 - core), "seq", core_bit)])

    got = [swap(base, "seq", bits) for bits in z_bits]
    got[0], queries_out, grad_out = together(got[0], queries, output_grad)
    tokens = (queries, output_grad)
    tokens += tuple(swap(array, "seq", core_bit) for array in packing(n_mp, blocks, queries_out, grad_out))
    got = [base] + got
    first, second = (jnp.concatenate([g[:, n * 2 * block : (n + 1) * 2 * block] for g in got]) for n in (0, 1))

    def wider(held, got):
        return jnp.concatenate([held, got])

    first_got, second_got = together(swap(first, "seq", x_bit), swap(second, "mp", y_bits[0]))
    first, second = wider(first, first_got), wider(second, second_got)
    for bits in y_bits[:-1]:
        first = wider(first, swap(first, "mp", bits))
    for bits in y_bits[1:]:
        second = wider(second, swap(second, "mp", bits))
    first_got, second_got = swap(first, "mp", y_bits[-1]), swap(second, "seq", x_bit)

    half = n_mp // 2
    *outputs, out, first_keep = attention(n_mp, blocks, 0, range(half), tokens, [first], [f32], [], None)
    *outputs, out_first, give = attention(
        n_mp, blocks, 0, range(half, n_mp), tokens, [first_got], [bf16], outputs, out
    )
    first_got = swap(give, "mp", y_bits[-1])
    *outputs, out_second, second_keep, give = attention(
        n_mp, blocks, 1, range(n_mp), tokens, [second, second_got], [f32, bf16], outputs, None
    )
    second_got = swap(give, "seq", x_bit)
    first, second = together(first_keep + first_got.astype(f32), second_keep + second_got.astype(f32))

    def fold(total, axis, bits):
        middle = total.shape[0] // 2
        return total[:middle] + swap(total[middle:].astype(bf16), axis, bits).astype(f32)

    for bits in y_bits[-2::-1]:
        first = fold(first, "mp", bits)
    for bits in y_bits[:0:-1]:
        second = fold(second, "mp", bits)
    first, second = fold(first, "seq", x_bit), fold(second, "mp", y_bits[0])
    first, second, out_first, out_second = together(first, second, out_first, out_second)
    returned = [swap(out, "seq", core_bit) for out in (out_first, out_second)]
    total = jnp.concatenate([first, second], axis=1)
    count, give = 2 * rows, total.astype(bf16)
    got = [swap(give[n * count : (n + 1) * count], "seq", bits) for n, bits in enumerate(z_bits, 1)]
    got[0], returned = together(got[0], returned)
    outputs = placing(n_mp, returned, *outputs)
    got[-1], outputs = together(got[-1], outputs)
    total = (total[:count] + sum(g.astype(f32) for g in got)).astype(bf16)
    mine, other = total[:rows], swap(total[rows:], "seq", core_bit)

    def joined(m):
        a, b = (
            jnp.concatenate([t[:, (2 * n + m) * block : (2 * n + m + 1) * block] for n in range(blocks)], axis=1)
            for t in (mine, other)
        )
        whole = lax.dynamic_update_slice_in_dim(jnp.zeros((rows, part), bf16), a, core * share, axis=1)
        return lax.dynamic_update_slice_in_dim(whole, b, (1 - core) * share, axis=1)

    return (*outputs, joined(0), joined(1))


def solution(mesh):
    body = functools.partial(shards, mesh.shape["seq"], mesh.shape["mp"])
    return jax.shard_map(
        body,
        mesh=mesh,
        in_specs=(P(("seq", "mp"), None), P("seq", "mp"), P("seq", "mp"), P(("seq", "mp"), None)),
        out_specs=(P(("seq", "mp"), None), P(("seq", "mp"), None), P("seq", "mp"), P("seq", "mp")),
        check_vma=False,
    )
```

```python
import functools
import math

import jax
import jax.numpy as jnp
from jax import lax
from jax.experimental import pallas as pl
from jax.experimental.pallas import tpu as pltpu
from jax.sharding import PartitionSpec as P

DH = 128

NT = (((1,), (1,)), ((), ()))
NN = (((1,), (0,)), ((), ()))

bf16, f32 = jnp.bfloat16, jnp.float32


def dot(a, b, dims):
    return lax.dot_general(a, b, dims, preferred_element_type=f32)


def softmax_part(raw, prob_grad):
    temper = 1.0 / math.sqrt(DH)
    peak = jnp.max(raw, axis=0, keepdims=True)
    powers = jnp.exp2((raw - peak) * (temper * math.log2(math.e)))
    inverse = 1.0 / jnp.sum(powers, axis=0, keepdims=True)
    delta = jnp.sum(powers * prob_grad, axis=0, keepdims=True) * inverse
    weights = (powers * inverse).astype(bf16)
    score_grad = (powers * (inverse * temper) * (prob_grad - delta)).astype(bf16)
    return score_grad, weights


def columns(n_mp, blocks, block, width, of_sibling):
    core, my = lax.axis_index("seq") & 1, lax.axis_index("mp")
    core = 1 - core if of_sibling else core
    return lambda r: pl.multiple_of((((my ^ r) * 2 + core) * blocks + block) * width, width)


def attention_kernel(n_mp, blocks, block, rs, n_memory, q_ref, g_ref, sq_ref, sg_ref, *refs):
    memory_refs, refs = refs[:n_memory], refs[-10 - n_memory :]
    (attended_ref, query_grad_ref, sibling_ref), term_refs = refs[:3], refs[3:-7]
    token_buf, result_buf, raw_ref, prob_ref, grad_ref, weight_ref, sems = refs[-7:]
    count, width = q_ref.shape[0], term_refs[0].shape[1] // 2
    heads = width // DH
    size = memory_refs[0].shape[0] // len(rs)
    column = columns(n_mp, blocks, block, width, False)
    step = min(DH, 2 * count)
    cols = [slice(n * DH, (n + 1) * DH) for n in range(heads)]
    targets = [[slice(m * width + n * DH, m * width + (n + 1) * DH) for n in range(heads)] for m in (0, 1)]

    def inputs(k):
        return [
            pltpu.make_async_copy(
                array.at[:, pl.ds(column(rs[0] + k), width)],
                token_buf.at[k, m, pl.ds(n * count, count)],
                sems.at[0, k, m, n],
            )
            for m, pair in enumerate(((q_ref, sq_ref), (g_ref, sg_ref)))
            for n, array in enumerate(pair)
        ]

    def outputs(k):
        copies = []
        for m, own in enumerate((query_grad_ref, attended_ref)):
            starts = (column(rs[0] + k), pl.multiple_of((2 * (rs[0] + k) + m) * width, width))
            for n, (array, start) in enumerate(zip((own, sibling_ref), starts)):
                copies.append(
                    pltpu.make_async_copy(
                        result_buf.at[k, m, pl.ds(n * count, count)],
                        array.at[:, pl.ds(start, width)],
                        sems.at[1, k, m, n],
                    )
                )
        return copies

    def repeat(body):
        if len(rs) == 1:
            body(0, None)
        else:
            lax.fori_loop(0, len(rs), body, None)

    def start_inputs(k, _):
        for copy in inputs(k):
            copy.start()

    def wait_outputs(k, _):
        for copy in outputs(k):
            copy.wait()

    def work(k, _):
        rows = pl.ds(pl.multiple_of(k * size, size), size)
        memory = [[jnp.concatenate([ref[rows, t] for ref in memory_refs], axis=0) for t in row] for row in targets]

        def scores(n):
            raw_ref[n] = dot(memory[0][n], token_buf[k, 0, :, cols[n]], NT)
            prob_ref[n] = dot(memory[1][n], token_buf[k, 1, :, cols[n]], NT)

        def softmax(n):
            for begin in range(0, 2 * count, step):
                part = slice(begin, begin + step)
                grad_ref[n, :, part], weight_ref[n, :, part] = softmax_part(raw_ref[n, :, part], prob_ref[n, :, part])

        def results(n):
            for m, pair_ref in enumerate((grad_ref, weight_ref)):
                result_buf[k, m, :, cols[n]] = dot(memory[m][n].T, pair_ref[n], NN).astype(bf16).T

        def terms(n):
            for m, pair_ref in enumerate((grad_ref, weight_ref)):
                term = dot(pair_ref[n], token_buf[k, m, :, cols[n]], NN)
                for i, term_ref in enumerate(term_refs):
                    term_ref[rows, targets[m][n]] = term[i * size : (i + 1) * size].astype(term_ref.dtype)

        for copy in inputs(k):
            copy.wait()
        for n in range(heads + 2):
            if n < heads:
                scores(n)
            if 1 <= n <= heads:
                softmax(n - 1)
            if n >= 2:
                results(n - 2)
                if n <= heads:
                    terms(n - 2)
        for copy in outputs(k):
            copy.start()
        terms(heads - 1)

    repeat(start_inputs)
    repeat(work)
    repeat(wait_outputs)


def pinned(space, *arrays):
    return [pltpu.with_memory_space_constraint(array, space) for array in arrays]


HBM, VMEM = pl.BlockSpec(memory_space=pltpu.HBM), pl.BlockSpec(memory_space=pltpu.VMEM)


def attention(n_mp, blocks, block, rs, tokens, memory, types, outputs, sent):
    rows, whole = tokens[0].shape
    width = memory[0].shape[1] // 2
    count = sum(m.shape[0] for m in memory) // len(rs)
    scratch = (width // DH, count, 2 * rows)
    earlier = [*outputs] + ([] if sent is None else [sent])
    first = 4 + len(memory)
    return pl.pallas_call(
        functools.partial(attention_kernel, n_mp, blocks, block, rs, len(memory)),
        in_specs=[HBM] * 4 + [VMEM] * len(memory) + [HBM] * len(earlier),
        out_specs=[HBM] * 3 + [VMEM] * len(memory),
        out_shape=[jax.ShapeDtypeStruct((rows, whole), bf16)] * 2
        + [jax.ShapeDtypeStruct((rows, whole // blocks), bf16)]
        + [pltpu.VMEM(m.shape, t) for m, t in zip(memory, types)],
        scratch_shapes=[pltpu.VMEM((len(rs), 2, 2 * rows, width), bf16)] * 2
        + [pltpu.VMEM(scratch, t) for t in (f32, f32, bf16, bf16)]
        + [pltpu.SemaphoreType.DMA((2, len(rs), 2, 2))],
        input_output_aliases={first + n: n for n in range(len(earlier))},
        compiler_params=pltpu.CompilerParams(vmem_limit_bytes=32 * 1024 * 1024),
        cost_estimate=pl.CostEstimate(
            flops=24 * rows * count * width * len(rs),
            bytes_accessed=16 * rows * width * len(rs),
            transcendentals=2 * rows * count * width * len(rs) // DH,
        ),
    )(*pinned(pltpu.HBM, *tokens[:2]), *tokens[2:], *pinned(pltpu.VMEM, *memory), *earlier)


def placing_kernel(n_mp, blocks, *refs):
    returned_refs, (attended_ref, query_grad_ref, sems) = refs[:blocks], refs[-3:]
    width = returned_refs[0].shape[1] // (2 * n_mp)
    copies = []
    for block, returned_ref in enumerate(returned_refs):
        column = columns(n_mp, blocks, block, width, True)
        for r in range(n_mp):
            for m, target in enumerate((query_grad_ref, attended_ref)):
                start = (2 * r + m) * width
                copies.append(
                    pltpu.make_async_copy(
                        returned_ref.at[:, start : start + width],
                        target.at[:, pl.ds(column(r), width)],
                        sems.at[len(copies)],
                    )
                )
    for copy in copies:
        copy.start()
    for copy in copies:
        copy.wait()


def placing(n_mp, returned, attended, query_grad):
    blocks = len(returned)
    return pl.pallas_call(
        functools.partial(placing_kernel, n_mp, blocks),
        in_specs=[VMEM] * blocks + [HBM] * 2,
        out_specs=[HBM] * 2,
        out_shape=[jax.ShapeDtypeStruct(attended.shape, bf16)] * 2,
        scratch_shapes=[pltpu.SemaphoreType.DMA((2 * blocks * n_mp,))],
        input_output_aliases={blocks: 0, blocks + 1: 1},
    )(*pinned(pltpu.VMEM, *returned), attended, query_grad)


def together(*values):
    return lax.optimization_barrier(values)


def shards(n_seq, n_mp, queries, memory_keys, memory_values, output_grad):
    def swap(array, axis, bits):
        size = n_seq if axis == "seq" else n_mp
        return lax.ppermute(array, axis, [(i, i ^ bits) for i in range(size)])

    core_bit, x_bit = 1, 2
    z_bits = range(4, n_seq, 4)
    y_bits = [1 << b for b in range(n_mp.bit_length() - 1)]
    rows, part = memory_keys.shape
    share, blocks = part // 2, 2
    block = share // blocks
    core = lax.axis_index("seq") & 1

    def packed(c):
        both = [lax.dynamic_slice_in_dim(array, c * share, share, axis=1) for array in (memory_keys, memory_values)]
        return jnp.concatenate([b[:, n * block : (n + 1) * block] for n in range(blocks) for b in both], axis=1)

    base = jnp.concatenate([packed(core), swap(packed(1 - core), "seq", core_bit)])
    base, queries_out, grad_out = together(base, queries, output_grad)
    sibling_queries, sibling_grad = swap(queries_out, "seq", core_bit), swap(grad_out, "seq", core_bit)
    tokens = (queries, output_grad, sibling_queries, sibling_grad)

    got = [base] + [swap(base, "seq", bits) for bits in z_bits]
    first, second = (jnp.concatenate([g[:, n * 2 * block : (n + 1) * 2 * block] for g in got]) for n in (0, 1))

    def wider(held, got):
        return jnp.concatenate([held, got])

    first_got, second_got = together(swap(first, "seq", x_bit), swap(second, "mp", y_bits[0]))
    first, second = wider(first, first_got), wider(second, second_got)
    for bits in y_bits[:-1]:
        first = wider(first, swap(first, "mp", bits))
    for bits in y_bits[1:]:
        second = wider(second, swap(second, "mp", bits))
    first_got, second_got = swap(first, "mp", y_bits[-1]), swap(second, "seq", x_bit)

    half = n_mp // 2
    *outputs, out, first_keep = attention(n_mp, blocks, 0, range(half), tokens, [first], [f32], [], None)
    *outputs, out_first, give = attention(
        n_mp, blocks, 0, range(half, n_mp), tokens, [first_got], [bf16], outputs, out
    )
    first_got = swap(give, "mp", y_bits[-1])
    *outputs, out_second, second_keep, give = attention(
        n_mp, blocks, 1, range(n_mp), tokens, [second, second_got], [f32, bf16], outputs, None
    )
    second_got = swap(give, "seq", x_bit)
    first, second, out_first, out_second = together(
        first_keep + first_got.astype(f32), second_keep + second_got.astype(f32), out_first, out_second
    )

    def fold(total, axis, bits):
        middle = total.shape[0] // 2
        return total[:middle] + swap(total[middle:].astype(bf16), axis, bits).astype(f32)

    for bits in y_bits[-2::-1]:
        first = fold(first, "mp", bits)
    for bits in y_bits[:0:-1]:
        second = fold(second, "mp", bits)
    first, second = fold(first, "seq", x_bit), fold(second, "mp", y_bits[0])
    returned = [swap(out, "seq", core_bit) for out in (out_first, out_second)]
    first, second, returned = together(first, second, returned)
    total = jnp.concatenate([first, second], axis=1)
    outputs = placing(n_mp, returned, *outputs)
    count, give = 2 * rows, total.astype(bf16)
    got = [swap(give[n * count : (n + 1) * count], "seq", bits) for n, bits in enumerate(z_bits, 1)]
    got, outputs = together(got, outputs)
    total = (total[:count] + sum(g.astype(f32) for g in got)).astype(bf16)
    mine, other = total[:rows], swap(total[rows:], "seq", core_bit)

    def joined(m):
        a, b = (
            jnp.concatenate([t[:, (2 * n + m) * block : (2 * n + m + 1) * block] for n in range(blocks)], axis=1)
            for t in (mine, other)
        )
        whole = lax.dynamic_update_slice_in_dim(jnp.zeros((rows, part), bf16), a, core * share, axis=1)
        return lax.dynamic_update_slice_in_dim(whole, b, (1 - core) * share, axis=1)

    return (*outputs, joined(0), joined(1))


def solution(mesh):
    body = functools.partial(shards, mesh.shape["seq"], mesh.shape["mp"])
    return jax.shard_map(
        body,
        mesh=mesh,
        in_specs=(P(("seq", "mp"), None), P("seq", "mp"), P("seq", "mp"), P(("seq", "mp"), None)),
        out_specs=(P(("seq", "mp"), None), P(("seq", "mp"), None), P("seq", "mp"), P("seq", "mp")),
        check_vma=False,
    )
```

```python
import functools
import math

import jax
import jax.numpy as jnp
from jax import lax
from jax.experimental import pallas as pl
from jax.experimental.pallas import tpu as pltpu
from jax.sharding import PartitionSpec as P

DH = 128

NT = (((1,), (1,)), ((), ()))
NN = (((1,), (0,)), ((), ()))

bf16, f32 = jnp.bfloat16, jnp.float32


def dot(a, b, dims):
    return lax.dot_general(a, b, dims, preferred_element_type=f32)


def softmax_part(raw, prob_grad):
    temper = 1.0 / math.sqrt(DH)
    peak = jnp.max(raw, axis=0, keepdims=True)
    powers = jnp.exp2((raw - peak) * (temper * math.log2(math.e)))
    inverse = 1.0 / jnp.sum(powers, axis=0, keepdims=True)
    delta = jnp.sum(powers * prob_grad, axis=0, keepdims=True) * inverse
    weights = (powers * inverse).astype(bf16)
    score_grad = (powers * (inverse * temper) * (prob_grad - delta)).astype(bf16)
    return score_grad, weights


def columns(n_mp, blocks, block, width, of_sibling):
    core, my = lax.axis_index("seq") & 1, lax.axis_index("mp")
    core = 1 - core if of_sibling else core
    return lambda r: pl.multiple_of((((my ^ r) * 2 + core) * blocks + block) * width, width)


def attention_kernel(n_mp, blocks, jobs, n_memory, q_ref, g_ref, sq_ref, sg_ref, *refs):
    used = sorted({block for block, *_ in jobs})
    memory_refs, refs = refs[:n_memory], refs[n_memory:]
    token_buf, result_buf, raw_ref, prob_ref, grad_ref, weight_ref, sems = refs[-7:]
    n_terms = 1 + max(i for *_, terms in jobs for i, _ in terms)
    term_refs, refs = refs[-7 - n_terms : -7], refs[: -7 - n_terms]
    attended_ref, query_grad_ref, *sent_refs = refs[-2 - len(used) :]
    count, width = q_ref.shape[0], memory_refs[0].shape[1] // 2
    heads, slots = width // DH, raw_ref.shape[0]
    step = min(DH, 2 * count)
    cols = [slice(n * DH, (n + 1) * DH) for n in range(heads)]
    targets = [[slice(m * width + n * DH, m * width + (n + 1) * DH) for n in range(heads)] for m in (0, 1)]

    def inputs(j):
        where = pl.ds(columns(n_mp, blocks, jobs[j][0], width, False)(jobs[j][1]), width)
        return [
            pltpu.make_async_copy(
                array.at[:, where], token_buf.at[j, m, pl.ds(n * count, count)], sems.at[0, j, m, n]
            )
            for m, pair in enumerate(((q_ref, sq_ref), (g_ref, sg_ref)))
            for n, array in enumerate(pair)
        ]

    def outputs(j):
        block, r = jobs[j][:2]
        where = pl.ds(columns(n_mp, blocks, block, width, False)(r), width)
        sent_ref, copies = sent_refs[used.index(block)], []
        for m, own in enumerate((query_grad_ref, attended_ref)):
            sent = sent_ref.at[:, pl.ds((2 * r + m) * width, width)]
            for n, target in enumerate((own.at[:, where], sent)):
                copies.append(
                    pltpu.make_async_copy(result_buf.at[j, m, pl.ds(n * count, count)], target, sems.at[1, j, m, n])
                )
        return copies

    def memory_of(j, m, n):
        return jnp.concatenate(
            [memory_refs[i][start : start + size, targets[m][n]] for i, start, size in jobs[j][2]], axis=0
        )

    def scores(j, n, slot):
        raw_ref[slot] = dot(memory_of(j, 0, n), token_buf[j, 0, :, cols[n]], NT)
        prob_ref[slot] = dot(memory_of(j, 1, n), token_buf[j, 1, :, cols[n]], NT)

    def softmax(slot):
        for begin in range(0, 2 * count, step):
            part = slice(begin, begin + step)
            grad_ref[slot, :, part], weight_ref[slot, :, part] = softmax_part(
                raw_ref[slot, :, part], prob_ref[slot, :, part]
            )

    def results(j, n, slot):
        for m, pair_ref in enumerate((grad_ref, weight_ref)):
            result_buf[j, m, :, cols[n]] = dot(memory_of(j, m, n).T, pair_ref[slot], NN).astype(bf16).T

    def terms(j, n, slot):
        for m, pair_ref in enumerate((grad_ref, weight_ref)):
            term, row = dot(pair_ref[slot], token_buf[j, m, :, cols[n]], NN), 0
            for (_, _, size), (i, start) in zip(*jobs[j][2:]):
                term_refs[i][start : start + size, targets[m][n]] = term[row : row + size].astype(term_refs[i].dtype)
                row += size

    for j in range(len(jobs)):
        for copy in inputs(j):
            copy.start()
    items = [(j, n) for j in range(len(jobs)) for n in range(heads)]
    for i in range(len(items) + 2):
        if i < len(items):
            j, n = items[i]
            if n == 0:
                for copy in inputs(j):
                    copy.wait()
            scores(j, n, i % slots)
        if 1 <= i <= len(items):
            softmax((i - 1) % slots)
        if i >= 2:
            j, n = items[i - 2]
            results(j, n, (i - 2) % slots)
            if n == heads - 1:
                for copy in outputs(j):
                    copy.start()
            terms(j, n, (i - 2) % slots)
    for j in range(len(jobs)):
        for copy in outputs(j):
            copy.wait()


def pinned(space, *arrays):
    return [pltpu.with_memory_space_constraint(array, space) for array in arrays]


HBM, VMEM = pl.BlockSpec(memory_space=pltpu.HBM), pl.BlockSpec(memory_space=pltpu.VMEM)


def attention(n_mp, blocks, jobs, tokens, memory, terms, outputs, sent):
    rows, whole = tokens[0].shape
    width = memory[0].shape[1] // 2
    count = sum(size for _, _, size in jobs[0][2])
    used = sorted({block for block, *_ in jobs})
    scratch = (min(4, len(jobs) * width // DH), count, 2 * rows)
    earlier = [*outputs] + [sent[block] for block in used if block in sent]
    first = 4 + len(memory)
    results = pl.pallas_call(
        functools.partial(attention_kernel, n_mp, blocks, jobs, len(memory)),
        in_specs=[HBM] * 4 + [VMEM] * len(memory) + [HBM] * len(earlier),
        out_specs=[HBM] * (2 + len(used)) + [VMEM] * len(terms),
        out_shape=[jax.ShapeDtypeStruct((rows, whole), bf16)] * 2
        + [jax.ShapeDtypeStruct((rows, whole // blocks), bf16)] * len(used)
        + [pltpu.VMEM(memory[0].shape, t) for t in terms],
        scratch_shapes=[pltpu.VMEM((len(jobs), 2, 2 * rows, width), bf16)] * 2
        + [pltpu.VMEM(scratch, t) for t in (f32, f32, bf16, bf16)]
        + [pltpu.SemaphoreType.DMA((2, len(jobs), 2, 2))],
        input_output_aliases={first + n: n for n in range(len(earlier))},
        compiler_params=pltpu.CompilerParams(vmem_limit_bytes=32 * 1024 * 1024),
        cost_estimate=pl.CostEstimate(
            flops=24 * rows * count * width * len(jobs),
            bytes_accessed=16 * rows * width * len(jobs),
            transcendentals=2 * rows * count * width * len(jobs) // DH,
        ),
    )(*pinned(pltpu.HBM, *tokens[:2]), *tokens[2:], *pinned(pltpu.VMEM, *memory), *earlier)
    sent = {**sent, **dict(zip(used, results[2:]))}
    return results[:2], sent, results[2 + len(used) :]


def placing_kernel(n_mp, blocks, *refs):
    returned_refs, (attended_ref, query_grad_ref, sems) = refs[:blocks], refs[-3:]
    width = returned_refs[0].shape[1] // (2 * n_mp)
    copies = []
    for block, returned_ref in enumerate(returned_refs):
        column = columns(n_mp, blocks, block, width, True)
        for r in range(n_mp):
            for m, target in enumerate((query_grad_ref, attended_ref)):
                start = (2 * r + m) * width
                copies.append(
                    pltpu.make_async_copy(
                        returned_ref.at[:, start : start + width],
                        target.at[:, pl.ds(column(r), width)],
                        sems.at[len(copies)],
                    )
                )
    for copy in copies:
        copy.start()
    for copy in copies:
        copy.wait()


def placing(n_mp, returned, attended, query_grad):
    blocks = len(returned)
    return pl.pallas_call(
        functools.partial(placing_kernel, n_mp, blocks),
        in_specs=[VMEM] * blocks + [HBM] * 2,
        out_specs=[HBM] * 2,
        out_shape=[jax.ShapeDtypeStruct(attended.shape, bf16)] * 2,
        scratch_shapes=[pltpu.SemaphoreType.DMA((2 * blocks * n_mp,))],
        input_output_aliases={blocks: 0, blocks + 1: 1},
    )(*pinned(pltpu.VMEM, *returned), attended, query_grad)


def together(*values):
    return lax.optimization_barrier(values)


def shards(n_seq, n_mp, queries, memory_keys, memory_values, output_grad):
    def swap(array, axis, bits):
        size = n_seq if axis == "seq" else n_mp
        return lax.ppermute(array, axis, [(i, i ^ bits) for i in range(size)])

    core_bit, x_bit = 1, 2
    z_bits = range(4, n_seq, 4)
    y_bits = [1 << b for b in range(n_mp.bit_length() - 1)]
    rows, part = memory_keys.shape
    share, blocks = part // 2, 2
    block = share // blocks
    core = lax.axis_index("seq") & 1

    def packed(c):
        both = [lax.dynamic_slice_in_dim(array, c * share, share, axis=1) for array in (memory_keys, memory_values)]
        return jnp.concatenate([b[:, n * block : (n + 1) * block] for n in range(blocks) for b in both], axis=1)

    base = jnp.concatenate([packed(core), swap(packed(1 - core), "seq", core_bit)])
    base, queries_out, grad_out = together(base, queries, output_grad)
    sibling_queries, sibling_grad = swap(queries_out, "seq", core_bit), swap(grad_out, "seq", core_bit)
    tokens = (queries, output_grad, sibling_queries, sibling_grad)

    got = [base] + [swap(base, "seq", bits) for bits in z_bits]
    first, second = (jnp.concatenate([g[:, n * 2 * block : (n + 1) * 2 * block] for g in got]) for n in (0, 1))

    def wider(held, got):
        return jnp.concatenate([held, got])

    first_got, second_got = together(swap(first, "seq", x_bit), swap(second, "mp", y_bits[0]))
    first, second = wider(first, first_got), wider(second, second_got)
    for bits in y_bits[:-1]:
        first = wider(first, swap(first, "mp", bits))
    for bits in y_bits[1:]:
        second = wider(second, swap(second, "mp", bits))
    first_got, second_got = swap(first, "mp", y_bits[-1]), swap(second, "seq", x_bit)

    half, size = n_mp // 2, second.shape[0] // n_mp

    def of_first(r, memory, term):
        start = (r % half) * 2 * size
        return (0, r, ((memory, start, 2 * size),), ((term, start),))

    def of_second(r, held, got, keep, give):
        return (1, r, ((held, r * size, size), (got, r * size, size)), ((keep, r * size), (give, r * size)))

    outputs, sent, (first_keep,) = attention(
        n_mp, blocks, [of_first(r, 0, 0) for r in range(half)], tokens, [first], [f32], [], {}
    )
    outputs, sent, (first_give, second_keep, second_give) = attention(
        n_mp,
        blocks,
        [of_first(r, 0, 0) for r in range(half, n_mp)] + [of_second(r, 1, 2, 1, 2) for r in range(n_mp)],
        tokens,
        [first_got, second, second_got],
        [bf16, f32, bf16],
        outputs,
        sent,
    )
    first_got, second_got = swap(first_give, "mp", y_bits[-1]), swap(second_give, "seq", x_bit)
    first, second, sent = together(
        first_keep + first_got.astype(f32), second_keep + second_got.astype(f32), sent
    )

    def fold(total, axis, bits):
        middle = total.shape[0] // 2
        return total[:middle] + swap(total[middle:].astype(bf16), axis, bits).astype(f32)

    for bits in y_bits[-2::-1]:
        first = fold(first, "mp", bits)
    for bits in y_bits[:0:-1]:
        second = fold(second, "mp", bits)
    first, second = fold(first, "seq", x_bit), fold(second, "mp", y_bits[0])
    returned = [swap(sent[block], "seq", core_bit) for block in range(blocks)]
    first, second, returned = together(first, second, returned)
    total = jnp.concatenate([first, second], axis=1)
    outputs = placing(n_mp, returned, *outputs)
    count, give = 2 * rows, total.astype(bf16)
    got = [swap(give[n * count : (n + 1) * count], "seq", bits) for n, bits in enumerate(z_bits, 1)]
    got, outputs = together(got, outputs)
    total = (total[:count] + sum(g.astype(f32) for g in got)).astype(bf16)
    mine, other = total[:rows], swap(total[rows:], "seq", core_bit)

    def joined(m):
        a, b = (
            jnp.concatenate([t[:, (2 * n + m) * block : (2 * n + m + 1) * block] for n in range(blocks)], axis=1)
            for t in (mine, other)
        )
        whole = lax.dynamic_update_slice_in_dim(jnp.zeros((rows, part), bf16), a, core * share, axis=1)
        return lax.dynamic_update_slice_in_dim(whole, b, (1 - core) * share, axis=1)

    return (*outputs, joined(0), joined(1))


def solution(mesh):
    body = functools.partial(shards, mesh.shape["seq"], mesh.shape["mp"])
    return jax.shard_map(
        body,
        mesh=mesh,
        in_specs=(P(("seq", "mp"), None), P("seq", "mp"), P("seq", "mp"), P(("seq", "mp"), None)),
        out_specs=(P(("seq", "mp"), None), P(("seq", "mp"), None), P("seq", "mp"), P("seq", "mp")),
        check_vma=False,
    )
```

```python
import functools
import math

import jax
import jax.numpy as jnp
from jax import lax
from jax.experimental import pallas as pl
from jax.experimental.pallas import tpu as pltpu
from jax.sharding import PartitionSpec as P

DH = 128

NT = (((1,), (1,)), ((), ()))
NN = (((1,), (0,)), ((), ()))

bf16, f32 = jnp.bfloat16, jnp.float32


def dot(a, b, dims):
    return lax.dot_general(a, b, dims, preferred_element_type=f32)


def softmax_part(raw, prob_grad):
    temper = 1.0 / math.sqrt(DH)
    peak = jnp.max(raw, axis=0, keepdims=True)
    powers = jnp.exp((raw - peak) * temper)
    inverse = 1.0 / jnp.sum(powers, axis=0, keepdims=True)
    delta = jnp.sum(powers * prob_grad, axis=0, keepdims=True) * inverse
    weights = (powers * inverse).astype(bf16)
    score_grad = (powers * (inverse * temper) * (prob_grad - delta)).astype(bf16)
    return score_grad, weights


def columns(n_mp, blocks, block, width, of_sibling):
    core, my = lax.axis_index("seq") & 1, lax.axis_index("mp")
    core = 1 - core if of_sibling else core
    return lambda r: pl.multiple_of((((my ^ r) * 2 + core) * blocks + block) * width, width)


def attention_kernel(n_mp, blocks, jobs, n_memory, q_ref, g_ref, sq_ref, sg_ref, *refs):
    used = sorted({block for block, *_ in jobs})
    memory_refs, refs = refs[:n_memory], refs[n_memory:]
    token_buf, result_buf, raw_ref, prob_ref, grad_ref, weight_ref, sems = refs[-7:]
    n_terms = 1 + max(i for *_, terms in jobs for i, _ in terms)
    term_refs, refs = refs[-7 - n_terms : -7], refs[: -7 - n_terms]
    attended_ref, query_grad_ref, *sent_refs = refs[-2 - len(used) :]
    count, width = q_ref.shape[0], memory_refs[0].shape[1] // 2
    heads, slots = width // DH, raw_ref.shape[0]
    step = min(DH, 2 * count)
    cols = [slice(n * DH, (n + 1) * DH) for n in range(heads)]
    targets = [[slice(m * width + n * DH, m * width + (n + 1) * DH) for n in range(heads)] for m in (0, 1)]

    def inputs(j):
        block, r = jobs[j][:2]
        starts = (columns(n_mp, blocks, block, width, False)(r), (block * n_mp + r) * width)
        return [
            pltpu.make_async_copy(
                array.at[:, pl.ds(starts[n], width)], token_buf.at[j, m, pl.ds(n * count, count)], sems.at[0, j, m, n]
            )
            for m, pair in enumerate(((q_ref, sq_ref), (g_ref, sg_ref)))
            for n, array in enumerate(pair)
        ]

    def outputs(j):
        block, r = jobs[j][:2]
        where = pl.ds(columns(n_mp, blocks, block, width, False)(r), width)
        sent_ref, copies = sent_refs[used.index(block)], []
        for m, own in enumerate((query_grad_ref, attended_ref)):
            sent = sent_ref.at[:, pl.ds((2 * r + m) * width, width)]
            for n, target in enumerate((own.at[:, where], sent)):
                copies.append(
                    pltpu.make_async_copy(result_buf.at[j, m, pl.ds(n * count, count)], target, sems.at[1, j, m, n])
                )
        return copies

    def memory_of(j, m, n):
        return jnp.concatenate(
            [memory_refs[i][start : start + size, targets[m][n]] for i, start, size in jobs[j][2]], axis=0
        )

    memory = {}

    def scores(j, n, slot):
        memory[j, n] = [memory_of(j, m, n) for m in (0, 1)]
        raw_ref[slot] = dot(memory[j, n][0], token_buf[j, 0, :, cols[n]], NT)
        prob_ref[slot] = dot(memory[j, n][1], token_buf[j, 1, :, cols[n]], NT)

    def softmax(slot):
        for begin in range(0, 2 * count, step):
            part = slice(begin, begin + step)
            grad_ref[slot, :, part], weight_ref[slot, :, part] = softmax_part(
                raw_ref[slot, :, part], prob_ref[slot, :, part]
            )

    def results(j, n, slot):
        for m, pair_ref in enumerate((grad_ref, weight_ref)):
            result_buf[j, m, :, cols[n]] = dot(memory[j, n][m].T, pair_ref[slot], NN).astype(bf16).T

    def terms(j, n, slot):
        for m, pair_ref in enumerate((grad_ref, weight_ref)):
            term, row = dot(pair_ref[slot], token_buf[j, m, :, cols[n]], NN), 0
            for (_, _, size), (i, start) in zip(*jobs[j][2:]):
                term_refs[i][start : start + size, targets[m][n]] = term[row : row + size].astype(term_refs[i].dtype)
                row += size

    for j in range(len(jobs)):
        for copy in inputs(j):
            copy.start()
    items = [(j, n) for j in range(len(jobs)) for n in range(heads)]
    for i in range(len(items) + 2):
        if i < len(items):
            j, n = items[i]
            if n == 0:
                for copy in inputs(j):
                    copy.wait()
            scores(j, n, i % slots)
        if 1 <= i <= len(items):
            softmax((i - 1) % slots)
        if i >= 2:
            j, n = items[i - 2]
            results(j, n, (i - 2) % slots)
            if n == heads - 1:
                for copy in outputs(j):
                    copy.start()
            terms(j, n, (i - 2) % slots)
    for j in range(len(jobs)):
        for copy in outputs(j):
            copy.wait()


def pinned(space, *arrays):
    return [pltpu.with_memory_space_constraint(array, space) for array in arrays]


HBM, VMEM = pl.BlockSpec(memory_space=pltpu.HBM), pl.BlockSpec(memory_space=pltpu.VMEM)


def attention(n_mp, blocks, jobs, tokens, memory, terms, outputs, sent):
    rows, whole = tokens[0].shape
    width = memory[0].shape[1] // 2
    count = sum(size for _, _, size in jobs[0][2])
    used = sorted({block for block, *_ in jobs})
    scratch = (min(4, len(jobs) * width // DH), count, 2 * rows)
    earlier = [*outputs] + [sent[block] for block in used if block in sent]
    first = 4 + len(memory)
    results = pl.pallas_call(
        functools.partial(attention_kernel, n_mp, blocks, jobs, len(memory)),
        in_specs=[HBM] * 4 + [VMEM] * len(memory) + [HBM] * len(earlier),
        out_specs=[HBM] * (2 + len(used)) + [VMEM] * len(terms),
        out_shape=[jax.ShapeDtypeStruct((rows, whole), bf16)] * 2
        + [jax.ShapeDtypeStruct((rows, whole // blocks), bf16)] * len(used)
        + [pltpu.VMEM(memory[0].shape, t) for t in terms],
        scratch_shapes=[pltpu.VMEM((len(jobs), 2, 2 * rows, width), bf16)] * 2
        + [pltpu.VMEM(scratch, t) for t in (f32, f32, bf16, bf16)]
        + [pltpu.SemaphoreType.DMA((2, len(jobs), 2, 2))],
        input_output_aliases={first + n: n for n in range(len(earlier))},
        compiler_params=pltpu.CompilerParams(vmem_limit_bytes=32 * 1024 * 1024),
        cost_estimate=pl.CostEstimate(
            flops=24 * rows * count * width * len(jobs),
            bytes_accessed=16 * rows * width * len(jobs),
            transcendentals=2 * rows * count * width * len(jobs) // DH,
        ),
    )(*pinned(pltpu.HBM, *tokens[:2]), *tokens[2:], *pinned(pltpu.VMEM, *memory), *earlier)
    sent = {**sent, **dict(zip(used, results[2:]))}
    return results[:2], sent, results[2 + len(used) :]


def packing_kernel(n_mp, blocks, q_ref, g_ref, packed_q_ref, packed_g_ref, sems):
    width = packed_q_ref.shape[1] // (blocks * n_mp)
    copies = []
    for block in range(blocks):
        column = columns(n_mp, blocks, block, width, True)
        for r in range(n_mp):
            where = pl.ds((block * n_mp + r) * width, width)
            for array, packed in ((q_ref, packed_q_ref), (g_ref, packed_g_ref)):
                copies.append(
                    pltpu.make_async_copy(
                        array.at[:, pl.ds(column(r), width)], packed.at[:, where], sems.at[len(copies)]
                    )
                )
    for copy in copies:
        copy.start()
    for copy in copies:
        copy.wait()


def packing(n_mp, blocks, queries, grad):
    rows, whole = queries.shape
    return pl.pallas_call(
        functools.partial(packing_kernel, n_mp, blocks),
        in_specs=[HBM] * 2,
        out_specs=[VMEM] * 2,
        out_shape=[pltpu.VMEM((rows, whole // 2), bf16)] * 2,
        scratch_shapes=[pltpu.SemaphoreType.DMA((2 * blocks * n_mp,))],
        cost_estimate=pl.CostEstimate(flops=0, bytes_accessed=4 * rows * whole, transcendentals=0),
    )(*pinned(pltpu.HBM, queries, grad))


def joining_kernel(blocks, mine_ref, other_ref, key_ref, value_ref, sems):
    core, block = lax.axis_index("seq") & 1, mine_ref.shape[1] // (2 * blocks)
    copies = []
    for place, source in ((core, mine_ref), (1 - core, other_ref)):
        for n in range(blocks):
            where = pl.ds(pl.multiple_of((place * blocks + n) * block, block), block)
            for m, target in enumerate((key_ref, value_ref)):
                part = source.at[:, pl.ds((2 * n + m) * block, block)]
                copies.append(pltpu.make_async_copy(part, target.at[:, where], sems.at[len(copies)]))
    for copy in copies:
        copy.start()
    for copy in copies:
        copy.wait()


def joining(blocks, mine, other):
    rows, width = mine.shape
    return pl.pallas_call(
        functools.partial(joining_kernel, blocks),
        in_specs=[VMEM] * 2,
        out_specs=[HBM] * 2,
        out_shape=[jax.ShapeDtypeStruct((rows, width), bf16)] * 2,
        scratch_shapes=[pltpu.SemaphoreType.DMA((4 * blocks,))],
    )(*pinned(pltpu.VMEM, mine, other))


def placing_kernel(n_mp, blocks, *refs):
    returned_refs, (attended_ref, query_grad_ref, sems) = refs[:blocks], refs[-3:]
    width = returned_refs[0].shape[1] // (2 * n_mp)
    copies = []
    for block, returned_ref in enumerate(returned_refs):
        column = columns(n_mp, blocks, block, width, True)
        for r in range(n_mp):
            for m, target in enumerate((query_grad_ref, attended_ref)):
                start = (2 * r + m) * width
                copies.append(
                    pltpu.make_async_copy(
                        returned_ref.at[:, start : start + width],
                        target.at[:, pl.ds(column(r), width)],
                        sems.at[len(copies)],
                    )
                )
    for copy in copies:
        copy.start()
    for copy in copies:
        copy.wait()


def placing(n_mp, returned, attended, query_grad):
    blocks = len(returned)
    return pl.pallas_call(
        functools.partial(placing_kernel, n_mp, blocks),
        in_specs=[VMEM] * blocks + [HBM] * 2,
        out_specs=[HBM] * 2,
        out_shape=[jax.ShapeDtypeStruct(attended.shape, bf16)] * 2,
        scratch_shapes=[pltpu.SemaphoreType.DMA((2 * blocks * n_mp,))],
        input_output_aliases={blocks: 0, blocks + 1: 1},
    )(*pinned(pltpu.VMEM, *returned), attended, query_grad)


def together(*values):
    return lax.optimization_barrier(values)


def shards(n_seq, n_mp, queries, memory_keys, memory_values, output_grad):
    def swap(array, axis, bits):
        size = n_seq if axis == "seq" else n_mp
        return lax.ppermute(array, axis, [(i, i ^ bits) for i in range(size)])

    core_bit, x_bit = 1, 2
    z_bits = range(n_seq - 4, 0, -4)
    y_bits = [1 << b for b in range(n_mp.bit_length() - 1)]
    rows, part = memory_keys.shape
    share, blocks = part // 2, 2
    block = share // blocks
    core = lax.axis_index("seq") & 1

    def packed(c):
        both = [lax.dynamic_slice_in_dim(array, c * share, share, axis=1) for array in (memory_keys, memory_values)]
        return jnp.concatenate([b[:, n * block : (n + 1) * block] for n in range(blocks) for b in both], axis=1)

    base = jnp.concatenate([packed(core), swap(packed(1 - core), "seq", core_bit)])

    got = [swap(base, "seq", bits) for bits in z_bits]
    got[-1], queries_out, grad_out = together(got[-1], queries, output_grad)
    tokens = (queries, output_grad)
    tokens += tuple(swap(array, "seq", core_bit) for array in packing(n_mp, blocks, queries_out, grad_out))
    got = [base] + got
    first, second = (jnp.concatenate([g[:, n * 2 * block : (n + 1) * 2 * block] for g in got]) for n in (0, 1))

    def wider(held, got):
        return jnp.concatenate([held, got])

    first_got, second_got = together(swap(first, "seq", x_bit), swap(second, "mp", y_bits[0]))
    first, second = wider(first, first_got), wider(second, second_got)
    for bits in y_bits[:-1]:
        first = wider(first, swap(first, "mp", bits))
    for bits in y_bits[1:]:
        second = wider(second, swap(second, "mp", bits))
    first_got, second_got = swap(first, "mp", y_bits[-1]), swap(second, "seq", x_bit)

    half, size = n_mp // 2, second.shape[0] // n_mp

    def of_first(r, memory, term):
        start = (r % half) * 2 * size
        return (0, r, ((memory, start, 2 * size),), ((term, start),))

    def of_second(r, held, got, keep, give):
        return (1, r, ((held, r * size, size), (got, r * size, size)), ((keep, r * size), (give, r * size)))

    outputs, sent, (first_keep,) = attention(
        n_mp, blocks, [of_first(r, 0, 0) for r in range(half)], tokens, [first], [f32], [], {}
    )
    outputs, sent, (first_give, second_keep, second_give) = attention(
        n_mp,
        blocks,
        [of_first(r, 0, 0) for r in range(half, n_mp)] + [of_second(r, 1, 2, 1, 2) for r in range(n_mp)],
        tokens,
        [first_got, second, second_got],
        [bf16, f32, bf16],
        outputs,
        sent,
    )
    first_got, second_got = swap(first_give, "mp", y_bits[-1]), swap(second_give, "seq", x_bit)
    first, second, sent = together(
        first_keep + first_got.astype(f32), second_keep + second_got.astype(f32), sent
    )

    def fold(total, axis, bits):
        middle = total.shape[0] // 2
        return total[:middle] + swap(total[middle:].astype(bf16), axis, bits).astype(f32)

    for bits in y_bits[-2::-1]:
        first = fold(first, "mp", bits)
    for bits in y_bits[:0:-1]:
        second = fold(second, "mp", bits)
    first, second = fold(first, "seq", x_bit), fold(second, "mp", y_bits[0])
    returned = [swap(sent[block], "seq", core_bit) for block in range(blocks)]
    first, second, returned = together(first, second, returned)
    total = jnp.concatenate([first, second], axis=1)
    outputs = placing(n_mp, returned, *outputs)
    count, give = 2 * rows, total.astype(bf16)
    got = [swap(give[n * count : (n + 1) * count], "seq", bits) for n, bits in enumerate(z_bits, 1)]
    got, outputs = together(got, outputs)
    total = (total[:count] + sum(g.astype(f32) for g in got)).astype(bf16)
    mine, other = total[:rows], swap(total[rows:], "seq", core_bit)

    return (*outputs, *joining(blocks, mine, other))


def solution(mesh):
    body = functools.partial(shards, mesh.shape["seq"], mesh.shape["mp"])
    return jax.shard_map(
        body,
        mesh=mesh,
        in_specs=(P(("seq", "mp"), None), P("seq", "mp"), P("seq", "mp"), P(("seq", "mp"), None)),
        out_specs=(P(("seq", "mp"), None), P(("seq", "mp"), None), P("seq", "mp"), P("seq", "mp")),
        check_vma=False,
    )
```

```python
import functools
import math

import jax
import jax.numpy as jnp
from jax import lax
from jax.experimental import pallas as pl
from jax.experimental.pallas import tpu as pltpu
from jax.sharding import PartitionSpec as P

DH = 128

NT = (((1,), (1,)), ((), ()))
NN = (((1,), (0,)), ((), ()))

bf16, f32 = jnp.bfloat16, jnp.float32


def dot(a, b, dims):
    return lax.dot_general(a, b, dims, preferred_element_type=f32)


def softmax_part(raw, prob_grad):
    temper = 1.0 / math.sqrt(DH)
    peak = jnp.max(raw, axis=0, keepdims=True)
    powers = jnp.exp((raw - peak) * temper)
    inverse = 1.0 / jnp.sum(powers, axis=0, keepdims=True)
    delta = jnp.sum(powers * prob_grad, axis=0, keepdims=True) * inverse
    weights = (powers * inverse).astype(bf16)
    score_grad = (powers * (inverse * temper) * (prob_grad - delta)).astype(bf16)
    return score_grad, weights


def columns(n_mp, blocks, block, width, of_sibling):
    core, my = lax.axis_index("seq") & 1, lax.axis_index("mp")
    core = 1 - core if of_sibling else core
    return lambda r: pl.multiple_of((((my ^ r) * 2 + core) * blocks + block) * width, width)


def attention_kernel(n_mp, blocks, groups, n_memory, q_ref, g_ref, sq_ref, sg_ref, *refs):
    used = sorted({block for block, *_ in groups})
    memory_refs, refs = refs[:n_memory], refs[n_memory:]
    token_buf, result_buf, raw_ref, prob_ref, grad_ref, weight_ref, sems = refs[-7:]
    n_terms = 1 + max(max(terms) for *_, terms in groups)
    term_refs, refs = refs[-7 - n_terms : -7], refs[: -7 - n_terms]
    attended_ref, query_grad_ref, *sent_refs = refs[-2 - len(used) :]
    count, width = q_ref.shape[0], memory_refs[0].shape[1] // 2
    heads = width // DH
    step = min(DH, 2 * count)
    cols = [slice(n * DH, (n + 1) * DH) for n in range(heads)]
    targets = [[slice(m * width + n * DH, m * width + (n + 1) * DH) for n in range(heads)] for m in (0, 1)]

    def of_group(block, r0, number, memories, terms, slot0):
        column = columns(n_mp, blocks, block, width, False)
        size = memory_refs[memories[0]].shape[0] // number
        sent_ref = sent_refs[used.index(block)]

        def inputs(k):
            starts = (column(r0 + k), pl.multiple_of((block * n_mp + r0 + k) * width, width))
            return [
                pltpu.make_async_copy(
                    array.at[:, pl.ds(start, width)],
                    token_buf.at[slot0 + k, m, pl.ds(n * count, count)],
                    sems.at[0, slot0 + k, m, n],
                )
                for m, pair in enumerate(((q_ref, sq_ref), (g_ref, sg_ref)))
                for n, (array, start) in enumerate(zip(pair, starts))
            ]

        def outputs(k):
            copies = []
            for m, own in enumerate((query_grad_ref, attended_ref)):
                starts = (column(r0 + k), pl.multiple_of((2 * (r0 + k) + m) * width, width))
                for n, (array, start) in enumerate(zip((own, sent_ref), starts)):
                    copies.append(
                        pltpu.make_async_copy(
                            result_buf.at[slot0 + k, m, pl.ds(n * count, count)],
                            array.at[:, pl.ds(start, width)],
                            sems.at[1, slot0 + k, m, n],
                        )
                    )
            return copies

        def repeat(body):
            if number == 1:
                body(0, None)
            else:
                lax.fori_loop(0, number, body, None)

        def start_inputs(k, _):
            for copy in inputs(k):
                copy.start()

        def wait_outputs(k, _):
            for copy in outputs(k):
                copy.wait()

        def work(k, _):
            rows = pl.ds(pl.multiple_of(k * size, size), size)
            memory = [
                [jnp.concatenate([memory_refs[i][rows, t] for i in memories], axis=0) for t in row] for row in targets
            ]

            def tokens(m, n):
                return token_buf[slot0 + k, m, :, cols[n]]

            def scores(n):
                raw_ref[n] = dot(memory[0][n], tokens(0, n), NT)
                prob_ref[n] = dot(memory[1][n], tokens(1, n), NT)

            def softmax(n):
                for begin in range(0, 2 * count, step):
                    part = slice(begin, begin + step)
                    grad_ref[n, :, part], weight_ref[n, :, part] = softmax_part(
                        raw_ref[n, :, part], prob_ref[n, :, part]
                    )

            def results(n):
                for m, pair_ref in enumerate((grad_ref, weight_ref)):
                    result = dot(memory[m][n].T, pair_ref[n], NN).astype(bf16)
                    result_buf[slot0 + k, m, :, cols[n]] = result.T

            def gradients(n):
                for m, pair_ref in enumerate((grad_ref, weight_ref)):
                    term = dot(pair_ref[n], tokens(m, n), NN)
                    for i, t in enumerate(terms):
                        term_refs[t][rows, targets[m][n]] = term[i * size : (i + 1) * size].astype(term_refs[t].dtype)

            for copy in inputs(k):
                copy.wait()
            for n in range(heads + 2):
                if n < heads:
                    scores(n)
                if 1 <= n <= heads:
                    softmax(n - 1)
                if n >= 2:
                    results(n - 2)
                    if n <= heads:
                        gradients(n - 2)
            for copy in outputs(k):
                copy.start()
            gradients(heads - 1)

        return [functools.partial(repeat, body) for body in (start_inputs, work, wait_outputs)]

    slot0, phases = 0, []
    for group in groups:
        phases.append(of_group(*group, slot0))
        slot0 += group[2]
    for phase in zip(*phases):
        for run in phase:
            run()


def pinned(space, *arrays):
    return [pltpu.with_memory_space_constraint(array, space) for array in arrays]


HBM, VMEM = pl.BlockSpec(memory_space=pltpu.HBM), pl.BlockSpec(memory_space=pltpu.VMEM)


def attention(n_mp, blocks, groups, tokens, memory, terms, outputs, sent):
    rows, whole = tokens[0].shape
    width = memory[0].shape[1] // 2
    number = sum(n for _, _, n, *_ in groups)
    count = len(groups[0][3]) * memory[0].shape[0] // groups[0][2]
    used = sorted({block for block, *_ in groups})
    scratch = (width // DH, count, 2 * rows)
    earlier = [*outputs] + [sent[block] for block in used if block in sent]
    first = 4 + len(memory)
    results = pl.pallas_call(
        functools.partial(attention_kernel, n_mp, blocks, groups, len(memory)),
        in_specs=[HBM] * 4 + [VMEM] * len(memory) + [HBM] * len(earlier),
        out_specs=[HBM] * (2 + len(used)) + [VMEM] * len(terms),
        out_shape=[jax.ShapeDtypeStruct((rows, whole), bf16)] * 2
        + [jax.ShapeDtypeStruct((rows, whole // blocks), bf16)] * len(used)
        + [pltpu.VMEM(memory[0].shape, t) for t in terms],
        scratch_shapes=[pltpu.VMEM((number, 2, 2 * rows, width), bf16)] * 2
        + [pltpu.VMEM(scratch, t) for t in (f32, f32, bf16, bf16)]
        + [pltpu.SemaphoreType.DMA((2, number, 2, 2))],
        input_output_aliases={first + n: n for n in range(len(earlier))},
        compiler_params=pltpu.CompilerParams(vmem_limit_bytes=32 * 1024 * 1024),
        cost_estimate=pl.CostEstimate(
            flops=24 * rows * count * width * number,
            bytes_accessed=16 * rows * width * number,
            transcendentals=2 * rows * count * width * number // DH,
        ),
    )(*pinned(pltpu.HBM, *tokens[:2]), *tokens[2:], *pinned(pltpu.VMEM, *memory), *earlier)
    sent = {**sent, **dict(zip(used, results[2:]))}
    return results[:2], sent, results[2 + len(used) :]


def packing_kernel(n_mp, blocks, q_ref, g_ref, packed_q_ref, packed_g_ref, sems):
    width = packed_q_ref.shape[1] // (blocks * n_mp)
    copies = []
    for block in range(blocks):
        column = columns(n_mp, blocks, block, width, True)
        for r in range(n_mp):
            where = pl.ds((block * n_mp + r) * width, width)
            for array, packed in ((q_ref, packed_q_ref), (g_ref, packed_g_ref)):
                copies.append(
                    pltpu.make_async_copy(
                        array.at[:, pl.ds(column(r), width)], packed.at[:, where], sems.at[len(copies)]
                    )
                )
    for copy in copies:
        copy.start()
    for copy in copies:
        copy.wait()


def packing(n_mp, blocks, queries, grad):
    rows, whole = queries.shape
    return pl.pallas_call(
        functools.partial(packing_kernel, n_mp, blocks),
        in_specs=[HBM] * 2,
        out_specs=[VMEM] * 2,
        out_shape=[pltpu.VMEM((rows, whole // 2), bf16)] * 2,
        scratch_shapes=[pltpu.SemaphoreType.DMA((2 * blocks * n_mp,))],
        cost_estimate=pl.CostEstimate(flops=0, bytes_accessed=4 * rows * whole, transcendentals=0),
    )(*pinned(pltpu.HBM, queries, grad))


def joining_kernel(blocks, mine_ref, other_ref, key_ref, value_ref, sems):
    core, block = lax.axis_index("seq") & 1, mine_ref.shape[1] // (2 * blocks)
    copies = []
    for place, source in ((core, mine_ref), (1 - core, other_ref)):
        for n in range(blocks):
            where = pl.ds(pl.multiple_of((place * blocks + n) * block, block), block)
            for m, target in enumerate((key_ref, value_ref)):
                part = source.at[:, pl.ds((2 * n + m) * block, block)]
                copies.append(pltpu.make_async_copy(part, target.at[:, where], sems.at[len(copies)]))
    for copy in copies:
        copy.start()
    for copy in copies:
        copy.wait()


def joining(blocks, mine, other):
    rows, width = mine.shape
    return pl.pallas_call(
        functools.partial(joining_kernel, blocks),
        in_specs=[VMEM] * 2,
        out_specs=[HBM] * 2,
        out_shape=[jax.ShapeDtypeStruct((rows, width), bf16)] * 2,
        scratch_shapes=[pltpu.SemaphoreType.DMA((4 * blocks,))],
    )(*pinned(pltpu.VMEM, mine, other))


def placing_kernel(n_mp, blocks, *refs):
    returned_refs, (attended_ref, query_grad_ref, sems) = refs[:blocks], refs[-3:]
    width = returned_refs[0].shape[1] // (2 * n_mp)
    copies = []
    for block, returned_ref in enumerate(returned_refs):
        column = columns(n_mp, blocks, block, width, True)
        for r in range(n_mp):
            for m, target in enumerate((query_grad_ref, attended_ref)):
                start = (2 * r + m) * width
                copies.append(
                    pltpu.make_async_copy(
                        returned_ref.at[:, start : start + width],
                        target.at[:, pl.ds(column(r), width)],
                        sems.at[len(copies)],
                    )
                )
    for copy in copies:
        copy.start()
    for copy in copies:
        copy.wait()


def placing(n_mp, returned, attended, query_grad):
    blocks = len(returned)
    return pl.pallas_call(
        functools.partial(placing_kernel, n_mp, blocks),
        in_specs=[VMEM] * blocks + [HBM] * 2,
        out_specs=[HBM] * 2,
        out_shape=[jax.ShapeDtypeStruct(attended.shape, bf16)] * 2,
        scratch_shapes=[pltpu.SemaphoreType.DMA((2 * blocks * n_mp,))],
        input_output_aliases={blocks: 0, blocks + 1: 1},
    )(*pinned(pltpu.VMEM, *returned), attended, query_grad)


def together(*values):
    return lax.optimization_barrier(values)


def shards(n_seq, n_mp, queries, memory_keys, memory_values, output_grad):
    def swap(array, axis, bits):
        size = n_seq if axis == "seq" else n_mp
        return lax.ppermute(array, axis, [(i, i ^ bits) for i in range(size)])

    core_bit, x_bit = 1, 2
    z_bits = [4, *range(n_seq - 4, 4, -4)]
    y_bits = [1 << b for b in range(n_mp.bit_length() - 1)]
    rows, part = memory_keys.shape
    share, blocks = part // 2, 2
    block = share // blocks
    core = lax.axis_index("seq") & 1

    def packed(c):
        both = [lax.dynamic_slice_in_dim(array, c * share, share, axis=1) for array in (memory_keys, memory_values)]
        return jnp.concatenate([b[:, n * block : (n + 1) * block] for n in range(blocks) for b in both], axis=1)

    base = jnp.concatenate([packed(core), swap(packed(1 - core), "seq", core_bit)])

    base, queries_out, grad_out = together(base, queries, output_grad)
    got = [swap(base, "seq", bits) for bits in z_bits]
    tokens = (queries, output_grad)
    tokens += tuple(swap(array, "seq", core_bit) for array in packing(n_mp, blocks, queries_out, grad_out))
    got = [base] + got
    first, second = (jnp.concatenate([g[:, n * 2 * block : (n + 1) * 2 * block] for g in got]) for n in (0, 1))

    def wider(held, got):
        return jnp.concatenate([held, got])

    first_got, second_got = together(swap(first, "seq", x_bit), swap(second, "mp", y_bits[0]))
    first, second = wider(first, first_got), wider(second, second_got)
    for bits in y_bits[:-1]:
        first = wider(first, swap(first, "mp", bits))
    for bits in y_bits[1:]:
        second = wider(second, swap(second, "mp", bits))
    first_got, second_got = swap(first, "mp", y_bits[-1]), swap(second, "seq", x_bit)

    half = n_mp // 2
    outputs, sent, (first_keep,) = attention(
        n_mp, blocks, [(0, 0, half, (0,), (0,))], tokens, [first], [f32], [], {}
    )
    outputs, sent, (first_give, second_keep, second_give) = attention(
        n_mp,
        blocks,
        [(0, half, n_mp - half, (0,), (0,)), (1, 0, n_mp, (1, 2), (1, 2))],
        tokens,
        [first_got, second, second_got],
        [bf16, f32, bf16],
        outputs,
        sent,
    )
    first_got, second_got = swap(first_give, "mp", y_bits[-1]), swap(second_give, "seq", x_bit)
    first, second, sent = together(
        first_keep + first_got.astype(f32), second_keep + second_got.astype(f32), sent
    )

    def fold(total, axis, bits):
        middle = total.shape[0] // 2
        return total[:middle] + swap(total[middle:].astype(bf16), axis, bits).astype(f32)

    for bits in y_bits[-2::-1]:
        first = fold(first, "mp", bits)
    for bits in y_bits[:0:-1]:
        second = fold(second, "mp", bits)
    first, second = fold(first, "seq", x_bit), fold(second, "mp", y_bits[0])
    returned = [swap(sent[block], "seq", core_bit) for block in range(blocks)]
    first, second, returned = together(first, second, returned)
    total = jnp.concatenate([first, second], axis=1)
    outputs = placing(n_mp, returned, *outputs)
    count, give = 2 * rows, total.astype(bf16)
    got = [swap(give[n * count : (n + 1) * count], "seq", bits) for n, bits in enumerate(z_bits, 1)]
    got, outputs = together(got, outputs)
    total = (total[:count] + sum(g.astype(f32) for g in got)).astype(bf16)
    mine, other = total[:rows], swap(total[rows:], "seq", core_bit)

    return (*outputs, *joining(blocks, mine, other))


def solution(mesh):
    body = functools.partial(shards, mesh.shape["seq"], mesh.shape["mp"])
    return jax.shard_map(
        body,
        mesh=mesh,
        in_specs=(P(("seq", "mp"), None), P("seq", "mp"), P("seq", "mp"), P(("seq", "mp"), None)),
        out_specs=(P(("seq", "mp"), None), P(("seq", "mp"), None), P("seq", "mp"), P("seq", "mp")),
        check_vma=False,
    )
```

```python
import functools
import math

import jax
import jax.numpy as jnp
from jax import lax
from jax.experimental import pallas as pl
from jax.experimental.pallas import tpu as pltpu
from jax.sharding import PartitionSpec as P

DH = 128

NT = (((1,), (1,)), ((), ()))
NN = (((1,), (0,)), ((), ()))

bf16, f32 = jnp.bfloat16, jnp.float32


def dot(a, b, dims):
    return lax.dot_general(a, b, dims, preferred_element_type=f32)


def softmax_part(raw, prob_grad):
    temper = 1.0 / math.sqrt(DH)
    peak = jnp.max(raw, axis=0, keepdims=True)
    powers = jnp.exp((raw - peak) * temper)
    inverse = 1.0 / jnp.sum(powers, axis=0, keepdims=True)
    delta = jnp.sum(powers * prob_grad, axis=0, keepdims=True) * inverse
    weights = (powers * inverse).astype(bf16)
    score_grad = (powers * (inverse * temper) * (prob_grad - delta)).astype(bf16)
    return score_grad, weights


def columns(n_mp, blocks, block, width, of_sibling):
    core, my = lax.axis_index("seq") & 1, lax.axis_index("mp")
    core = 1 - core if of_sibling else core
    return lambda r: pl.multiple_of((((my ^ r) * 2 + core) * blocks + block) * width, width)


def attention_kernel(n_mp, blocks, groups, n_memory, q_ref, g_ref, sq_ref, sg_ref, *refs):
    used = sorted({block for block, *_ in groups})
    memory_refs, refs = refs[:n_memory], refs[n_memory:]
    token_buf, result_buf, raw_ref, prob_ref, grad_ref, weight_ref, sems = refs[-7:]
    n_terms = 1 + max(max(terms) for *_, terms in groups)
    term_refs, refs = refs[-7 - n_terms : -7], refs[: -7 - n_terms]
    attended_ref, query_grad_ref, *sent_refs = refs[-2 - len(used) :]
    count, width = q_ref.shape[0], memory_refs[0].shape[1] // 2
    heads = width // DH
    step = min(DH, 2 * count)
    cols = [slice(n * DH, (n + 1) * DH) for n in range(heads)]
    targets = [[slice(m * width + n * DH, m * width + (n + 1) * DH) for n in range(heads)] for m in (0, 1)]

    def of_group(block, r0, number, memories, terms, slot0):
        column = columns(n_mp, blocks, block, width, False)
        size = memory_refs[memories[0]].shape[0] // number
        sent_ref = sent_refs[used.index(block)]

        def inputs(k):
            starts = (column(r0 + k), pl.multiple_of((block * n_mp + r0 + k) * width, width))
            return [
                pltpu.make_async_copy(
                    array.at[:, pl.ds(start, width)],
                    token_buf.at[slot0 + k, m, pl.ds(n * count, count)],
                    sems.at[0, slot0 + k, m, n],
                )
                for m, pair in enumerate(((q_ref, sq_ref), (g_ref, sg_ref)))
                for n, (array, start) in enumerate(zip(pair, starts))
            ]

        def outputs(k):
            copies = []
            for m, own in enumerate((query_grad_ref, attended_ref)):
                starts = (column(r0 + k), pl.multiple_of((2 * (r0 + k) + m) * width, width))
                for n, (array, start) in enumerate(zip((own, sent_ref), starts)):
                    copies.append(
                        pltpu.make_async_copy(
                            result_buf.at[slot0 + k, m, pl.ds(n * count, count)],
                            array.at[:, pl.ds(start, width)],
                            sems.at[1, slot0 + k, m, n],
                        )
                    )
            return copies

        def repeat(body):
            if number == 1:
                body(0, None)
            else:
                lax.fori_loop(0, number, body, None)

        def start_inputs(k, _):
            for copy in inputs(k):
                copy.start()

        def wait_outputs(k, _):
            for copy in outputs(k):
                copy.wait()

        def work(k, _):
            rows = pl.ds(pl.multiple_of(k * size, size), size)
            memory = [
                [jnp.concatenate([memory_refs[i][rows, t] for i in memories], axis=0) for t in row] for row in targets
            ]

            def tokens(m, n):
                return token_buf[slot0 + k, m, :, cols[n]]

            def scores(n):
                raw_ref[n] = dot(memory[0][n], tokens(0, n), NT)
                if n == 0:
                    for copy in inputs(k)[2:]:
                        copy.wait()
                prob_ref[n] = dot(memory[1][n], tokens(1, n), NT)

            def softmax(n):
                for begin in range(0, 2 * count, step):
                    part = slice(begin, begin + step)
                    grad_ref[n, :, part], weight_ref[n, :, part] = softmax_part(
                        raw_ref[n, :, part], prob_ref[n, :, part]
                    )

            def results(n):
                for m, pair_ref in enumerate((grad_ref, weight_ref)):
                    result = dot(memory[m][n].T, pair_ref[n], NN).astype(bf16)
                    result_buf[slot0 + k, m, :, cols[n]] = result.T

            def gradients(n):
                for m, pair_ref in enumerate((grad_ref, weight_ref)):
                    term = dot(pair_ref[n], tokens(m, n), NN)
                    for i, t in enumerate(terms):
                        term_refs[t][rows, targets[m][n]] = term[i * size : (i + 1) * size].astype(term_refs[t].dtype)

            for copy in inputs(k)[:2]:
                copy.wait()
            for n in range(heads + 2):
                if n < heads:
                    scores(n)
                if 1 <= n <= heads:
                    softmax(n - 1)
                if n >= 2:
                    results(n - 2)
                    if n <= heads:
                        gradients(n - 2)
            for copy in outputs(k):
                copy.start()
            gradients(heads - 1)

        return [functools.partial(repeat, body) for body in (start_inputs, work, wait_outputs)]

    slot0, phases = 0, []
    for group in groups:
        phases.append(of_group(*group, slot0))
        slot0 += group[2]
    for phase in zip(*phases):
        for run in phase:
            run()


def pinned(space, *arrays):
    return [pltpu.with_memory_space_constraint(array, space) for array in arrays]


HBM, VMEM = pl.BlockSpec(memory_space=pltpu.HBM), pl.BlockSpec(memory_space=pltpu.VMEM)


def attention(n_mp, blocks, groups, tokens, memory, terms, outputs, sent):
    rows, whole = tokens[0].shape
    width = memory[0].shape[1] // 2
    number = sum(n for _, _, n, *_ in groups)
    count = len(groups[0][3]) * memory[0].shape[0] // groups[0][2]
    used = sorted({block for block, *_ in groups})
    scratch = (width // DH, count, 2 * rows)
    earlier = [*outputs] + [sent[block] for block in used if block in sent]
    first = 4 + len(memory)
    results = pl.pallas_call(
        functools.partial(attention_kernel, n_mp, blocks, groups, len(memory)),
        in_specs=[HBM] * 4 + [VMEM] * len(memory) + [HBM] * len(earlier),
        out_specs=[HBM] * (2 + len(used)) + [VMEM] * len(terms),
        out_shape=[jax.ShapeDtypeStruct((rows, whole), bf16)] * 2
        + [jax.ShapeDtypeStruct((rows, whole // blocks), bf16)] * len(used)
        + [pltpu.VMEM(memory[0].shape, t) for t in terms],
        scratch_shapes=[pltpu.VMEM((number, 2, 2 * rows, width), bf16)] * 2
        + [pltpu.VMEM(scratch, t) for t in (f32, f32, bf16, bf16)]
        + [pltpu.SemaphoreType.DMA((2, number, 2, 2))],
        input_output_aliases={first + n: n for n in range(len(earlier))},
        compiler_params=pltpu.CompilerParams(vmem_limit_bytes=32 * 1024 * 1024),
        cost_estimate=pl.CostEstimate(
            flops=24 * rows * count * width * number,
            bytes_accessed=16 * rows * width * number,
            transcendentals=2 * rows * count * width * number // DH,
        ),
    )(*pinned(pltpu.HBM, *tokens[:2]), *tokens[2:], *pinned(pltpu.VMEM, *memory), *earlier)
    sent = {**sent, **dict(zip(used, results[2:]))}
    return results[:2], sent, results[2 + len(used) :]


def packing_kernel(n_mp, blocks, q_ref, g_ref, packed_q_ref, packed_g_ref, sems):
    width = packed_q_ref.shape[1] // (blocks * n_mp)
    copies = []
    for block in range(blocks):
        column = columns(n_mp, blocks, block, width, True)
        for r in range(n_mp):
            where = pl.ds((block * n_mp + r) * width, width)
            for array, packed in ((q_ref, packed_q_ref), (g_ref, packed_g_ref)):
                copies.append(
                    pltpu.make_async_copy(
                        array.at[:, pl.ds(column(r), width)], packed.at[:, where], sems.at[len(copies)]
                    )
                )
    for copy in copies:
        copy.start()
    for copy in copies:
        copy.wait()


def packing(n_mp, blocks, queries, grad):
    rows, whole = queries.shape
    return pl.pallas_call(
        functools.partial(packing_kernel, n_mp, blocks),
        in_specs=[HBM] * 2,
        out_specs=[VMEM] * 2,
        out_shape=[pltpu.VMEM((rows, whole // 2), bf16)] * 2,
        scratch_shapes=[pltpu.SemaphoreType.DMA((2 * blocks * n_mp,))],
        cost_estimate=pl.CostEstimate(flops=0, bytes_accessed=4 * rows * whole, transcendentals=0),
    )(*pinned(pltpu.HBM, queries, grad))


def joining_kernel(blocks, mine_ref, other_ref, key_ref, value_ref, sems):
    core, block = lax.axis_index("seq") & 1, mine_ref.shape[1] // (2 * blocks)
    copies = []
    for place, source in ((core, mine_ref), (1 - core, other_ref)):
        for n in range(blocks):
            where = pl.ds(pl.multiple_of((place * blocks + n) * block, block), block)
            for m, target in enumerate((key_ref, value_ref)):
                part = source.at[:, pl.ds((2 * n + m) * block, block)]
                copies.append(pltpu.make_async_copy(part, target.at[:, where], sems.at[len(copies)]))
    for copy in copies:
        copy.start()
    for copy in copies:
        copy.wait()


def joining(blocks, mine, other):
    rows, width = mine.shape
    return pl.pallas_call(
        functools.partial(joining_kernel, blocks),
        in_specs=[VMEM] * 2,
        out_specs=[HBM] * 2,
        out_shape=[jax.ShapeDtypeStruct((rows, width), bf16)] * 2,
        scratch_shapes=[pltpu.SemaphoreType.DMA((4 * blocks,))],
    )(*pinned(pltpu.VMEM, mine, other))


def placing_kernel(n_mp, blocks, *refs):
    returned_refs, (attended_ref, query_grad_ref, sems) = refs[:blocks], refs[-3:]
    width = returned_refs[0].shape[1] // (2 * n_mp)
    copies = []
    for block, returned_ref in enumerate(returned_refs):
        column = columns(n_mp, blocks, block, width, True)
        for r in range(n_mp):
            for m, target in enumerate((query_grad_ref, attended_ref)):
                start = (2 * r + m) * width
                copies.append(
                    pltpu.make_async_copy(
                        returned_ref.at[:, start : start + width],
                        target.at[:, pl.ds(column(r), width)],
                        sems.at[len(copies)],
                    )
                )
    for copy in copies:
        copy.start()
    for copy in copies:
        copy.wait()


def placing(n_mp, returned, attended, query_grad):
    blocks = len(returned)
    return pl.pallas_call(
        functools.partial(placing_kernel, n_mp, blocks),
        in_specs=[VMEM] * blocks + [HBM] * 2,
        out_specs=[HBM] * 2,
        out_shape=[jax.ShapeDtypeStruct(attended.shape, bf16)] * 2,
        scratch_shapes=[pltpu.SemaphoreType.DMA((2 * blocks * n_mp,))],
        input_output_aliases={blocks: 0, blocks + 1: 1},
    )(*pinned(pltpu.VMEM, *returned), attended, query_grad)


def together(*values):
    return lax.optimization_barrier(values)


def shards(n_seq, n_mp, queries, memory_keys, memory_values, output_grad):
    def swap(array, axis, bits):
        size = n_seq if axis == "seq" else n_mp
        return lax.ppermute(array, axis, [(i, i ^ bits) for i in range(size)])

    core_bit, x_bit = 1, 2
    z_bits = range(4, n_seq, 4)
    y_bits = [1 << b for b in range(n_mp.bit_length() - 1)]
    rows, part = memory_keys.shape
    share, blocks = part // 2, 2
    block = share // blocks
    core = lax.axis_index("seq") & 1

    def packed(keys, values):
        both = [lax.dynamic_slice_in_dim(array, core * share, share, axis=1) for array in (keys, values)]
        return jnp.concatenate([b[:, n * block : (n + 1) * block] for n in range(blocks) for b in both], axis=1)

    other = [swap(array, "seq", core_bit) for array in (memory_keys, memory_values)]
    base = jnp.concatenate([packed(memory_keys, memory_values), packed(*other)])
    base, queries_out, grad_out = together(base, queries, output_grad)
    got = [swap(base, "seq", bits) for bits in z_bits]
    tokens = (queries, output_grad)
    tokens += tuple(swap(array, "seq", core_bit) for array in packing(n_mp, blocks, queries_out, grad_out))
    got = [base] + got
    first, second = (jnp.concatenate([g[:, n * 2 * block : (n + 1) * 2 * block] for g in got]) for n in (0, 1))

    def wider(held, got):
        return jnp.concatenate([held, got])

    first_got, second_got = together(swap(first, "seq", x_bit), swap(second, "mp", y_bits[0]))
    first, second = wider(first, first_got), wider(second, second_got)
    for bits in y_bits[:-1]:
        first = wider(first, swap(first, "mp", bits))
    for bits in y_bits[1:]:
        second = wider(second, swap(second, "mp", bits))
    first_got, second_got = swap(first, "mp", y_bits[-1]), swap(second, "seq", x_bit)

    half = n_mp // 2
    outputs, sent, (first_keep,) = attention(
        n_mp, blocks, [(0, 0, half, (0,), (0,))], tokens, [first], [f32], [], {}
    )
    outputs, sent, (first_give, second_keep, second_give) = attention(
        n_mp,
        blocks,
        [(0, half, n_mp - half, (0,), (0,)), (1, 0, n_mp, (1, 2), (1, 2))],
        tokens,
        [first_got, second, second_got],
        [bf16, f32, bf16],
        outputs,
        sent,
    )
    first_got, second_got = swap(first_give, "mp", y_bits[-1]), swap(second_give, "seq", x_bit)
    first, second, sent = together(
        first_keep + first_got.astype(f32), second_keep + second_got.astype(f32), sent
    )

    def fold(total, axis, bits):
        middle = total.shape[0] // 2
        return total[:middle] + swap(total[middle:].astype(bf16), axis, bits).astype(f32)

    for bits in y_bits[-2::-1]:
        first = fold(first, "mp", bits)
    for bits in y_bits[:0:-1]:
        second = fold(second, "mp", bits)
    first, second = fold(first, "seq", x_bit), fold(second, "mp", y_bits[0])
    returned = [swap(sent[block], "seq", core_bit) for block in range(blocks)]
    first, second, returned = together(first, second, returned)
    total = jnp.concatenate([first, second], axis=1)
    outputs = placing(n_mp, returned, *outputs)
    count, give = 2 * rows, total.astype(bf16)
    got = [swap(give[n * count : (n + 1) * count], "seq", bits) for n, bits in enumerate(z_bits, 1)]
    got, outputs = together(got, outputs)
    total = (total[:count] + sum(g.astype(f32) for g in got)).astype(bf16)
    mine, other = total[:rows], swap(total[rows:], "seq", core_bit)

    return (*outputs, *joining(blocks, mine, other))


def solution(mesh):
    body = functools.partial(shards, mesh.shape["seq"], mesh.shape["mp"])
    return jax.shard_map(
        body,
        mesh=mesh,
        in_specs=(P(("seq", "mp"), None), P("seq", "mp"), P("seq", "mp"), P(("seq", "mp"), None)),
        out_specs=(P(("seq", "mp"), None), P(("seq", "mp"), None), P("seq", "mp"), P("seq", "mp")),
        check_vma=False,
    )
```

```python
import functools
import math

import jax
import jax.numpy as jnp
from jax import lax
from jax.experimental import pallas as pl
from jax.experimental.pallas import tpu as pltpu
from jax.sharding import PartitionSpec as P

DH = 128

NT = (((1,), (1,)), ((), ()))
NN = (((1,), (0,)), ((), ()))

bf16, f32 = jnp.bfloat16, jnp.float32


def dot(a, b, dims):
    return lax.dot_general(a, b, dims, preferred_element_type=f32)


def softmax_part(raw, prob_grad):
    temper = 1.0 / math.sqrt(DH)
    peak = jnp.max(raw, axis=0, keepdims=True)
    powers = jnp.exp((raw - peak) * temper)
    inverse = 1.0 / jnp.sum(powers, axis=0, keepdims=True)
    delta = jnp.sum(powers * prob_grad, axis=0, keepdims=True) * inverse
    weights = (powers * inverse).astype(bf16)
    score_grad = (powers * (inverse * temper) * (prob_grad - delta)).astype(bf16)
    return score_grad, weights


def columns(n_mp, blocks, block, width, of_sibling):
    core, my = lax.axis_index("seq") & 1, lax.axis_index("mp")
    core = 1 - core if of_sibling else core
    return lambda r: pl.multiple_of((((my ^ r) * 2 + core) * blocks + block) * width, width)


def attention_kernel(n_mp, blocks, groups, n_memory, q_ref, g_ref, sq_ref, sg_ref, *refs):
    memory_refs, refs = refs[:n_memory], refs[n_memory:]
    token_buf, result_buf, raw_ref, prob_ref, grad_ref, weight_ref, sems = refs[-7:]
    n_terms = 1 + max(max(terms) for *_, terms in groups)
    term_refs, refs = refs[-7 - n_terms : -7], refs[: -7 - n_terms]
    attended_ref, query_grad_ref, sent_ref = refs[-3:]
    count, width = q_ref.shape[0], memory_refs[0].shape[1] // 2
    heads = width // DH
    step = min(DH, 2 * count)
    cols = [slice(n * DH, (n + 1) * DH) for n in range(heads)]
    targets = [[slice(m * width + n * DH, m * width + (n + 1) * DH) for n in range(heads)] for m in (0, 1)]

    def of_group(block, r0, number, memories, terms, slot0):
        column = columns(n_mp, blocks, block, width, False)
        size = memory_refs[memories[0]].shape[0] // number

        def inputs(k):
            starts = (column(r0 + k), pl.multiple_of((block * n_mp + r0 + k) * width, width))
            return [
                pltpu.make_async_copy(
                    array.at[:, pl.ds(start, width)],
                    token_buf.at[slot0 + k, m, pl.ds(n * count, count)],
                    sems.at[0, slot0 + k, m, n],
                )
                for m, pair in enumerate(((q_ref, sq_ref), (g_ref, sg_ref)))
                for n, (array, start) in enumerate(zip(pair, starts))
            ]

        def outputs(k):
            copies = []
            for m, own in enumerate((query_grad_ref, attended_ref)):
                starts = (column(r0 + k), pl.multiple_of((2 * (block * n_mp + r0 + k) + m) * width, width))
                for n, (array, start) in enumerate(zip((own, sent_ref), starts)):
                    copies.append(
                        pltpu.make_async_copy(
                            result_buf.at[slot0 + k, m, pl.ds(n * count, count)],
                            array.at[:, pl.ds(start, width)],
                            sems.at[1, slot0 + k, m, n],
                        )
                    )
            return copies

        def repeat(body):
            if number == 1:
                body(0, None)
            else:
                lax.fori_loop(0, number, body, None)

        def start_inputs(k, _):
            for copy in inputs(k):
                copy.start()

        def wait_outputs(k, _):
            for copy in outputs(k):
                copy.wait()

        def work(k, _):
            rows = pl.ds(pl.multiple_of(k * size, size), size)
            memory = [
                [jnp.concatenate([memory_refs[i][rows, t] for i in memories], axis=0) for t in row] for row in targets
            ]

            def tokens(m, n):
                return token_buf[slot0 + k, m, :, cols[n]]

            def scores(n):
                raw_ref[n] = dot(memory[0][n], tokens(0, n), NT)
                prob_ref[n] = dot(memory[1][n], tokens(1, n), NT)

            def softmax(n):
                for begin in range(0, 2 * count, step):
                    part = slice(begin, begin + step)
                    grad_ref[n, :, part], weight_ref[n, :, part] = softmax_part(
                        raw_ref[n, :, part], prob_ref[n, :, part]
                    )

            def results(n):
                for m, pair_ref in enumerate((grad_ref, weight_ref)):
                    result = dot(memory[m][n].T, pair_ref[n], NN).astype(bf16)
                    result_buf[slot0 + k, m, :, cols[n]] = result.T

            def gradients(n):
                for m, pair_ref in enumerate((grad_ref, weight_ref)):
                    term = dot(pair_ref[n], tokens(m, n), NN)
                    for i, t in enumerate(terms):
                        term_refs[t][rows, targets[m][n]] = term[i * size : (i + 1) * size].astype(term_refs[t].dtype)

            for copy in inputs(k):
                copy.wait()
            for n in range(heads + 2):
                if n < heads:
                    scores(n)
                if 1 <= n <= heads:
                    softmax(n - 1)
                if n >= 2:
                    results(n - 2)
                    if n <= heads:
                        gradients(n - 2)
            for copy in outputs(k):
                copy.start()
            gradients(heads - 1)

        return [functools.partial(repeat, body) for body in (start_inputs, work, wait_outputs)]

    slot0, phases = 0, []
    for group in groups:
        phases.append(of_group(*group, slot0))
        slot0 += group[2]
    for phase in zip(*phases):
        for run in phase:
            run()


def pinned(space, *arrays):
    return [pltpu.with_memory_space_constraint(array, space) for array in arrays]


HBM, VMEM = pl.BlockSpec(memory_space=pltpu.HBM), pl.BlockSpec(memory_space=pltpu.VMEM)


def attention(n_mp, blocks, groups, tokens, memory, terms, outputs):
    rows, whole = tokens[0].shape
    width = memory[0].shape[1] // 2
    number = sum(n for _, _, n, *_ in groups)
    count = len(groups[0][3]) * memory[0].shape[0] // groups[0][2]
    scratch = (width // DH, count, 2 * rows)
    first = 4 + len(memory)
    results = pl.pallas_call(
        functools.partial(attention_kernel, n_mp, blocks, groups, len(memory)),
        in_specs=[HBM] * 4 + [VMEM] * len(memory) + [HBM] * len(outputs),
        out_specs=[HBM] * 3 + [VMEM] * len(terms),
        out_shape=[jax.ShapeDtypeStruct((rows, whole), bf16)] * 3
        + [pltpu.VMEM(memory[0].shape, t) for t in terms],
        scratch_shapes=[pltpu.VMEM((number, 2, 2 * rows, width), bf16)] * 2
        + [pltpu.VMEM(scratch, t) for t in (f32, f32, bf16, bf16)]
        + [pltpu.SemaphoreType.DMA((2, number, 2, 2))],
        input_output_aliases={first + n: n for n in range(len(outputs))},
        compiler_params=pltpu.CompilerParams(vmem_limit_bytes=16 * 1024 * 1024),
        cost_estimate=pl.CostEstimate(
            flops=24 * rows * count * width * number,
            bytes_accessed=16 * rows * width * number,
            transcendentals=2 * rows * count * width * number // DH,
        ),
    )(*pinned(pltpu.HBM, *tokens[:2]), *tokens[2:], *pinned(pltpu.VMEM, *memory), *outputs)
    return results[:3], results[3:]


def packing_kernel(n_mp, blocks, q_ref, g_ref, packed_q_ref, packed_g_ref, sems):
    width = packed_q_ref.shape[1] // (blocks * n_mp)
    copies = []
    for block in range(blocks):
        column = columns(n_mp, blocks, block, width, True)
        for r in range(n_mp):
            where = pl.ds((block * n_mp + r) * width, width)
            for array, packed in ((q_ref, packed_q_ref), (g_ref, packed_g_ref)):
                copies.append(
                    pltpu.make_async_copy(
                        array.at[:, pl.ds(column(r), width)], packed.at[:, where], sems.at[len(copies)]
                    )
                )
    for copy in copies:
        copy.start()
    for copy in copies:
        copy.wait()


def packing(n_mp, blocks, queries, grad):
    rows, whole = queries.shape
    return pl.pallas_call(
        functools.partial(packing_kernel, n_mp, blocks),
        in_specs=[HBM] * 2,
        out_specs=[VMEM] * 2,
        out_shape=[pltpu.VMEM((rows, whole // 2), bf16)] * 2,
        scratch_shapes=[pltpu.SemaphoreType.DMA((2 * blocks * n_mp,))],
        cost_estimate=pl.CostEstimate(flops=0, bytes_accessed=4 * rows * whole, transcendentals=0),
    )(*pinned(pltpu.HBM, queries, grad))


def joining_kernel(blocks, mine_ref, other_ref, key_ref, value_ref, sems):
    core, block = lax.axis_index("seq") & 1, mine_ref.shape[1] // (2 * blocks)
    copies = []
    for place, source in ((core, mine_ref), (1 - core, other_ref)):
        for n in range(blocks):
            where = pl.ds(pl.multiple_of((place * blocks + n) * block, block), block)
            for m, target in enumerate((key_ref, value_ref)):
                part = source.at[:, pl.ds((2 * n + m) * block, block)]
                copies.append(pltpu.make_async_copy(part, target.at[:, where], sems.at[len(copies)]))
    for copy in copies:
        copy.start()
    for copy in copies:
        copy.wait()


def joining(blocks, mine, other):
    rows, width = mine.shape
    return pl.pallas_call(
        functools.partial(joining_kernel, blocks),
        in_specs=[VMEM] * 2,
        out_specs=[HBM] * 2,
        out_shape=[jax.ShapeDtypeStruct((rows, width), bf16)] * 2,
        scratch_shapes=[pltpu.SemaphoreType.DMA((4 * blocks,))],
    )(*pinned(pltpu.VMEM, mine, other))


def placing_kernel(n_mp, blocks, returned_ref, _attended, _query_grad, attended_ref, query_grad_ref, sems):
    width = returned_ref.shape[1] // (2 * blocks * n_mp)
    copies = []
    for block in range(blocks):
        column = columns(n_mp, blocks, block, width, True)
        for r in range(n_mp):
            for m, target in enumerate((query_grad_ref, attended_ref)):
                part = returned_ref.at[:, pl.ds((2 * (block * n_mp + r) + m) * width, width)]
                copies.append(
                    pltpu.make_async_copy(part, target.at[:, pl.ds(column(r), width)], sems.at[len(copies)])
                )
    for copy in copies:
        copy.start()
    for copy in copies:
        copy.wait()


def placing(n_mp, blocks, returned, attended, query_grad):
    return pl.pallas_call(
        functools.partial(placing_kernel, n_mp, blocks),
        in_specs=[VMEM] + [HBM] * 2,
        out_specs=[HBM] * 2,
        out_shape=[jax.ShapeDtypeStruct(attended.shape, bf16)] * 2,
        scratch_shapes=[pltpu.SemaphoreType.DMA((2 * blocks * n_mp,))],
        input_output_aliases={1: 0, 2: 1},
    )(*pinned(pltpu.VMEM, returned), attended, query_grad)


def together(*values):
    return lax.optimization_barrier(values)


def shards(n_seq, n_mp, queries, memory_keys, memory_values, output_grad):
    def swap(array, axis, bits):
        size = n_seq if axis == "seq" else n_mp
        return lax.ppermute(array, axis, [(i, i ^ bits) for i in range(size)])

    core_bit, x_bit = 1, 2
    z_bits = range(4, n_seq, 4)
    y_bits = [1 << b for b in range(n_mp.bit_length() - 1)]
    rows, part = memory_keys.shape
    share, blocks = part // 2, 2
    block = share // blocks
    core = lax.axis_index("seq") & 1

    def packed(keys, values):
        both = [lax.dynamic_slice_in_dim(array, core * share, share, axis=1) for array in (keys, values)]
        return jnp.concatenate([b[:, n * block : (n + 1) * block] for n in range(blocks) for b in both], axis=1)

    other = [swap(array, "seq", core_bit) for array in (memory_keys, memory_values)]
    base = jnp.concatenate([packed(memory_keys, memory_values), packed(*other)])
    base, queries_out, grad_out = together(base, queries, output_grad)
    got = [swap(base, "seq", bits) for bits in z_bits]
    tokens = (queries, output_grad)
    tokens += tuple(swap(array, "seq", core_bit) for array in packing(n_mp, blocks, queries_out, grad_out))
    got = [base] + got
    first, second = (jnp.concatenate([g[:, n * 2 * block : (n + 1) * 2 * block] for g in got]) for n in (0, 1))

    def wider(held, got):
        return jnp.concatenate([held, got])

    first_got, second_got = together(swap(first, "seq", x_bit), swap(second, "mp", y_bits[0]))
    first, second = wider(first, first_got), wider(second, second_got)
    for bits in y_bits[:-1]:
        first = wider(first, swap(first, "mp", bits))
    for bits in y_bits[1:]:
        second = wider(second, swap(second, "mp", bits))
    first_got, second_got = swap(first, "mp", y_bits[-1]), swap(second, "seq", x_bit)

    half = n_mp // 2
    outputs, (first_keep,) = attention(n_mp, blocks, [(0, 0, half, (0,), (0,))], tokens, [first], [f32], [])
    (*outputs, sent), (first_give, second_keep, second_give) = attention(
        n_mp,
        blocks,
        [(0, half, n_mp - half, (0,), (0,)), (1, 0, n_mp, (1, 2), (1, 2))],
        tokens,
        [first_got, second, second_got],
        [bf16, f32, bf16],
        outputs,
    )
    first_got, second_got = swap(first_give, "mp", y_bits[-1]), swap(second_give, "seq", x_bit)
    first, second, sent = together(
        first_keep + first_got.astype(f32), second_keep + second_got.astype(f32), sent
    )

    def fold(total, axis, bits):
        middle = total.shape[0] // 2
        return total[:middle] + swap(total[middle:].astype(bf16), axis, bits).astype(f32)

    for bits in y_bits[-2::-1]:
        first = fold(first, "mp", bits)
    for bits in y_bits[:0:-1]:
        second = fold(second, "mp", bits)
    first, second = fold(first, "seq", x_bit), fold(second, "mp", y_bits[0])
    returned = swap(sent, "seq", core_bit)
    first, second, returned = together(first, second, returned)
    total = jnp.concatenate([first, second], axis=1)
    outputs = placing(n_mp, blocks, returned, *outputs)
    count, give = 2 * rows, total.astype(bf16)
    got = [swap(give[n * count : (n + 1) * count], "seq", bits) for n, bits in enumerate(z_bits, 1)]
    got, outputs = together(got, outputs)
    total = (total[:count] + sum(g.astype(f32) for g in got)).astype(bf16)
    mine, other = total[:rows], swap(total[rows:], "seq", core_bit)

    return (*outputs, *joining(blocks, mine, other))


def solution(mesh):
    body = functools.partial(shards, mesh.shape["seq"], mesh.shape["mp"])
    return jax.shard_map(
        body,
        mesh=mesh,
        in_specs=(P(("seq", "mp"), None), P("seq", "mp"), P("seq", "mp"), P(("seq", "mp"), None)),
        out_specs=(P(("seq", "mp"), None), P(("seq", "mp"), None), P("seq", "mp"), P("seq", "mp")),
        check_vma=False,
    )
```

```python
import functools
import math

import jax
import jax.numpy as jnp
from jax import lax
from jax.experimental import pallas as pl
from jax.experimental.pallas import tpu as pltpu
from jax.sharding import PartitionSpec as P

DH = 128

NT = (((1,), (1,)), ((), ()))
TN = (((0,), (0,)), ((), ()))
NN = (((1,), (0,)), ((), ()))

bf16, f32 = jnp.bfloat16, jnp.float32


def dot(a, b, dims):
    return lax.dot_general(a, b, dims, preferred_element_type=f32)


def softmax_part(raw, prob_grad):
    temper = 1.0 / math.sqrt(DH)
    peak = jnp.max(raw, axis=0, keepdims=True)
    powers = jnp.exp((raw - peak) * temper)
    inverse = 1.0 / jnp.sum(powers, axis=0, keepdims=True)
    delta = jnp.sum(powers * prob_grad, axis=0, keepdims=True) * inverse
    weights = (powers * inverse).astype(bf16)
    score_grad = (powers * (inverse * temper) * (prob_grad - delta)).astype(bf16)
    return score_grad, weights


def columns(n_mp, blocks, block, width, of_sibling):
    core, my = lax.axis_index("seq") & 1, lax.axis_index("mp")
    core = 1 - core if of_sibling else core
    return lambda r: pl.multiple_of((((my ^ r) * 2 + core) * blocks + block) * width, width)


def attention_kernel(n_mp, blocks, groups, n_memory, q_ref, g_ref, sq_ref, sg_ref, *refs):
    used = sorted({block for block, *_ in groups})
    memory_refs, refs = refs[:n_memory], refs[n_memory:]
    token_buf, result_buf, raw_ref, prob_ref, grad_ref, weight_ref, sems = refs[-7:]
    n_terms = 1 + max(max(terms) for *_, terms in groups)
    term_refs, refs = refs[-7 - n_terms : -7], refs[: -7 - n_terms]
    attended_ref, query_grad_ref, *sent_refs = refs[-2 - len(used) :]
    count, width = q_ref.shape[0], memory_refs[0].shape[1] // 2
    heads = width // DH
    step = min(DH, 2 * count)
    cols = [slice(n * DH, (n + 1) * DH) for n in range(heads)]
    targets = [[slice(m * width + n * DH, m * width + (n + 1) * DH) for n in range(heads)] for m in (0, 1)]

    def of_group(block, r0, number, memories, terms, slot0):
        column = columns(n_mp, blocks, block, width, False)
        size = memory_refs[memories[0]].shape[0] // number
        sent_ref = sent_refs[used.index(block)]

        def inputs(k):
            starts = (column(r0 + k), pl.multiple_of((block * n_mp + r0 + k) * width, width))
            return [
                pltpu.make_async_copy(
                    array.at[:, pl.ds(start, width)],
                    token_buf.at[slot0 + k, m, pl.ds(n * count, count)],
                    sems.at[0, slot0 + k, m, n],
                )
                for m, pair in enumerate(((q_ref, sq_ref), (g_ref, sg_ref)))
                for n, (array, start) in enumerate(zip(pair, starts))
            ]

        def outputs(k):
            copies = []
            for m, own in enumerate((query_grad_ref, attended_ref)):
                starts = (column(r0 + k), pl.multiple_of((2 * (r0 + k) + m) * width, width))
                for n, (array, start) in enumerate(zip((own, sent_ref), starts)):
                    copies.append(
                        pltpu.make_async_copy(
                            result_buf.at[slot0 + k, m, pl.ds(n * count, count)],
                            array.at[:, pl.ds(start, width)],
                            sems.at[1, slot0 + k, m, n],
                        )
                    )
            return copies

        def repeat(body):
            if number == 1:
                body(0, None)
            else:
                lax.fori_loop(0, number, body, None)

        def start_inputs(k, _):
            for copy in inputs(k):
                copy.start()

        def wait_outputs(k, _):
            for copy in outputs(k):
                copy.wait()

        def work(k, _):
            rows = pl.ds(pl.multiple_of(k * size, size), size)
            memory = [
                [jnp.concatenate([memory_refs[i][rows, t] for i in memories], axis=0) for t in row] for row in targets
            ]

            def tokens(m, n):
                return token_buf[slot0 + k, m, :, cols[n]]

            def scores(n):
                raw_ref[n] = dot(memory[0][n], tokens(0, n), NT)
                prob_ref[n] = dot(memory[1][n], tokens(1, n), NT)

            def softmax(n):
                for begin in range(0, 2 * count, step):
                    part = slice(begin, begin + step)
                    grad_ref[n, :, part], weight_ref[n, :, part] = softmax_part(
                        raw_ref[n, :, part], prob_ref[n, :, part]
                    )

            def results(n):
                for m, pair_ref in enumerate((grad_ref, weight_ref)):
                    result_buf[slot0 + k, m, :, cols[n]] = dot(pair_ref[n], memory[m][n], TN).astype(bf16)

            def gradients(n):
                for m, pair_ref in enumerate((grad_ref, weight_ref)):
                    term = dot(pair_ref[n], tokens(m, n), NN)
                    for i, t in enumerate(terms):
                        term_refs[t][rows, targets[m][n]] = term[i * size : (i + 1) * size].astype(term_refs[t].dtype)

            for copy in inputs(k):
                copy.wait()
            for n in range(heads + 2):
                if n < heads:
                    scores(n)
                if 1 <= n <= heads:
                    softmax(n - 1)
                if n >= 2:
                    results(n - 2)
                    if n <= heads:
                        gradients(n - 2)
            for copy in outputs(k):
                copy.start()
            gradients(heads - 1)

        return [functools.partial(repeat, body) for body in (start_inputs, work, wait_outputs)]

    slot0, phases = 0, []
    for group in groups:
        phases.append(of_group(*group, slot0))
        slot0 += group[2]
    for phase in zip(*phases):
        for run in phase:
            run()


def pinned(space, *arrays):
    return [pltpu.with_memory_space_constraint(array, space) for array in arrays]


HBM, VMEM = pl.BlockSpec(memory_space=pltpu.HBM), pl.BlockSpec(memory_space=pltpu.VMEM)


def attention(n_mp, blocks, groups, tokens, memory, terms, outputs, sent):
    rows, whole = tokens[0].shape
    width = memory[0].shape[1] // 2
    number = sum(n for _, _, n, *_ in groups)
    count = len(groups[0][3]) * memory[0].shape[0] // groups[0][2]
    used = sorted({block for block, *_ in groups})
    scratch = (width // DH, count, 2 * rows)
    earlier = [*outputs] + [sent[block] for block in used if block in sent]
    first = 4 + len(memory)
    results = pl.pallas_call(
        functools.partial(attention_kernel, n_mp, blocks, groups, len(memory)),
        in_specs=[HBM] * 4 + [VMEM] * len(memory) + [HBM] * len(earlier),
        out_specs=[HBM] * (2 + len(used)) + [VMEM] * len(terms),
        out_shape=[jax.ShapeDtypeStruct((rows, whole), bf16)] * 2
        + [jax.ShapeDtypeStruct((rows, whole // blocks), bf16)] * len(used)
        + [pltpu.VMEM(memory[0].shape, t) for t in terms],
        scratch_shapes=[pltpu.VMEM((number, 2, 2 * rows, width), bf16)] * 2
        + [pltpu.VMEM(scratch, t) for t in (f32, f32, bf16, bf16)]
        + [pltpu.SemaphoreType.DMA((2, number, 2, 2))],
        input_output_aliases={first + n: n for n in range(len(earlier))},
        compiler_params=pltpu.CompilerParams(vmem_limit_bytes=32 * 1024 * 1024),
        cost_estimate=pl.CostEstimate(
            flops=24 * rows * count * width * number,
            bytes_accessed=16 * rows * width * number,
            transcendentals=2 * rows * count * width * number // DH,
        ),
    )(*pinned(pltpu.HBM, *tokens[:2]), *tokens[2:], *pinned(pltpu.VMEM, *memory), *earlier)
    sent = {**sent, **dict(zip(used, results[2:]))}
    return results[:2], sent, results[2 + len(used) :]


def packing_kernel(n_mp, blocks, q_ref, g_ref, packed_q_ref, packed_g_ref, sems):
    width = packed_q_ref.shape[1] // (blocks * n_mp)
    copies = []
    for block in range(blocks):
        column = columns(n_mp, blocks, block, width, True)
        for r in range(n_mp):
            where = pl.ds((block * n_mp + r) * width, width)
            for array, packed in ((q_ref, packed_q_ref), (g_ref, packed_g_ref)):
                copies.append(
                    pltpu.make_async_copy(
                        array.at[:, pl.ds(column(r), width)], packed.at[:, where], sems.at[len(copies)]
                    )
                )
    for copy in copies:
        copy.start()
    for copy in copies:
        copy.wait()


def packing(n_mp, blocks, queries, grad):
    rows, whole = queries.shape
    return pl.pallas_call(
        functools.partial(packing_kernel, n_mp, blocks),
        in_specs=[HBM] * 2,
        out_specs=[VMEM] * 2,
        out_shape=[pltpu.VMEM((rows, whole // 2), bf16)] * 2,
        scratch_shapes=[pltpu.SemaphoreType.DMA((2 * blocks * n_mp,))],
        cost_estimate=pl.CostEstimate(flops=0, bytes_accessed=4 * rows * whole, transcendentals=0),
    )(*pinned(pltpu.HBM, queries, grad))


def joining_kernel(blocks, mine_ref, other_ref, key_ref, value_ref, sems):
    core, block = lax.axis_index("seq") & 1, mine_ref.shape[1] // (2 * blocks)
    copies = []
    for place, source in ((core, mine_ref), (1 - core, other_ref)):
        for n in range(blocks):
            where = pl.ds(pl.multiple_of((place * blocks + n) * block, block), block)
            for m, target in enumerate((key_ref, value_ref)):
                part = source.at[:, pl.ds((2 * n + m) * block, block)]
                copies.append(pltpu.make_async_copy(part, target.at[:, where], sems.at[len(copies)]))
    for copy in copies:
        copy.start()
    for copy in copies:
        copy.wait()


def joining(blocks, mine, other):
    rows, width = mine.shape
    return pl.pallas_call(
        functools.partial(joining_kernel, blocks),
        in_specs=[VMEM] * 2,
        out_specs=[HBM] * 2,
        out_shape=[jax.ShapeDtypeStruct((rows, width), bf16)] * 2,
        scratch_shapes=[pltpu.SemaphoreType.DMA((4 * blocks,))],
    )(*pinned(pltpu.VMEM, mine, other))


def placing_kernel(n_mp, blocks, *refs):
    returned_refs, (attended_ref, query_grad_ref, sems) = refs[:blocks], refs[-3:]
    width = returned_refs[0].shape[1] // (2 * n_mp)
    copies = []
    for block, returned_ref in enumerate(returned_refs):
        column = columns(n_mp, blocks, block, width, True)
        for r in range(n_mp):
            for m, target in enumerate((query_grad_ref, attended_ref)):
                start = (2 * r + m) * width
                copies.append(
                    pltpu.make_async_copy(
                        returned_ref.at[:, start : start + width],
                        target.at[:, pl.ds(column(r), width)],
                        sems.at[len(copies)],
                    )
                )
    for copy in copies:
        copy.start()
    for copy in copies:
        copy.wait()


def placing(n_mp, returned, attended, query_grad):
    blocks = len(returned)
    return pl.pallas_call(
        functools.partial(placing_kernel, n_mp, blocks),
        in_specs=[VMEM] * blocks + [HBM] * 2,
        out_specs=[HBM] * 2,
        out_shape=[jax.ShapeDtypeStruct(attended.shape, bf16)] * 2,
        scratch_shapes=[pltpu.SemaphoreType.DMA((2 * blocks * n_mp,))],
        input_output_aliases={blocks: 0, blocks + 1: 1},
    )(*pinned(pltpu.VMEM, *returned), attended, query_grad)


def together(*values):
    return lax.optimization_barrier(values)


def shards(n_seq, n_mp, queries, memory_keys, memory_values, output_grad):
    def swap(array, axis, bits):
        size = n_seq if axis == "seq" else n_mp
        return lax.ppermute(array, axis, [(i, i ^ bits) for i in range(size)])

    core_bit, x_bit = 1, 2
    z_bits = range(4, n_seq, 4)
    y_bits = [1 << b for b in range(n_mp.bit_length() - 1)]
    rows, part = memory_keys.shape
    share, blocks = part // 2, 2
    block = share // blocks
    core = lax.axis_index("seq") & 1

    def packed(keys, values):
        both = [lax.dynamic_slice_in_dim(array, core * share, share, axis=1) for array in (keys, values)]
        return jnp.concatenate([b[:, n * block : (n + 1) * block] for n in range(blocks) for b in both], axis=1)

    other = [swap(array, "seq", core_bit) for array in (memory_keys, memory_values)]
    base = jnp.concatenate([packed(memory_keys, memory_values), packed(*other)])
    base, queries_out, grad_out = together(base, queries, output_grad)
    got = [swap(base, "seq", bits) for bits in z_bits]
    tokens = (queries, output_grad)
    tokens += tuple(swap(array, "seq", core_bit) for array in packing(n_mp, blocks, queries_out, grad_out))
    got = [base] + got
    first, second = (jnp.concatenate([g[:, n * 2 * block : (n + 1) * 2 * block] for g in got]) for n in (0, 1))

    def wider(held, got):
        return jnp.concatenate([held, got])

    first_got, second_got = together(swap(first, "seq", x_bit), swap(second, "mp", y_bits[0]))
    first, second = wider(first, first_got), wider(second, second_got)
    for bits in y_bits[:-1]:
        first = wider(first, swap(first, "mp", bits))
    for bits in y_bits[1:]:
        second = wider(second, swap(second, "mp", bits))
    first_got, second_got = swap(first, "mp", y_bits[-1]), swap(second, "seq", x_bit)

    half = n_mp // 2
    outputs, sent, (first_keep,) = attention(
        n_mp, blocks, [(0, 0, half, (0,), (0,))], tokens, [first], [f32], [], {}
    )
    outputs, sent, (first_give, second_keep, second_give) = attention(
        n_mp,
        blocks,
        [(0, half, n_mp - half, (0,), (0,)), (1, 0, n_mp, (1, 2), (1, 2))],
        tokens,
        [first_got, second, second_got],
        [bf16, f32, bf16],
        outputs,
        sent,
    )
    first_got, second_got = swap(first_give, "mp", y_bits[-1]), swap(second_give, "seq", x_bit)
    first, second, sent = together(
        first_keep + first_got.astype(f32), second_keep + second_got.astype(f32), sent
    )

    def fold(total, axis, bits):
        middle = total.shape[0] // 2
        return total[:middle] + swap(total[middle:].astype(bf16), axis, bits).astype(f32)

    for bits in y_bits[-2::-1]:
        first = fold(first, "mp", bits)
    for bits in y_bits[:0:-1]:
        second = fold(second, "mp", bits)
    first, second = fold(first, "seq", x_bit), fold(second, "mp", y_bits[0])
    returned = [swap(sent[block], "seq", core_bit) for block in range(blocks)]
    first, second, returned = together(first, second, returned)
    total = jnp.concatenate([first, second], axis=1)
    outputs = placing(n_mp, returned, *outputs)
    count, give = 2 * rows, total.astype(bf16)
    got = [swap(give[n * count : (n + 1) * count], "seq", bits) for n, bits in enumerate(z_bits, 1)]
    got, outputs = together(got, outputs)
    total = (total[:count] + sum(g.astype(f32) for g in got)).astype(bf16)
    mine, other = total[:rows], swap(total[rows:], "seq", core_bit)

    return (*outputs, *joining(blocks, mine, other))


def solution(mesh):
    body = functools.partial(shards, mesh.shape["seq"], mesh.shape["mp"])
    return jax.shard_map(
        body,
        mesh=mesh,
        in_specs=(P(("seq", "mp"), None), P("seq", "mp"), P("seq", "mp"), P(("seq", "mp"), None)),
        out_specs=(P(("seq", "mp"), None), P(("seq", "mp"), None), P("seq", "mp"), P("seq", "mp")),
        check_vma=False,
    )
```

```python
import functools
import math

import jax
import jax.numpy as jnp
from jax import lax
from jax.experimental import pallas as pl
from jax.experimental.pallas import tpu as pltpu
from jax.sharding import PartitionSpec as P

DH = 128

NT = (((1,), (1,)), ((), ()))
NN = (((1,), (0,)), ((), ()))

bf16, f32 = jnp.bfloat16, jnp.float32


def dot(a, b, dims):
    return lax.dot_general(a, b, dims, preferred_element_type=f32)


def softmax_part(raw, prob_grad):
    temper = 1.0 / math.sqrt(DH)
    peak = jnp.max(raw, axis=0, keepdims=True)
    powers = jnp.exp((raw - peak) * temper)
    inverse = 1.0 / jnp.sum(powers, axis=0, keepdims=True)
    delta = jnp.sum(powers * prob_grad, axis=0, keepdims=True) * inverse
    weights = (powers * inverse).astype(bf16)
    score_grad = (powers * (inverse * temper) * (prob_grad - delta)).astype(bf16)
    return score_grad, weights


def columns(n_mp, blocks, block, width, of_sibling):
    core, my = lax.axis_index("seq") & 1, lax.axis_index("mp")
    core = 1 - core if of_sibling else core
    return lambda r: pl.multiple_of((((my ^ r) * 2 + core) * blocks + block) * width, width)


def attention_kernel(n_mp, blocks, groups, n_memory, with_outputs, q_ref, g_ref, sq_ref, sg_ref, *refs):
    used = sorted({block for block, *_ in groups})
    memory_refs, refs = refs[:n_memory], refs[n_memory:]
    token_buf, result_buf, raw_ref, prob_ref, grad_ref, weight_ref, sems = refs[-7:]
    n_terms = max([1 + t for *_, terms in groups for t in terms], default=0)
    term_refs, refs = refs[len(refs) - 7 - n_terms : -7], refs[: len(refs) - 7 - n_terms]
    if with_outputs:
        attended_ref, query_grad_ref, *sent_refs = refs[-2 - len(used) :]
    count, width = q_ref.shape[0], memory_refs[0].shape[1] // 2
    heads = width // DH
    step = min(DH, 2 * count)
    cols = [slice(n * DH, (n + 1) * DH) for n in range(heads)]
    targets = [[slice(m * width + n * DH, m * width + (n + 1) * DH) for n in range(heads)] for m in (0, 1)]

    def of_group(block, r0, number, memories, terms, slot0):
        column = columns(n_mp, blocks, block, width, False)
        size = memory_refs[memories[0]].shape[0] // number
        sent_ref = sent_refs[used.index(block)] if with_outputs else None

        def inputs(k):
            starts = (column(r0 + k), pl.multiple_of((block * n_mp + r0 + k) * width, width))
            return [
                pltpu.make_async_copy(
                    array.at[:, pl.ds(start, width)],
                    token_buf.at[slot0 + k, m, pl.ds(n * count, count)],
                    sems.at[0, slot0 + k, m, n],
                )
                for m, pair in enumerate(((q_ref, sq_ref), (g_ref, sg_ref)))
                for n, (array, start) in enumerate(zip(pair, starts))
            ]

        def outputs(k):
            copies = []
            for m, own in enumerate((query_grad_ref, attended_ref)):
                starts = (column(r0 + k), pl.multiple_of((2 * (r0 + k) + m) * width, width))
                for n, (array, start) in enumerate(zip((own, sent_ref), starts)):
                    copies.append(
                        pltpu.make_async_copy(
                            result_buf.at[slot0 + k, m, pl.ds(n * count, count)],
                            array.at[:, pl.ds(start, width)],
                            sems.at[1, slot0 + k, m, n],
                        )
                    )
            return copies

        def repeat(body):
            if number == 1:
                body(0, None)
            else:
                lax.fori_loop(0, number, body, None)

        def start_inputs(k, _):
            for copy in inputs(k):
                copy.start()

        def wait_outputs(k, _):
            for copy in outputs(k):
                copy.wait()

        def work(k, _):
            rows = pl.ds(pl.multiple_of(k * size, size), size)
            memory = [
                [jnp.concatenate([memory_refs[i][rows, t] for i in memories], axis=0) for t in row] for row in targets
            ]

            def tokens(m, n):
                return token_buf[slot0 + k, m, :, cols[n]]

            def scores(n):
                raw_ref[n] = dot(memory[0][n], tokens(0, n), NT)
                prob_ref[n] = dot(memory[1][n], tokens(1, n), NT)

            def softmax(n):
                for begin in range(0, 2 * count, step):
                    part = slice(begin, begin + step)
                    grad_ref[n, :, part], weight_ref[n, :, part] = softmax_part(
                        raw_ref[n, :, part], prob_ref[n, :, part]
                    )

            def results(n):
                for m, pair_ref in enumerate((grad_ref, weight_ref)):
                    result = dot(memory[m][n].T, pair_ref[n], NN).astype(bf16)
                    result_buf[slot0 + k, m, :, cols[n]] = result.T

            def gradients(n):
                for m, pair_ref in enumerate((grad_ref, weight_ref) if terms else ()):
                    term = dot(pair_ref[n], tokens(m, n), NN)
                    for i, t in enumerate(terms):
                        term_refs[t][rows, targets[m][n]] = term[i * size : (i + 1) * size].astype(term_refs[t].dtype)

            for copy in inputs(k):
                copy.wait()
            for n in range(heads + 2):
                if n < heads:
                    scores(n)
                if 1 <= n <= heads:
                    softmax(n - 1)
                if n >= 2 and with_outputs:
                    results(n - 2)
                if 2 <= n <= heads:
                    gradients(n - 2)
            if with_outputs:
                for copy in outputs(k):
                    copy.start()
            gradients(heads - 1)

        bodies = (start_inputs, work) + ((wait_outputs,) if with_outputs else ())
        return [functools.partial(repeat, body) for body in bodies]

    slot0, phases = 0, []
    for group in groups:
        phases.append(of_group(*group, slot0))
        slot0 += group[2]
    for phase in zip(*phases):
        for run in phase:
            run()


def pinned(space, *arrays):
    return [pltpu.with_memory_space_constraint(array, space) for array in arrays]


HBM, VMEM = pl.BlockSpec(memory_space=pltpu.HBM), pl.BlockSpec(memory_space=pltpu.VMEM)


def attention(n_mp, blocks, groups, tokens, memory, terms, outputs, sent):
    with_outputs = outputs is not None
    rows, whole = tokens[0].shape
    width = memory[0].shape[1] // 2
    number = sum(n for _, _, n, *_ in groups)
    count = len(groups[0][3]) * memory[0].shape[0] // groups[0][2]
    used = sorted({block for block, *_ in groups})
    scratch = (width // DH, count, 2 * rows)
    earlier = [*outputs] + [sent[block] for block in used if block in sent] if with_outputs else []
    token_outs = [jax.ShapeDtypeStruct((rows, whole), bf16)] * 2
    token_outs += [jax.ShapeDtypeStruct((rows, whole // blocks), bf16)] * len(used)
    token_outs = token_outs if with_outputs else []
    first = 4 + len(memory)
    results = pl.pallas_call(
        functools.partial(attention_kernel, n_mp, blocks, groups, len(memory), with_outputs),
        in_specs=[HBM] * 4 + [VMEM] * len(memory) + [HBM] * len(earlier),
        out_specs=[HBM] * len(token_outs) + [VMEM] * len(terms),
        out_shape=token_outs
        + [pltpu.VMEM(memory[0].shape, t) for t in terms],
        scratch_shapes=[pltpu.VMEM((number, 2, 2 * rows, width), bf16)] * 2
        + [pltpu.VMEM(scratch, t) for t in (f32, f32, bf16, bf16)]
        + [pltpu.SemaphoreType.DMA((2, number, 2, 2))],
        input_output_aliases={first + n: n for n in range(len(earlier))},
        compiler_params=pltpu.CompilerParams(vmem_limit_bytes=32 * 1024 * 1024),
        cost_estimate=pl.CostEstimate(
            flops=24 * rows * count * width * number,
            bytes_accessed=16 * rows * width * number,
            transcendentals=2 * rows * count * width * number // DH,
        ),
    )(*pinned(pltpu.HBM, *tokens[:2]), *tokens[2:], *pinned(pltpu.VMEM, *memory), *earlier)
    if not with_outputs:
        return outputs, sent, results
    sent = {**sent, **dict(zip(used, results[2:]))}
    return results[:2], sent, results[2 + len(used) :]


def packing_kernel(n_mp, blocks, q_ref, g_ref, packed_q_ref, packed_g_ref, sems):
    width = packed_q_ref.shape[1] // (blocks * n_mp)
    copies = []
    for block in range(blocks):
        column = columns(n_mp, blocks, block, width, True)
        for r in range(n_mp):
            where = pl.ds((block * n_mp + r) * width, width)
            for array, packed in ((q_ref, packed_q_ref), (g_ref, packed_g_ref)):
                copies.append(
                    pltpu.make_async_copy(
                        array.at[:, pl.ds(column(r), width)], packed.at[:, where], sems.at[len(copies)]
                    )
                )
    for copy in copies:
        copy.start()
    for copy in copies:
        copy.wait()


def packing(n_mp, blocks, queries, grad):
    rows, whole = queries.shape
    return pl.pallas_call(
        functools.partial(packing_kernel, n_mp, blocks),
        in_specs=[HBM] * 2,
        out_specs=[VMEM] * 2,
        out_shape=[pltpu.VMEM((rows, whole // 2), bf16)] * 2,
        scratch_shapes=[pltpu.SemaphoreType.DMA((2 * blocks * n_mp,))],
        cost_estimate=pl.CostEstimate(flops=0, bytes_accessed=4 * rows * whole, transcendentals=0),
    )(*pinned(pltpu.HBM, queries, grad))


def joining_kernel(blocks, mine_ref, other_ref, key_ref, value_ref, sems):
    core, block = lax.axis_index("seq") & 1, mine_ref.shape[1] // (2 * blocks)
    copies = []
    for place, source in ((core, mine_ref), (1 - core, other_ref)):
        for n in range(blocks):
            where = pl.ds(pl.multiple_of((place * blocks + n) * block, block), block)
            for m, target in enumerate((key_ref, value_ref)):
                part = source.at[:, pl.ds((2 * n + m) * block, block)]
                copies.append(pltpu.make_async_copy(part, target.at[:, where], sems.at[len(copies)]))
    for copy in copies:
        copy.start()
    for copy in copies:
        copy.wait()


def joining(blocks, mine, other):
    rows, width = mine.shape
    return pl.pallas_call(
        functools.partial(joining_kernel, blocks),
        in_specs=[VMEM] * 2,
        out_specs=[HBM] * 2,
        out_shape=[jax.ShapeDtypeStruct((rows, width), bf16)] * 2,
        scratch_shapes=[pltpu.SemaphoreType.DMA((4 * blocks,))],
    )(*pinned(pltpu.VMEM, mine, other))


def placing_kernel(n_mp, blocks, *refs):
    returned_refs, (attended_ref, query_grad_ref, sems) = refs[:blocks], refs[-3:]
    width = returned_refs[0].shape[1] // (2 * n_mp)
    copies = []
    for block, returned_ref in enumerate(returned_refs):
        column = columns(n_mp, blocks, block, width, True)
        for r in range(n_mp):
            for m, target in enumerate((query_grad_ref, attended_ref)):
                start = (2 * r + m) * width
                copies.append(
                    pltpu.make_async_copy(
                        returned_ref.at[:, start : start + width],
                        target.at[:, pl.ds(column(r), width)],
                        sems.at[len(copies)],
                    )
                )
    for copy in copies:
        copy.start()
    for copy in copies:
        copy.wait()


def placing(n_mp, returned, attended, query_grad):
    blocks = len(returned)
    return pl.pallas_call(
        functools.partial(placing_kernel, n_mp, blocks),
        in_specs=[VMEM] * blocks + [HBM] * 2,
        out_specs=[HBM] * 2,
        out_shape=[jax.ShapeDtypeStruct(attended.shape, bf16)] * 2,
        scratch_shapes=[pltpu.SemaphoreType.DMA((2 * blocks * n_mp,))],
        input_output_aliases={blocks: 0, blocks + 1: 1},
    )(*pinned(pltpu.VMEM, *returned), attended, query_grad)


def together(*values):
    return lax.optimization_barrier(values)


def shards(n_seq, n_mp, queries, memory_keys, memory_values, output_grad):
    def swap(array, axis, bits):
        size = n_seq if axis == "seq" else n_mp
        return lax.ppermute(array, axis, [(i, i ^ bits) for i in range(size)])

    core_bit, x_bit = 1, 2
    z_bits = range(4, n_seq, 4)
    y_bits = [1 << b for b in range(n_mp.bit_length() - 1)]
    rows, part = memory_keys.shape
    share, blocks = part // 2, 2
    block = share // blocks
    core = lax.axis_index("seq") & 1

    def packed(keys, values):
        both = [lax.dynamic_slice_in_dim(array, core * share, share, axis=1) for array in (keys, values)]
        return jnp.concatenate([b[:, n * block : (n + 1) * block] for n in range(blocks) for b in both], axis=1)

    other = [swap(array, "seq", core_bit) for array in (memory_keys, memory_values)]
    base = jnp.concatenate([packed(memory_keys, memory_values), packed(*other)])
    base, queries_out, grad_out = together(base, queries, output_grad)
    got = [swap(base, "seq", bits) for bits in z_bits]
    tokens = (queries, output_grad)
    tokens += tuple(swap(array, "seq", core_bit) for array in packing(n_mp, blocks, queries_out, grad_out))
    got = [base] + got
    first, second = (jnp.concatenate([g[:, n * 2 * block : (n + 1) * 2 * block] for g in got]) for n in (0, 1))

    def wider(held, got):
        return jnp.concatenate([held, got])

    first_got, second_got = together(swap(first, "seq", x_bit), swap(second, "mp", y_bits[0]))
    first, second = wider(first, first_got), wider(second, second_got)
    for bits in y_bits[:-1]:
        first = wider(first, swap(first, "mp", bits))
    for bits in y_bits[1:]:
        second = wider(second, swap(second, "mp", bits))
    first_got, second_got = swap(first, "mp", y_bits[-1]), swap(second, "seq", x_bit)

    half = n_mp // 2
    outputs, sent, (first_keep,) = attention(
        n_mp, blocks, [(0, 0, half, (0,), (0,))], tokens, [first], [f32], [], {}
    )
    rest = [(0, half, n_mp - half, (0,), (0,)), (1, 0, n_mp, (1, 2), (1, 2))]
    first_keep, second = together(first_keep, second)
    memory = [first_got, second, second_got]
    *_, (first_give, second_keep, second_give) = attention(
        n_mp, blocks, rest, tokens, memory, [bf16, f32, bf16], None, {}
    )
    outputs, sent, _ = attention(
        n_mp, blocks, [(*group[:4], ()) for group in rest], tokens, memory, [], outputs, sent
    )
    first_got, second_got = swap(first_give, "mp", y_bits[-1]), swap(second_give, "seq", x_bit)
    first, second, sent = together(
        first_keep + first_got.astype(f32), second_keep + second_got.astype(f32), sent
    )

    def fold(total, axis, bits):
        middle = total.shape[0] // 2
        return total[:middle] + swap(total[middle:].astype(bf16), axis, bits).astype(f32)

    for bits in y_bits[-2::-1]:
        first = fold(first, "mp", bits)
    for bits in y_bits[:0:-1]:
        second = fold(second, "mp", bits)
    first, second = fold(first, "seq", x_bit), fold(second, "mp", y_bits[0])
    returned = [swap(sent[block], "seq", core_bit) for block in range(blocks)]
    first, second, returned = together(first, second, returned)
    total = jnp.concatenate([first, second], axis=1)
    outputs = placing(n_mp, returned, *outputs)
    count, give = 2 * rows, total.astype(bf16)
    got = [swap(give[n * count : (n + 1) * count], "seq", bits) for n, bits in enumerate(z_bits, 1)]
    got, outputs = together(got, outputs)
    total = (total[:count] + sum(g.astype(f32) for g in got)).astype(bf16)
    mine, other = total[:rows], swap(total[rows:], "seq", core_bit)

    return (*outputs, *joining(blocks, mine, other))


def solution(mesh):
    body = functools.partial(shards, mesh.shape["seq"], mesh.shape["mp"])
    return jax.shard_map(
        body,
        mesh=mesh,
        in_specs=(P(("seq", "mp"), None), P("seq", "mp"), P("seq", "mp"), P(("seq", "mp"), None)),
        out_specs=(P(("seq", "mp"), None), P(("seq", "mp"), None), P("seq", "mp"), P("seq", "mp")),
        check_vma=False,
    )
```

```python
import functools
import math

import jax
import jax.numpy as jnp
from jax import lax
from jax.experimental import pallas as pl
from jax.experimental.pallas import tpu as pltpu
from jax.sharding import PartitionSpec as P

DH = 128

NT = (((1,), (1,)), ((), ()))
NN = (((1,), (0,)), ((), ()))

bf16, f32 = jnp.bfloat16, jnp.float32


def dot(a, b, dims):
    return lax.dot_general(a, b, dims, preferred_element_type=f32)


def softmax_part(raw, prob_grad):
    temper = 1.0 / math.sqrt(DH)
    peak = jnp.max(raw, axis=0, keepdims=True)
    powers = jnp.exp((raw - peak) * temper)
    inverse = 1.0 / jnp.sum(powers, axis=0, keepdims=True)
    delta = jnp.sum(powers * prob_grad, axis=0, keepdims=True) * inverse
    weights = (powers * inverse).astype(bf16)
    score_grad = (powers * (inverse * temper) * (prob_grad - delta)).astype(bf16)
    return score_grad, weights


def columns(n_mp, blocks, block, width, of_sibling):
    core, my = lax.axis_index("seq") & 1, lax.axis_index("mp")
    core = 1 - core if of_sibling else core
    return lambda r: pl.multiple_of((((my ^ r) * 2 + core) * blocks + block) * width, width)


def attention_kernel(n_mp, blocks, groups, n_memory, with_outputs, q_ref, g_ref, sq_ref, sg_ref, *refs):
    used = sorted({block for block, *_ in groups})
    memory_refs, refs = refs[:n_memory], refs[n_memory:]
    token_buf, result_buf, raw_ref, prob_ref, grad_ref, weight_ref, sems = refs[-7:]
    n_terms = max([1 + t for *_, terms in groups for t in terms if t is not None], default=0)
    term_refs, refs = refs[len(refs) - 7 - n_terms : -7], refs[: len(refs) - 7 - n_terms]
    if with_outputs:
        attended_ref, query_grad_ref, *sent_refs = refs[-2 - len(used) :]
    count, width = q_ref.shape[0], memory_refs[0].shape[1] // 2
    heads = width // DH
    step = min(DH, 2 * count)
    cols = [slice(n * DH, (n + 1) * DH) for n in range(heads)]
    targets = [[slice(m * width + n * DH, m * width + (n + 1) * DH) for n in range(heads)] for m in (0, 1)]

    def of_group(block, r0, number, memories, terms, slot0):
        column = columns(n_mp, blocks, block, width, False)
        size = memory_refs[memories[0]].shape[0] // number
        sent_ref = sent_refs[used.index(block)] if with_outputs else None

        def inputs(k):
            starts = (column(r0 + k), pl.multiple_of((block * n_mp + r0 + k) * width, width))
            return [
                pltpu.make_async_copy(
                    array.at[:, pl.ds(start, width)],
                    token_buf.at[slot0 + k, m, pl.ds(n * count, count)],
                    sems.at[0, slot0 + k, m, n],
                )
                for m, pair in enumerate(((q_ref, sq_ref), (g_ref, sg_ref)))
                for n, (array, start) in enumerate(zip(pair, starts))
            ]

        def outputs(k):
            copies = []
            for m, own in enumerate((query_grad_ref, attended_ref)):
                starts = (column(r0 + k), pl.multiple_of((2 * (r0 + k) + m) * width, width))
                for n, (array, start) in enumerate(zip((own, sent_ref), starts)):
                    copies.append(
                        pltpu.make_async_copy(
                            result_buf.at[slot0 + k, m, pl.ds(n * count, count)],
                            array.at[:, pl.ds(start, width)],
                            sems.at[1, slot0 + k, m, n],
                        )
                    )
            return copies

        def repeat(body):
            if number == 1:
                body(0, None)
            else:
                lax.fori_loop(0, number, body, None)

        def start_inputs(k, _):
            for copy in inputs(k):
                copy.start()

        def wait_outputs(k, _):
            for copy in outputs(k):
                copy.wait()

        def work(k, _):
            rows = pl.ds(pl.multiple_of(k * size, size), size)
            memory = [
                [jnp.concatenate([memory_refs[i][rows, t] for i in memories], axis=0) for t in row] for row in targets
            ]

            def tokens(m, n):
                return token_buf[slot0 + k, m, :, cols[n]]

            def scores(n):
                raw_ref[n] = dot(memory[0][n], tokens(0, n), NT)
                prob_ref[n] = dot(memory[1][n], tokens(1, n), NT)

            def softmax(n):
                for begin in range(0, 2 * count, step):
                    part = slice(begin, begin + step)
                    grad_ref[n, :, part], weight_ref[n, :, part] = softmax_part(
                        raw_ref[n, :, part], prob_ref[n, :, part]
                    )

            def results(n):
                for m, pair_ref in enumerate((grad_ref, weight_ref)):
                    result = dot(memory[m][n].T, pair_ref[n], NN).astype(bf16)
                    result_buf[slot0 + k, m, :, cols[n]] = result.T

            def gradients(n):
                for m, pair_ref in enumerate((grad_ref, weight_ref) if terms else ()):
                    if None not in terms:
                        whole = dot(pair_ref[n], tokens(m, n), NN)
                    for i, t in enumerate(terms):
                        if t is None:
                            continue
                        part = slice(i * size, (i + 1) * size)
                        term = dot(pair_ref[n, part], tokens(m, n), NN) if None in terms else whole[part]
                        term_refs[t][rows, targets[m][n]] = term.astype(term_refs[t].dtype)

            for copy in inputs(k):
                copy.wait()
            for n in range(heads + 2):
                if n < heads:
                    scores(n)
                if 1 <= n <= heads:
                    softmax(n - 1)
                if n >= 2 and with_outputs:
                    results(n - 2)
                if 2 <= n <= heads:
                    gradients(n - 2)
            if with_outputs:
                for copy in outputs(k):
                    copy.start()
            gradients(heads - 1)

        bodies = (start_inputs, work) + ((wait_outputs,) if with_outputs else ())
        return [functools.partial(repeat, body) for body in bodies]

    slot0, phases = 0, []
    for group in groups:
        phases.append(of_group(*group, slot0))
        slot0 += group[2]
    for phase in zip(*phases):
        for run in phase:
            run()


def pinned(space, *arrays):
    return [pltpu.with_memory_space_constraint(array, space) for array in arrays]


HBM, VMEM = pl.BlockSpec(memory_space=pltpu.HBM), pl.BlockSpec(memory_space=pltpu.VMEM)


def attention(n_mp, blocks, groups, tokens, memory, terms, outputs, sent):
    with_outputs = outputs is not None
    rows, whole = tokens[0].shape
    width = memory[0].shape[1] // 2
    number = sum(n for _, _, n, *_ in groups)
    count = len(groups[0][3]) * memory[0].shape[0] // groups[0][2]
    used = sorted({block for block, *_ in groups})
    scratch = (width // DH, count, 2 * rows)
    earlier = [*outputs] + [sent[block] for block in used if block in sent] if with_outputs else []
    token_outs = [jax.ShapeDtypeStruct((rows, whole), bf16)] * 2
    token_outs += [jax.ShapeDtypeStruct((rows, whole // blocks), bf16)] * len(used)
    token_outs = token_outs if with_outputs else []
    first = 4 + len(memory)
    results = pl.pallas_call(
        functools.partial(attention_kernel, n_mp, blocks, groups, len(memory), with_outputs),
        in_specs=[HBM] * 4 + [VMEM] * len(memory) + [HBM] * len(earlier),
        out_specs=[HBM] * len(token_outs) + [VMEM] * len(terms),
        out_shape=token_outs
        + [pltpu.VMEM(memory[0].shape, t) for t in terms],
        scratch_shapes=[pltpu.VMEM((number, 2, 2 * rows, width), bf16)] * 2
        + [pltpu.VMEM(scratch, t) for t in (f32, f32, bf16, bf16)]
        + [pltpu.SemaphoreType.DMA((2, number, 2, 2))],
        input_output_aliases={first + n: n for n in range(len(earlier))},
        compiler_params=pltpu.CompilerParams(vmem_limit_bytes=32 * 1024 * 1024),
        cost_estimate=pl.CostEstimate(
            flops=24 * rows * count * width * number,
            bytes_accessed=16 * rows * width * number,
            transcendentals=2 * rows * count * width * number // DH,
        ),
    )(*pinned(pltpu.HBM, *tokens[:2]), *tokens[2:], *pinned(pltpu.VMEM, *memory), *earlier)
    if not with_outputs:
        return outputs, sent, results
    sent = {**sent, **dict(zip(used, results[2:]))}
    return results[:2], sent, results[2 + len(used) :]


def packing_kernel(n_mp, blocks, q_ref, g_ref, packed_q_ref, packed_g_ref, sems):
    width = packed_q_ref.shape[1] // (blocks * n_mp)
    copies = []
    for block in range(blocks):
        column = columns(n_mp, blocks, block, width, True)
        for r in range(n_mp):
            where = pl.ds((block * n_mp + r) * width, width)
            for array, packed in ((q_ref, packed_q_ref), (g_ref, packed_g_ref)):
                copies.append(
                    pltpu.make_async_copy(
                        array.at[:, pl.ds(column(r), width)], packed.at[:, where], sems.at[len(copies)]
                    )
                )
    for copy in copies:
        copy.start()
    for copy in copies:
        copy.wait()


def packing(n_mp, blocks, queries, grad):
    rows, whole = queries.shape
    return pl.pallas_call(
        functools.partial(packing_kernel, n_mp, blocks),
        in_specs=[HBM] * 2,
        out_specs=[VMEM] * 2,
        out_shape=[pltpu.VMEM((rows, whole // 2), bf16)] * 2,
        scratch_shapes=[pltpu.SemaphoreType.DMA((2 * blocks * n_mp,))],
        cost_estimate=pl.CostEstimate(flops=0, bytes_accessed=4 * rows * whole, transcendentals=0),
    )(*pinned(pltpu.HBM, queries, grad))


def joining_kernel(blocks, mine_ref, other_ref, key_ref, value_ref, sems):
    core, block = lax.axis_index("seq") & 1, mine_ref.shape[1] // (2 * blocks)
    copies = []
    for place, source in ((core, mine_ref), (1 - core, other_ref)):
        for n in range(blocks):
            where = pl.ds(pl.multiple_of((place * blocks + n) * block, block), block)
            for m, target in enumerate((key_ref, value_ref)):
                part = source.at[:, pl.ds((2 * n + m) * block, block)]
                copies.append(pltpu.make_async_copy(part, target.at[:, where], sems.at[len(copies)]))
    for copy in copies:
        copy.start()
    for copy in copies:
        copy.wait()


def joining(blocks, mine, other):
    rows, width = mine.shape
    return pl.pallas_call(
        functools.partial(joining_kernel, blocks),
        in_specs=[VMEM] * 2,
        out_specs=[HBM] * 2,
        out_shape=[jax.ShapeDtypeStruct((rows, width), bf16)] * 2,
        scratch_shapes=[pltpu.SemaphoreType.DMA((4 * blocks,))],
    )(*pinned(pltpu.VMEM, mine, other))


def placing_kernel(n_mp, blocks, *refs):
    returned_refs, (attended_ref, query_grad_ref, sems) = refs[:blocks], refs[-3:]
    width = returned_refs[0].shape[1] // (2 * n_mp)
    copies = []
    for block, returned_ref in enumerate(returned_refs):
        column = columns(n_mp, blocks, block, width, True)
        for r in range(n_mp):
            for m, target in enumerate((query_grad_ref, attended_ref)):
                start = (2 * r + m) * width
                copies.append(
                    pltpu.make_async_copy(
                        returned_ref.at[:, start : start + width],
                        target.at[:, pl.ds(column(r), width)],
                        sems.at[len(copies)],
                    )
                )
    for copy in copies:
        copy.start()
    for copy in copies:
        copy.wait()


def placing(n_mp, returned, attended, query_grad):
    blocks = len(returned)
    return pl.pallas_call(
        functools.partial(placing_kernel, n_mp, blocks),
        in_specs=[VMEM] * blocks + [HBM] * 2,
        out_specs=[HBM] * 2,
        out_shape=[jax.ShapeDtypeStruct(attended.shape, bf16)] * 2,
        scratch_shapes=[pltpu.SemaphoreType.DMA((2 * blocks * n_mp,))],
        input_output_aliases={blocks: 0, blocks + 1: 1},
    )(*pinned(pltpu.VMEM, *returned), attended, query_grad)


def together(*values):
    return lax.optimization_barrier(values)


def shards(n_seq, n_mp, queries, memory_keys, memory_values, output_grad):
    def swap(array, axis, bits):
        size = n_seq if axis == "seq" else n_mp
        return lax.ppermute(array, axis, [(i, i ^ bits) for i in range(size)])

    core_bit, x_bit = 1, 2
    z_bits = range(4, n_seq, 4)
    y_bits = [1 << b for b in range(n_mp.bit_length() - 1)]
    rows, part = memory_keys.shape
    share, blocks = part // 2, 2
    block = share // blocks
    core = lax.axis_index("seq") & 1

    def packed(keys, values):
        both = [lax.dynamic_slice_in_dim(array, core * share, share, axis=1) for array in (keys, values)]
        return jnp.concatenate([b[:, n * block : (n + 1) * block] for n in range(blocks) for b in both], axis=1)

    other = [swap(array, "seq", core_bit) for array in (memory_keys, memory_values)]
    base = jnp.concatenate([packed(memory_keys, memory_values), packed(*other)])
    base, queries_out, grad_out = together(base, queries, output_grad)
    got = [swap(base, "seq", bits) for bits in z_bits]
    tokens = (queries, output_grad)
    tokens += tuple(swap(array, "seq", core_bit) for array in packing(n_mp, blocks, queries_out, grad_out))
    got = [base] + got
    first, second = (jnp.concatenate([g[:, n * 2 * block : (n + 1) * 2 * block] for g in got]) for n in (0, 1))

    def wider(held, got):
        return jnp.concatenate([held, got])

    first_got, second_got = together(swap(first, "seq", x_bit), swap(second, "mp", y_bits[0]))
    first, second = wider(first, first_got), wider(second, second_got)
    for bits in y_bits[:-1]:
        first = wider(first, swap(first, "mp", bits))
    for bits in y_bits[1:]:
        second = wider(second, swap(second, "mp", bits))
    first_got, second_got = swap(first, "mp", y_bits[-1]), swap(second, "seq", x_bit)

    half = n_mp // 2
    outputs, sent, (first_keep,) = attention(
        n_mp, blocks, [(0, 0, half, (0,), (0,))], tokens, [first], [f32], [], {}
    )
    first_keep, second = together(first_keep, second)
    of_first = (0, half, n_mp - half, (0,))
    *_, (first_give, second_give) = attention(
        n_mp,
        blocks,
        [(*of_first, (0,)), (1, 0, n_mp, (1, 2), (None, 1))],
        tokens,
        [first_got, second, second_got],
        [bf16, bf16],
        None,
        {},
    )
    outputs, sent, (second_keep,) = attention(
        n_mp, blocks, [(1, 0, n_mp, (0, 1), (0, None))], tokens, [second, second_got], [f32], outputs, sent
    )
    first_terms, second_terms = swap(first_give, "mp", y_bits[-1]), swap(second_give, "seq", x_bit)
    first, second, sent[1], first_got = together(
        first_keep + first_terms.astype(f32), second_keep + second_terms.astype(f32), sent[1], first_got
    )
    outputs, sent, _ = attention(n_mp, blocks, [(*of_first, ())], tokens, [first_got], [], outputs, sent)

    def fold(total, axis, bits):
        middle = total.shape[0] // 2
        return total[:middle] + swap(total[middle:].astype(bf16), axis, bits).astype(f32)

    for bits in y_bits[-2::-1]:
        first = fold(first, "mp", bits)
    for bits in y_bits[:0:-1]:
        second = fold(second, "mp", bits)
    first, second = fold(first, "seq", x_bit), fold(second, "mp", y_bits[0])
    first, second, sent[0], returned = together(first, second, sent[0], swap(sent[1], "seq", core_bit))
    returned = [swap(sent[0], "seq", core_bit), returned]
    total = jnp.concatenate([first, second], axis=1)
    outputs = placing(n_mp, returned, *outputs)
    count, give = 2 * rows, total.astype(bf16)
    got = [swap(give[n * count : (n + 1) * count], "seq", bits) for n, bits in enumerate(z_bits, 1)]
    got, outputs = together(got, outputs)
    total = (total[:count] + sum(g.astype(f32) for g in got)).astype(bf16)
    mine, other = total[:rows], swap(total[rows:], "seq", core_bit)

    return (*outputs, *joining(blocks, mine, other))


def solution(mesh):
    body = functools.partial(shards, mesh.shape["seq"], mesh.shape["mp"])
    return jax.shard_map(
        body,
        mesh=mesh,
        in_specs=(P(("seq", "mp"), None), P("seq", "mp"), P("seq", "mp"), P(("seq", "mp"), None)),
        out_specs=(P(("seq", "mp"), None), P(("seq", "mp"), None), P("seq", "mp"), P("seq", "mp")),
        check_vma=False,
    )
```

```python
import functools
import math

import jax
import jax.numpy as jnp
from jax import lax
from jax.experimental import pallas as pl
from jax.experimental.pallas import tpu as pltpu
from jax.sharding import PartitionSpec as P

DH = 128

NT = (((1,), (1,)), ((), ()))
NN = (((1,), (0,)), ((), ()))

bf16, f32 = jnp.bfloat16, jnp.float32


def dot(a, b, dims):
    return lax.dot_general(a, b, dims, preferred_element_type=f32)


def softmax_part(raw, prob_grad):
    temper = 1.0 / math.sqrt(DH)
    peak = jnp.max(raw, axis=0, keepdims=True)
    powers = jnp.exp((raw - peak) * temper)
    inverse = 1.0 / jnp.sum(powers, axis=0, keepdims=True)
    delta = jnp.sum(powers * prob_grad, axis=0, keepdims=True) * inverse
    weights = (powers * inverse).astype(bf16)
    score_grad = (powers * (inverse * temper) * (prob_grad - delta)).astype(bf16)
    return score_grad, weights


def columns(n_mp, blocks, block, width, of_sibling):
    core, my = lax.axis_index("seq") & 1, lax.axis_index("mp")
    core = 1 - core if of_sibling else core
    return lambda r: pl.multiple_of((((my ^ r) * 2 + core) * blocks + block) * width, width)


def attention_kernel(n_mp, blocks, groups, n_memory, with_outputs, q_ref, g_ref, sq_ref, sg_ref, *refs):
    used = sorted({block for block, *_ in groups})
    memory_refs, refs = refs[:n_memory], refs[n_memory:]
    token_buf, result_buf, raw_ref, prob_ref, grad_ref, weight_ref, sems = refs[-7:]
    n_terms = max([1 + t for *_, terms in groups for t in terms if t is not None], default=0)
    term_refs, refs = refs[len(refs) - 7 - n_terms : -7], refs[: len(refs) - 7 - n_terms]
    if with_outputs:
        attended_ref, query_grad_ref, *sent_refs = refs[-2 - len(used) :]
    count, width = q_ref.shape[0], memory_refs[0].shape[1] // 2
    heads = width // DH
    step = min(DH, 2 * count)
    cols = [slice(n * DH, (n + 1) * DH) for n in range(heads)]
    targets = [[slice(m * width + n * DH, m * width + (n + 1) * DH) for n in range(heads)] for m in (0, 1)]

    def of_group(block, r0, number, memories, terms, slot0):
        column = columns(n_mp, blocks, block, width, False)
        size = memory_refs[memories[0]].shape[0] // number
        sent_ref = sent_refs[used.index(block)] if with_outputs else None

        def inputs(k):
            starts = (column(r0 + k), pl.multiple_of((block * n_mp + r0 + k) * width, width))
            return [
                pltpu.make_async_copy(
                    array.at[:, pl.ds(start, width)],
                    token_buf.at[slot0 + k, m, pl.ds(n * count, count)],
                    sems.at[0, slot0 + k, m, n],
                )
                for m, pair in enumerate(((q_ref, sq_ref), (g_ref, sg_ref)))
                for n, (array, start) in enumerate(zip(pair, starts))
            ]

        def outputs(k):
            copies = []
            for m, own in enumerate((query_grad_ref, attended_ref)):
                starts = (column(r0 + k), pl.multiple_of((2 * (r0 + k) + m) * width, width))
                for n, (array, start) in enumerate(zip((own, sent_ref), starts)):
                    copies.append(
                        pltpu.make_async_copy(
                            result_buf.at[slot0 + k, m, pl.ds(n * count, count)],
                            array.at[:, pl.ds(start, width)],
                            sems.at[1, slot0 + k, m, n],
                        )
                    )
            return copies

        def repeat(body):
            if number == 1:
                body(0, None)
            else:
                lax.fori_loop(0, number, body, None)

        def start_inputs(k, _):
            for copy in inputs(k):
                copy.start()

        def wait_outputs(k, _):
            for copy in outputs(k):
                copy.wait()

        def work(k, _):
            rows = pl.ds(pl.multiple_of(k * size, size), size)
            memory = [
                [jnp.concatenate([memory_refs[i][rows, t] for i in memories], axis=0) for t in row] for row in targets
            ]

            def tokens(m, n):
                return token_buf[slot0 + k, m, :, cols[n]]

            def scores(n):
                raw_ref[n] = dot(memory[0][n], tokens(0, n), NT)
                prob_ref[n] = dot(memory[1][n], tokens(1, n), NT)

            def softmax(n):
                for begin in range(0, 2 * count, step):
                    part = slice(begin, begin + step)
                    grad_ref[n, :, part], weight_ref[n, :, part] = softmax_part(
                        raw_ref[n, :, part], prob_ref[n, :, part]
                    )

            def results(n):
                for m, pair_ref in enumerate((grad_ref, weight_ref)):
                    result = dot(memory[m][n].T, pair_ref[n], NN).astype(bf16)
                    result_buf[slot0 + k, m, :, cols[n]] = result.T

            def gradients(n):
                for m, pair_ref in enumerate((grad_ref, weight_ref) if terms else ()):
                    if None not in terms:
                        whole = dot(pair_ref[n], tokens(m, n), NN)
                    for i, t in enumerate(terms):
                        if t is None:
                            continue
                        part = slice(i * size, (i + 1) * size)
                        term = dot(pair_ref[n, part], tokens(m, n), NN) if None in terms else whole[part]
                        term_refs[t][rows, targets[m][n]] = term.astype(term_refs[t].dtype)

            for copy in inputs(k):
                copy.wait()
            for n in range(heads + 2):
                if n < heads:
                    scores(n)
                if 1 <= n <= heads:
                    softmax(n - 1)
                if n >= 2 and with_outputs:
                    results(n - 2)
                if 2 <= n <= heads:
                    gradients(n - 2)
            if with_outputs:
                for copy in outputs(k):
                    copy.start()
            gradients(heads - 1)

        bodies = (start_inputs, work) + ((wait_outputs,) if with_outputs else ())
        return [functools.partial(repeat, body) for body in bodies]

    slot0, phases = 0, []
    for group in groups:
        phases.append(of_group(*group, slot0))
        slot0 += group[2]
    for phase in zip(*phases):
        for run in phase:
            run()


def pinned(space, *arrays):
    return [pltpu.with_memory_space_constraint(array, space) for array in arrays]


HBM, VMEM = pl.BlockSpec(memory_space=pltpu.HBM), pl.BlockSpec(memory_space=pltpu.VMEM)


def attention(n_mp, blocks, groups, tokens, memory, terms, outputs, sent):
    with_outputs = outputs is not None
    rows, whole = tokens[0].shape
    width = memory[0].shape[1] // 2
    number = sum(n for _, _, n, *_ in groups)
    count = len(groups[0][3]) * memory[0].shape[0] // groups[0][2]
    used = sorted({block for block, *_ in groups})
    scratch = (width // DH, count, 2 * rows)
    earlier = [*outputs] + [sent[block] for block in used if block in sent] if with_outputs else []
    token_outs = [jax.ShapeDtypeStruct((rows, whole), bf16)] * 2
    token_outs += [jax.ShapeDtypeStruct((rows, whole // blocks), bf16)] * len(used)
    token_outs = token_outs if with_outputs else []
    first = 4 + len(memory)
    results = pl.pallas_call(
        functools.partial(attention_kernel, n_mp, blocks, groups, len(memory), with_outputs),
        in_specs=[HBM] * 4 + [VMEM] * len(memory) + [HBM] * len(earlier),
        out_specs=[HBM] * len(token_outs) + [VMEM] * len(terms),
        out_shape=token_outs
        + [pltpu.VMEM(memory[0].shape, t) for t in terms],
        scratch_shapes=[pltpu.VMEM((number, 2, 2 * rows, width), bf16)] * 2
        + [pltpu.VMEM(scratch, t) for t in (f32, f32, bf16, bf16)]
        + [pltpu.SemaphoreType.DMA((2, number, 2, 2))],
        input_output_aliases={first + n: n for n in range(len(earlier))},
        compiler_params=pltpu.CompilerParams(vmem_limit_bytes=32 * 1024 * 1024),
        cost_estimate=pl.CostEstimate(
            flops=24 * rows * count * width * number,
            bytes_accessed=16 * rows * width * number,
            transcendentals=2 * rows * count * width * number // DH,
        ),
    )(*pinned(pltpu.HBM, *tokens[:2]), *tokens[2:], *pinned(pltpu.VMEM, *memory), *earlier)
    if not with_outputs:
        return outputs, sent, results
    sent = {**sent, **dict(zip(used, results[2:]))}
    return results[:2], sent, results[2 + len(used) :]


def packing_kernel(n_mp, blocks, q_ref, g_ref, packed_q_ref, packed_g_ref, sems):
    width = packed_q_ref.shape[1] // (blocks * n_mp)
    copies = []
    for block in range(blocks):
        column = columns(n_mp, blocks, block, width, True)
        for r in range(n_mp):
            where = pl.ds((block * n_mp + r) * width, width)
            for array, packed in ((q_ref, packed_q_ref), (g_ref, packed_g_ref)):
                copies.append(
                    pltpu.make_async_copy(
                        array.at[:, pl.ds(column(r), width)], packed.at[:, where], sems.at[len(copies)]
                    )
                )
    for copy in copies:
        copy.start()
    for copy in copies:
        copy.wait()


def packing(n_mp, blocks, queries, grad):
    rows, whole = queries.shape
    return pl.pallas_call(
        functools.partial(packing_kernel, n_mp, blocks),
        in_specs=[HBM] * 2,
        out_specs=[VMEM] * 2,
        out_shape=[pltpu.VMEM((rows, whole // 2), bf16)] * 2,
        scratch_shapes=[pltpu.SemaphoreType.DMA((2 * blocks * n_mp,))],
        cost_estimate=pl.CostEstimate(flops=0, bytes_accessed=4 * rows * whole, transcendentals=0),
    )(*pinned(pltpu.HBM, queries, grad))


def joining_kernel(blocks, mine_ref, other_ref, key_ref, value_ref, sems):
    core, block = lax.axis_index("seq") & 1, mine_ref.shape[1] // (2 * blocks)
    copies = []
    for place, source in ((core, mine_ref), (1 - core, other_ref)):
        for n in range(blocks):
            where = pl.ds(pl.multiple_of((place * blocks + n) * block, block), block)
            for m, target in enumerate((key_ref, value_ref)):
                part = source.at[:, pl.ds((2 * n + m) * block, block)]
                copies.append(pltpu.make_async_copy(part, target.at[:, where], sems.at[len(copies)]))
    for copy in copies:
        copy.start()
    for copy in copies:
        copy.wait()


def joining(blocks, mine, other):
    rows, width = mine.shape
    return pl.pallas_call(
        functools.partial(joining_kernel, blocks),
        in_specs=[VMEM] * 2,
        out_specs=[HBM] * 2,
        out_shape=[jax.ShapeDtypeStruct((rows, width), bf16)] * 2,
        scratch_shapes=[pltpu.SemaphoreType.DMA((4 * blocks,))],
    )(*pinned(pltpu.VMEM, mine, other))


def placing_kernel(n_mp, blocks, *refs):
    returned_refs, (attended_ref, query_grad_ref, sems) = refs[:blocks], refs[-3:]
    width = returned_refs[0].shape[1] // (2 * n_mp)
    copies = []
    for block, returned_ref in enumerate(returned_refs):
        column = columns(n_mp, blocks, block, width, True)
        for r in range(n_mp):
            for m, target in enumerate((query_grad_ref, attended_ref)):
                start = (2 * r + m) * width
                copies.append(
                    pltpu.make_async_copy(
                        returned_ref.at[:, start : start + width],
                        target.at[:, pl.ds(column(r), width)],
                        sems.at[len(copies)],
                    )
                )
    for copy in copies:
        copy.start()
    for copy in copies:
        copy.wait()


def placing(n_mp, returned, attended, query_grad):
    blocks = len(returned)
    return pl.pallas_call(
        functools.partial(placing_kernel, n_mp, blocks),
        in_specs=[VMEM] * blocks + [HBM] * 2,
        out_specs=[HBM] * 2,
        out_shape=[jax.ShapeDtypeStruct(attended.shape, bf16)] * 2,
        scratch_shapes=[pltpu.SemaphoreType.DMA((2 * blocks * n_mp,))],
        input_output_aliases={blocks: 0, blocks + 1: 1},
    )(*pinned(pltpu.VMEM, *returned), attended, query_grad)


def together(*values):
    return lax.optimization_barrier(values)


def shards(n_seq, n_mp, queries, memory_keys, memory_values, output_grad):
    def swap(array, axis, bits):
        size = n_seq if axis == "seq" else n_mp
        return lax.ppermute(array, axis, [(i, i ^ bits) for i in range(size)])

    core_bit, x_bit = 1, 2
    z_bits = range(n_seq - 4, 0, -4)
    y_bits = [1 << b for b in range(n_mp.bit_length() - 1)]
    rows, part = memory_keys.shape
    share, blocks = part // 2, 2
    block = share // blocks
    core = lax.axis_index("seq") & 1

    def packed(keys, values):
        both = [lax.dynamic_slice_in_dim(array, core * share, share, axis=1) for array in (keys, values)]
        return jnp.concatenate([b[:, n * block : (n + 1) * block] for n in range(blocks) for b in both], axis=1)

    other = [swap(array, "seq", core_bit) for array in (memory_keys, memory_values)]
    base = jnp.concatenate([packed(memory_keys, memory_values), packed(*other)])
    base, queries_out, grad_out = together(base, queries, output_grad)
    got = [swap(base, "seq", bits) for bits in z_bits]
    tokens = (queries, output_grad)
    tokens += tuple(swap(array, "seq", core_bit) for array in packing(n_mp, blocks, queries_out, grad_out))
    got = [base] + got
    first, second = (jnp.concatenate([g[:, n * 2 * block : (n + 1) * 2 * block] for g in got]) for n in (0, 1))

    def wider(held, got):
        return jnp.concatenate([held, got])

    first_got, second_got = together(swap(first, "seq", x_bit), swap(second, "mp", y_bits[0]))
    first, second = wider(first, first_got), wider(second, second_got)
    for bits in y_bits[:-1]:
        first = wider(first, swap(first, "mp", bits))
    for bits in y_bits[1:]:
        second = wider(second, swap(second, "mp", bits))
    first_got, second_got = swap(first, "mp", y_bits[-1]), swap(second, "seq", x_bit)

    half = n_mp // 2
    outputs, sent, (first_keep,) = attention(
        n_mp, blocks, [(0, 0, half, (0,), (0,))], tokens, [first], [f32], [], {}
    )
    first_keep, second = together(first_keep, second)
    of_first = (0, half, n_mp - half, (0,))
    *_, (first_give, second_give) = attention(
        n_mp,
        blocks,
        [(*of_first, (0,)), (1, 0, n_mp, (1, 2), (None, 1))],
        tokens,
        [first_got, second, second_got],
        [bf16, bf16],
        None,
        {},
    )
    outputs, sent, (second_keep,) = attention(
        n_mp, blocks, [(1, 0, n_mp, (0, 1), (0, None))], tokens, [second, second_got], [f32], outputs, sent
    )
    first_terms, second_terms = swap(first_give, "mp", y_bits[-1]), swap(second_give, "seq", x_bit)
    first, second, sent[1], first_got = together(
        first_keep + first_terms.astype(f32), second_keep + second_terms.astype(f32), sent[1], first_got
    )
    outputs, sent, _ = attention(n_mp, blocks, [(*of_first, ())], tokens, [first_got], [], outputs, sent)

    def fold(total, axis, bits):
        middle = total.shape[0] // 2
        return total[:middle] + swap(total[middle:].astype(bf16), axis, bits).astype(f32)

    for bits in y_bits[-2::-1]:
        first = fold(first, "mp", bits)
    for bits in y_bits[:0:-1]:
        second = fold(second, "mp", bits)
    first, second = fold(first, "seq", x_bit), fold(second, "mp", y_bits[0])
    first, second, sent[0], returned = together(first, second, sent[0], swap(sent[1], "seq", core_bit))
    returned = [swap(sent[0], "seq", core_bit), returned]
    total = jnp.concatenate([first, second], axis=1)
    outputs = placing(n_mp, returned, *outputs)
    count, give = 2 * rows, total.astype(bf16)
    got = [swap(give[n * count : (n + 1) * count], "seq", bits) for n, bits in enumerate(z_bits, 1)]
    got, outputs = together(got, outputs)
    total = (total[:count] + sum(g.astype(f32) for g in got)).astype(bf16)
    mine, other = total[:rows], swap(total[rows:], "seq", core_bit)

    return (*outputs, *joining(blocks, mine, other))


def solution(mesh):
    body = functools.partial(shards, mesh.shape["seq"], mesh.shape["mp"])
    return jax.shard_map(
        body,
        mesh=mesh,
        in_specs=(P(("seq", "mp"), None), P("seq", "mp"), P("seq", "mp"), P(("seq", "mp"), None)),
        out_specs=(P(("seq", "mp"), None), P(("seq", "mp"), None), P("seq", "mp"), P("seq", "mp")),
        check_vma=False,
    )
```

```python
import functools
import math

import jax
import jax.numpy as jnp
from jax import lax
from jax.experimental import pallas as pl
from jax.experimental.pallas import tpu as pltpu
from jax.sharding import PartitionSpec as P

DH = 128

NT = (((1,), (1,)), ((), ()))
NN = (((1,), (0,)), ((), ()))

bf16, f32 = jnp.bfloat16, jnp.float32


def dot(a, b, dims):
    return lax.dot_general(a, b, dims, preferred_element_type=f32)


def softmax_part(raw, prob_grad):
    temper = 1.0 / math.sqrt(DH)
    peak = jnp.max(raw, axis=0, keepdims=True)
    powers = jnp.exp((raw - peak) * temper)
    inverse = 1.0 / jnp.sum(powers, axis=0, keepdims=True)
    delta = jnp.sum(powers * prob_grad, axis=0, keepdims=True) * inverse
    weights = (powers * inverse).astype(bf16)
    score_grad = (powers * (inverse * temper) * (prob_grad - delta)).astype(bf16)
    return score_grad, weights


def columns(n_mp, blocks, block, width, of_sibling):
    core, my = lax.axis_index("seq") & 1, lax.axis_index("mp")
    core = 1 - core if of_sibling else core
    return lambda r: pl.multiple_of((((my ^ r) * 2 + core) * blocks + block) * width, width)


def attention_kernel(n_mp, blocks, groups, n_memory, with_outputs, q_ref, g_ref, sq_ref, sg_ref, *refs):
    used = sorted({block for block, *_ in groups})
    memory_refs, refs = refs[:n_memory], refs[n_memory:]
    token_buf, result_buf, raw_ref, prob_ref, grad_ref, weight_ref, sems = refs[-7:]
    n_terms = max([1 + t for *_, terms in groups for t in terms if t is not None], default=0)
    term_refs, refs = refs[len(refs) - 7 - n_terms : -7], refs[: len(refs) - 7 - n_terms]
    if with_outputs:
        attended_ref, query_grad_ref, *sent_refs = refs[-2 - len(used) :]
    count, width = q_ref.shape[0], memory_refs[0].shape[1] // 2
    heads = width // DH
    step = min(DH, 2 * count)
    cols = [slice(n * DH, (n + 1) * DH) for n in range(heads)]
    targets = [[slice(m * width + n * DH, m * width + (n + 1) * DH) for n in range(heads)] for m in (0, 1)]

    def of_group(block, r0, number, memories, terms, slot0):
        column = columns(n_mp, blocks, block, width, False)
        size = memory_refs[memories[0]].shape[0] // number
        sent_ref = sent_refs[used.index(block)] if with_outputs else None

        def inputs(k):
            starts = (column(r0 + k), pl.multiple_of((block * n_mp + r0 + k) * width, width))
            return [
                pltpu.make_async_copy(
                    array.at[:, pl.ds(start, width)],
                    token_buf.at[slot0 + k, m, pl.ds(n * count, count)],
                    sems.at[0, slot0 + k, m, n],
                )
                for m, pair in enumerate(((q_ref, sq_ref), (g_ref, sg_ref)))
                for n, (array, start) in enumerate(zip(pair, starts))
            ]

        def outputs(k):
            copies = []
            for m, own in enumerate((query_grad_ref, attended_ref)):
                starts = (column(r0 + k), pl.multiple_of((2 * (r0 + k) + m) * width, width))
                for n, (array, start) in enumerate(zip((own, sent_ref), starts)):
                    copies.append(
                        pltpu.make_async_copy(
                            result_buf.at[slot0 + k, m, pl.ds(n * count, count)],
                            array.at[:, pl.ds(start, width)],
                            sems.at[1, slot0 + k, m, n],
                        )
                    )
            return copies

        def repeat(body):
            if number == 1:
                body(0, None)
            else:
                lax.fori_loop(0, number, body, None)

        def start_inputs(k, _):
            for copy in inputs(k):
                copy.start()

        def wait_outputs(k, _):
            for copy in outputs(k):
                copy.wait()

        def work(k, _):
            rows = pl.ds(pl.multiple_of(k * size, size), size)
            memory = [
                [jnp.concatenate([memory_refs[i][rows, t] for i in memories], axis=0) for t in row] for row in targets
            ]

            def tokens(m, n):
                return token_buf[slot0 + k, m, :, cols[n]]

            def scores(n):
                raw_ref[n] = dot(memory[0][n], tokens(0, n), NT)
                prob_ref[n] = dot(memory[1][n], tokens(1, n), NT)

            def softmax(n):
                for begin in range(0, 2 * count, step):
                    part = slice(begin, begin + step)
                    grad_ref[n, :, part], weight_ref[n, :, part] = softmax_part(
                        raw_ref[n, :, part], prob_ref[n, :, part]
                    )

            def results(n):
                for m, pair_ref in enumerate((grad_ref, weight_ref)):
                    result = dot(memory[m][n].T, pair_ref[n], NN).astype(bf16)
                    result_buf[slot0 + k, m, :, cols[n]] = result.T

            def gradients(n):
                for m, pair_ref in enumerate((grad_ref, weight_ref) if terms else ()):
                    if None not in terms:
                        whole = dot(pair_ref[n], tokens(m, n), NN)
                    for i, t in enumerate(terms):
                        if t is None:
                            continue
                        part = slice(i * size, (i + 1) * size)
                        term = dot(pair_ref[n, part], tokens(m, n), NN) if None in terms else whole[part]
                        term_refs[t][rows, targets[m][n]] = term.astype(term_refs[t].dtype)

            for copy in inputs(k):
                copy.wait()
            for n in range(heads + 2):
                if n < heads:
                    scores(n)
                if 1 <= n <= heads:
                    softmax(n - 1)
                if n >= 2 and with_outputs:
                    results(n - 2)
                if 2 <= n <= heads:
                    gradients(n - 2)
            if with_outputs:
                for copy in outputs(k):
                    copy.start()
            gradients(heads - 1)

        bodies = (start_inputs, work) + ((wait_outputs,) if with_outputs else ())
        return [functools.partial(repeat, body) for body in bodies]

    slot0, phases = 0, []
    for group in groups:
        phases.append(of_group(*group, slot0))
        slot0 += group[2]
    for phase in zip(*phases):
        for run in phase:
            run()


def pinned(space, *arrays):
    return [pltpu.with_memory_space_constraint(array, space) for array in arrays]


HBM, VMEM = pl.BlockSpec(memory_space=pltpu.HBM), pl.BlockSpec(memory_space=pltpu.VMEM)


def attention(n_mp, blocks, groups, tokens, memory, terms, outputs, sent):
    with_outputs = outputs is not None
    rows, whole = tokens[0].shape
    width = memory[0].shape[1] // 2
    number = sum(n for _, _, n, *_ in groups)
    count = len(groups[0][3]) * memory[0].shape[0] // groups[0][2]
    used = sorted({block for block, *_ in groups})
    scratch = (width // DH, count, 2 * rows)
    earlier = [*outputs] + [sent[block] for block in used if block in sent] if with_outputs else []
    token_outs = [jax.ShapeDtypeStruct((rows, whole), bf16)] * 2
    token_outs += [jax.ShapeDtypeStruct((rows, whole // blocks), bf16)] * len(used)
    token_outs = token_outs if with_outputs else []
    first = 4 + len(memory)
    results = pl.pallas_call(
        functools.partial(attention_kernel, n_mp, blocks, groups, len(memory), with_outputs),
        in_specs=[HBM] * 4 + [VMEM] * len(memory) + [HBM] * len(earlier),
        out_specs=[HBM] * len(token_outs) + [VMEM] * len(terms),
        out_shape=token_outs
        + [pltpu.VMEM(memory[0].shape, t) for t in terms],
        scratch_shapes=[pltpu.VMEM((number, 2, 2 * rows, width), bf16)] * 2
        + [pltpu.VMEM(scratch, t) for t in (f32, f32, bf16, bf16)]
        + [pltpu.SemaphoreType.DMA((2, number, 2, 2))],
        input_output_aliases={first + n: n for n in range(len(earlier))},
        compiler_params=pltpu.CompilerParams(vmem_limit_bytes=32 * 1024 * 1024),
        cost_estimate=pl.CostEstimate(
            flops=24 * rows * count * width * number,
            bytes_accessed=16 * rows * width * number,
            transcendentals=2 * rows * count * width * number // DH,
        ),
    )(*pinned(pltpu.HBM, *tokens[:2]), *tokens[2:], *pinned(pltpu.VMEM, *memory), *earlier)
    if not with_outputs:
        return outputs, sent, results
    sent = {**sent, **dict(zip(used, results[2:]))}
    return results[:2], sent, results[2 + len(used) :]


def packing_kernel(n_mp, blocks, q_ref, g_ref, packed_q_ref, packed_g_ref, sems):
    width = packed_q_ref.shape[1] // (blocks * n_mp)
    copies = []
    for block in range(blocks):
        column = columns(n_mp, blocks, block, width, True)
        for r in range(n_mp):
            where = pl.ds((block * n_mp + r) * width, width)
            for array, packed in ((q_ref, packed_q_ref), (g_ref, packed_g_ref)):
                copies.append(
                    pltpu.make_async_copy(
                        array.at[:, pl.ds(column(r), width)], packed.at[:, where], sems.at[len(copies)]
                    )
                )
    for copy in copies:
        copy.start()
    for copy in copies:
        copy.wait()


def packing(n_mp, blocks, queries, grad):
    rows, whole = queries.shape
    return pl.pallas_call(
        functools.partial(packing_kernel, n_mp, blocks),
        in_specs=[HBM] * 2,
        out_specs=[VMEM] * 2,
        out_shape=[pltpu.VMEM((rows, whole // 2), bf16)] * 2,
        scratch_shapes=[pltpu.SemaphoreType.DMA((2 * blocks * n_mp,))],
        cost_estimate=pl.CostEstimate(flops=0, bytes_accessed=4 * rows * whole, transcendentals=0),
    )(*pinned(pltpu.HBM, queries, grad))


def joining_kernel(blocks, mine_ref, other_ref, key_ref, value_ref, sems):
    core, block = lax.axis_index("seq") & 1, mine_ref.shape[1] // (2 * blocks)
    copies = []
    for place, source in ((core, mine_ref), (1 - core, other_ref)):
        for n in range(blocks):
            where = pl.ds(pl.multiple_of((place * blocks + n) * block, block), block)
            for m, target in enumerate((key_ref, value_ref)):
                part = source.at[:, pl.ds((2 * n + m) * block, block)]
                copies.append(pltpu.make_async_copy(part, target.at[:, where], sems.at[len(copies)]))
    for copy in copies:
        copy.start()
    for copy in copies:
        copy.wait()


def joining(blocks, mine, other):
    rows, width = mine.shape
    return pl.pallas_call(
        functools.partial(joining_kernel, blocks),
        in_specs=[VMEM] * 2,
        out_specs=[HBM] * 2,
        out_shape=[jax.ShapeDtypeStruct((rows, width), bf16)] * 2,
        scratch_shapes=[pltpu.SemaphoreType.DMA((4 * blocks,))],
    )(*pinned(pltpu.VMEM, mine, other))


def placing_kernel(n_mp, blocks, *refs):
    returned_refs, (attended_ref, query_grad_ref, sems) = refs[:blocks], refs[-3:]
    width = returned_refs[0].shape[1] // (2 * n_mp)
    copies = []
    for block, returned_ref in enumerate(returned_refs):
        column = columns(n_mp, blocks, block, width, True)
        for r in range(n_mp):
            for m, target in enumerate((query_grad_ref, attended_ref)):
                start = (2 * r + m) * width
                copies.append(
                    pltpu.make_async_copy(
                        returned_ref.at[:, start : start + width],
                        target.at[:, pl.ds(column(r), width)],
                        sems.at[len(copies)],
                    )
                )
    for copy in copies:
        copy.start()
    for copy in copies:
        copy.wait()


def placing(n_mp, returned, attended, query_grad):
    blocks = len(returned)
    return pl.pallas_call(
        functools.partial(placing_kernel, n_mp, blocks),
        in_specs=[VMEM] * blocks + [HBM] * 2,
        out_specs=[HBM] * 2,
        out_shape=[jax.ShapeDtypeStruct(attended.shape, bf16)] * 2,
        scratch_shapes=[pltpu.SemaphoreType.DMA((2 * blocks * n_mp,))],
        input_output_aliases={blocks: 0, blocks + 1: 1},
    )(*pinned(pltpu.VMEM, *returned), attended, query_grad)


def together(*values):
    return lax.optimization_barrier(values)


def shards(n_seq, n_mp, queries, memory_keys, memory_values, output_grad):
    def swap(array, axis, bits):
        size = n_seq if axis == "seq" else n_mp
        return lax.ppermute(array, axis, [(i, i ^ bits) for i in range(size)])

    core_bit, x_bit = 1, 2
    z_bits = range(n_seq - 4, 0, -4)
    y_bits = [1 << b for b in range(n_mp.bit_length() - 1)]
    rows, part = memory_keys.shape
    share, blocks = part // 2, 2
    block = share // blocks
    core = lax.axis_index("seq") & 1

    def packed(keys, values):
        both = [lax.dynamic_slice_in_dim(array, core * share, share, axis=1) for array in (keys, values)]
        return jnp.concatenate([b[:, n * block : (n + 1) * block] for n in range(blocks) for b in both], axis=1)

    other = [swap(array, "seq", core_bit) for array in (memory_keys, memory_values)]
    base = jnp.concatenate([packed(memory_keys, memory_values), packed(*other)])
    base, queries_out, grad_out = together(base, queries, output_grad)
    got = [swap(base, "seq", bits) for bits in z_bits]
    tokens = (queries, output_grad)
    tokens += tuple(swap(array, "seq", core_bit) for array in packing(n_mp, blocks, queries_out, grad_out))
    got = [base] + got
    first, second = (jnp.concatenate([g[:, n * 2 * block : (n + 1) * 2 * block] for g in got]) for n in (0, 1))

    def wider(held, got):
        return jnp.concatenate([held, got])

    first_got, second_got = together(swap(first, "seq", x_bit), swap(second, "mp", y_bits[0]))
    first, second = wider(first, first_got), wider(second, second_got)
    for bits in y_bits[:-1]:
        first = wider(first, swap(first, "mp", bits))
    for bits in y_bits[1:]:
        second = wider(second, swap(second, "mp", bits))
    first_got, second_got = swap(first, "mp", y_bits[-1]), swap(second, "seq", x_bit)

    half = n_mp // 2
    outputs, sent, (first_keep,) = attention(
        n_mp, blocks, [(0, 0, half, (0,), (0,))], tokens, [first], [f32], [], {}
    )
    first_keep, second = together(first_keep, second)
    of_first = (0, half, n_mp - half, (0,))
    *_, (first_give, second_give) = attention(
        n_mp,
        blocks,
        [(*of_first, (0,)), (1, 0, n_mp, (1, 2), (None, 1))],
        tokens,
        [first_got, second, second_got],
        [bf16, bf16],
        None,
        {},
    )
    outputs, sent, (second_keep,) = attention(
        n_mp, blocks, [(1, 0, n_mp, (0, 1), (0, None))], tokens, [second, second_got], [f32], outputs, sent
    )
    first_terms, second_terms = swap(first_give, "mp", y_bits[-1]), swap(second_give, "seq", x_bit)
    first, second, sent[1], first_got = together(
        first_keep + first_terms.astype(f32), second_keep + second_terms.astype(f32), sent[1], first_got
    )
    outputs, sent, _ = attention(n_mp, blocks, [(*of_first, ())], tokens, [first_got], [], outputs, sent)

    def fold(total, axis, bits):
        middle = total.shape[0] // 2
        return total[:middle] + swap(total[middle:].astype(bf16), axis, bits).astype(f32)

    for bits in y_bits[-2::-1]:
        first = fold(first, "mp", bits)
    for bits in y_bits[:0:-1]:
        second = fold(second, "mp", bits)
    first, second = fold(first, "seq", x_bit), fold(second, "mp", y_bits[0])
    returned = [swap(sent[block], "seq", core_bit) for block in range(blocks)]
    first, second, returned[1] = together(first, second, returned[1])
    total = jnp.concatenate([first, second], axis=1)
    outputs = placing(n_mp, returned, *outputs)
    count, give = 2 * rows, total.astype(bf16)
    got = [swap(give[n * count : (n + 1) * count], "seq", bits) for n, bits in enumerate(z_bits, 1)]
    got, outputs = together(got, outputs)
    total = (total[:count] + sum(g.astype(f32) for g in got)).astype(bf16)
    mine, other = total[:rows], swap(total[rows:], "seq", core_bit)

    return (*outputs, *joining(blocks, mine, other))


def solution(mesh):
    body = functools.partial(shards, mesh.shape["seq"], mesh.shape["mp"])
    return jax.shard_map(
        body,
        mesh=mesh,
        in_specs=(P(("seq", "mp"), None), P("seq", "mp"), P("seq", "mp"), P(("seq", "mp"), None)),
        out_specs=(P(("seq", "mp"), None), P(("seq", "mp"), None), P("seq", "mp"), P("seq", "mp")),
        check_vma=False,
    )
```

```python
import functools
import math

import jax
import jax.numpy as jnp
from jax import lax
from jax.experimental import pallas as pl
from jax.experimental.pallas import tpu as pltpu
from jax.sharding import PartitionSpec as P

DH = 128

NT = (((1,), (1,)), ((), ()))
NN = (((1,), (0,)), ((), ()))

bf16, f32 = jnp.bfloat16, jnp.float32


def dot(a, b, dims):
    return lax.dot_general(a, b, dims, preferred_element_type=f32)


def softmax_part(raw, prob_grad):
    temper = 1.0 / math.sqrt(DH)
    peak = jnp.max(raw, axis=0, keepdims=True)
    powers = jnp.exp((raw - peak) * temper)
    inverse = 1.0 / jnp.sum(powers, axis=0, keepdims=True)
    delta = jnp.sum(powers * prob_grad, axis=0, keepdims=True) * inverse
    weights = (powers * inverse).astype(bf16)
    score_grad = (powers * (inverse * temper) * (prob_grad - delta)).astype(bf16)
    return score_grad, weights


def columns(n_mp, blocks, block, width, of_sibling):
    core, my = lax.axis_index("seq") & 1, lax.axis_index("mp")
    core = 1 - core if of_sibling else core
    return lambda r: pl.multiple_of((((my ^ r) * 2 + core) * blocks + block) * width, width)


def attention_kernel(n_mp, blocks, groups, n_memory, with_outputs, q_ref, g_ref, sq_ref, sg_ref, *refs):
    used = sorted({block for block, *_ in groups})
    memory_refs, refs = refs[:n_memory], refs[n_memory:]
    token_buf, result_buf, raw_ref, prob_ref, grad_ref, weight_ref, sems = refs[-7:]
    n_terms = max([1 + t for *_, terms in groups for t in terms if t is not None], default=0)
    term_refs, refs = refs[len(refs) - 7 - n_terms : -7], refs[: len(refs) - 7 - n_terms]
    if with_outputs:
        attended_ref, query_grad_ref, *sent_refs = refs[-2 - len(used) :]
    count, width = q_ref.shape[0], memory_refs[0].shape[1] // 2
    heads = width // DH
    step = min(DH, 2 * count)
    cols = [slice(n * DH, (n + 1) * DH) for n in range(heads)]
    targets = [[slice(m * width + n * DH, m * width + (n + 1) * DH) for n in range(heads)] for m in (0, 1)]

    def of_group(block, r0, number, memories, terms, slot0):
        column = columns(n_mp, blocks, block, width, False)
        size = memory_refs[memories[0]].shape[0] // number
        sent_ref = sent_refs[used.index(block)] if with_outputs else None

        def inputs(k):
            starts = (column(r0 + k), pl.multiple_of((block * n_mp + r0 + k) * width, width))
            return [
                pltpu.make_async_copy(
                    array.at[:, pl.ds(start, width)],
                    token_buf.at[slot0 + k, m, pl.ds(n * count, count)],
                    sems.at[0, slot0 + k, m, n],
                )
                for m, pair in enumerate(((q_ref, sq_ref), (g_ref, sg_ref)))
                for n, (array, start) in enumerate(zip(pair, starts))
            ]

        def outputs(k):
            copies = []
            for m, own in enumerate((query_grad_ref, attended_ref)):
                starts = (column(r0 + k), pl.multiple_of((2 * (r0 + k) + m) * width, width))
                for n, (array, start) in enumerate(zip((own, sent_ref), starts)):
                    copies.append(
                        pltpu.make_async_copy(
                            result_buf.at[slot0 + k, m, pl.ds(n * count, count)],
                            array.at[:, pl.ds(start, width)],
                            sems.at[1, slot0 + k, m, n],
                        )
                    )
            return copies

        def repeat(body):
            if number == 1:
                body(0, None)
            else:
                lax.fori_loop(0, number, body, None)

        def start_inputs(k, _):
            for copy in inputs(k):
                copy.start()

        def wait_outputs(k, _):
            for copy in outputs(k):
                copy.wait()

        def work(k, _):
            rows = pl.ds(pl.multiple_of(k * size, size), size)
            memory = [
                [jnp.concatenate([memory_refs[i][rows, t] for i in memories], axis=0) for t in row] for row in targets
            ]

            def tokens(m, n):
                return token_buf[slot0 + k, m, :, cols[n]]

            def scores(n):
                raw_ref[n] = dot(memory[0][n], tokens(0, n), NT)
                prob_ref[n] = dot(memory[1][n], tokens(1, n), NT)

            def softmax(n):
                for begin in range(0, 2 * count, step):
                    part = slice(begin, begin + step)
                    grad_ref[n, :, part], weight_ref[n, :, part] = softmax_part(
                        raw_ref[n, :, part], prob_ref[n, :, part]
                    )

            def results(n):
                for m, pair_ref in enumerate((grad_ref, weight_ref)):
                    result = dot(memory[m][n].T, pair_ref[n], NN).astype(bf16)
                    result_buf[slot0 + k, m, :, cols[n]] = result.T

            def gradients(n):
                for m, pair_ref in enumerate((grad_ref, weight_ref) if terms else ()):
                    if None not in terms:
                        whole = dot(pair_ref[n], tokens(m, n), NN)
                    for i, t in enumerate(terms):
                        if t is None:
                            continue
                        part = slice(i * size, (i + 1) * size)
                        term = dot(pair_ref[n, part], tokens(m, n), NN) if None in terms else whole[part]
                        term_refs[t][rows, targets[m][n]] = term.astype(term_refs[t].dtype)

            for copy in inputs(k):
                copy.wait()
            for n in range(heads + 2):
                if n < heads:
                    scores(n)
                if 1 <= n <= heads:
                    softmax(n - 1)
                if n >= 2 and with_outputs:
                    results(n - 2)
                if 2 <= n <= heads:
                    gradients(n - 2)
            if with_outputs:
                for copy in outputs(k):
                    copy.start()
            gradients(heads - 1)

        bodies = (start_inputs, work) + ((wait_outputs,) if with_outputs else ())
        return [functools.partial(repeat, body) for body in bodies]

    slot0, phases = 0, []
    for group in groups:
        phases.append(of_group(*group, slot0))
        slot0 += group[2]
    for phase in zip(*phases):
        for run in phase:
            run()


def pinned(space, *arrays):
    return [pltpu.with_memory_space_constraint(array, space) for array in arrays]


HBM, VMEM = pl.BlockSpec(memory_space=pltpu.HBM), pl.BlockSpec(memory_space=pltpu.VMEM)


def attention(n_mp, blocks, groups, tokens, memory, terms, outputs, sent):
    with_outputs = outputs is not None
    rows, whole = tokens[0].shape
    width = memory[0].shape[1] // 2
    number = sum(n for _, _, n, *_ in groups)
    count = len(groups[0][3]) * memory[0].shape[0] // groups[0][2]
    used = sorted({block for block, *_ in groups})
    scratch = (width // DH, count, 2 * rows)
    earlier = [*outputs] + [sent[block] for block in used if block in sent] if with_outputs else []
    token_outs = [jax.ShapeDtypeStruct((rows, whole), bf16)] * 2
    token_outs += [jax.ShapeDtypeStruct((rows, whole // blocks), bf16)] * len(used)
    token_outs = token_outs if with_outputs else []
    first = 4 + len(memory)
    results = pl.pallas_call(
        functools.partial(attention_kernel, n_mp, blocks, groups, len(memory), with_outputs),
        in_specs=[HBM] * 4 + [VMEM] * len(memory) + [HBM] * len(earlier),
        out_specs=[HBM] * len(token_outs) + [VMEM] * len(terms),
        out_shape=token_outs
        + [pltpu.VMEM(memory[0].shape, t) for t in terms],
        scratch_shapes=[pltpu.VMEM((number, 2, 2 * rows, width), bf16)] * 2
        + [pltpu.VMEM(scratch, t) for t in (f32, f32, bf16, bf16)]
        + [pltpu.SemaphoreType.DMA((2, number, 2, 2))],
        input_output_aliases={first + n: n for n in range(len(earlier))},
        compiler_params=pltpu.CompilerParams(vmem_limit_bytes=32 * 1024 * 1024),
        cost_estimate=pl.CostEstimate(
            flops=24 * rows * count * width * number,
            bytes_accessed=16 * rows * width * number,
            transcendentals=2 * rows * count * width * number // DH,
        ),
    )(*pinned(pltpu.HBM, *tokens[:2]), *tokens[2:], *pinned(pltpu.VMEM, *memory), *earlier)
    if not with_outputs:
        return outputs, sent, results
    sent = {**sent, **dict(zip(used, results[2:]))}
    return results[:2], sent, results[2 + len(used) :]


def packing_kernel(n_mp, blocks, q_ref, g_ref, packed_q_ref, packed_g_ref, sems):
    width = packed_q_ref.shape[1] // (blocks * n_mp)
    copies = []
    for block in range(blocks):
        column = columns(n_mp, blocks, block, width, True)
        for r in range(n_mp):
            where = pl.ds((block * n_mp + r) * width, width)
            for array, packed in ((q_ref, packed_q_ref), (g_ref, packed_g_ref)):
                copies.append(
                    pltpu.make_async_copy(
                        array.at[:, pl.ds(column(r), width)], packed.at[:, where], sems.at[len(copies)]
                    )
                )
    for copy in copies:
        copy.start()
    for copy in copies:
        copy.wait()


def packing(n_mp, blocks, queries, grad):
    rows, whole = queries.shape
    return pl.pallas_call(
        functools.partial(packing_kernel, n_mp, blocks),
        in_specs=[HBM] * 2,
        out_specs=[VMEM] * 2,
        out_shape=[pltpu.VMEM((rows, whole // 2), bf16)] * 2,
        scratch_shapes=[pltpu.SemaphoreType.DMA((2 * blocks * n_mp,))],
        cost_estimate=pl.CostEstimate(flops=0, bytes_accessed=4 * rows * whole, transcendentals=0),
    )(*pinned(pltpu.HBM, queries, grad))


def joining_kernel(blocks, mine_ref, other_ref, key_ref, value_ref, sems):
    core, block = lax.axis_index("seq") & 1, mine_ref.shape[1] // (2 * blocks)
    copies = []
    for place, source in ((core, mine_ref), (1 - core, other_ref)):
        for n in range(blocks):
            where = pl.ds(pl.multiple_of((place * blocks + n) * block, block), block)
            for m, target in enumerate((key_ref, value_ref)):
                part = source.at[:, pl.ds((2 * n + m) * block, block)]
                copies.append(pltpu.make_async_copy(part, target.at[:, where], sems.at[len(copies)]))
    for copy in copies:
        copy.start()
    for copy in copies:
        copy.wait()


def joining(blocks, mine, other):
    rows, width = mine.shape
    return pl.pallas_call(
        functools.partial(joining_kernel, blocks),
        in_specs=[VMEM] * 2,
        out_specs=[HBM] * 2,
        out_shape=[jax.ShapeDtypeStruct((rows, width), bf16)] * 2,
        scratch_shapes=[pltpu.SemaphoreType.DMA((4 * blocks,))],
    )(*pinned(pltpu.VMEM, mine, other))


def placing_kernel(n_mp, blocks, *refs):
    returned_refs, (attended_ref, query_grad_ref, sems) = refs[:blocks], refs[-3:]
    width = returned_refs[0].shape[1] // (2 * n_mp)
    copies = []
    for block, returned_ref in enumerate(returned_refs):
        column = columns(n_mp, blocks, block, width, True)
        for r in range(n_mp):
            for m, target in enumerate((query_grad_ref, attended_ref)):
                start = (2 * r + m) * width
                copies.append(
                    pltpu.make_async_copy(
                        returned_ref.at[:, start : start + width],
                        target.at[:, pl.ds(column(r), width)],
                        sems.at[len(copies)],
                    )
                )
    for copy in copies:
        copy.start()
    for copy in copies:
        copy.wait()


def placing(n_mp, returned, attended, query_grad):
    blocks = len(returned)
    return pl.pallas_call(
        functools.partial(placing_kernel, n_mp, blocks),
        in_specs=[VMEM] * blocks + [HBM] * 2,
        out_specs=[HBM] * 2,
        out_shape=[jax.ShapeDtypeStruct(attended.shape, bf16)] * 2,
        scratch_shapes=[pltpu.SemaphoreType.DMA((2 * blocks * n_mp,))],
        input_output_aliases={blocks: 0, blocks + 1: 1},
    )(*pinned(pltpu.VMEM, *returned), attended, query_grad)


def together(*values):
    return lax.optimization_barrier(values)


def shards(n_seq, n_mp, queries, memory_keys, memory_values, output_grad):
    def swap(array, axis, bits):
        size = n_seq if axis == "seq" else n_mp
        return lax.ppermute(array, axis, [(i, i ^ bits) for i in range(size)])

    core_bit, x_bit = 1, 2
    z_bits = range(n_seq - 4, 0, -4)
    y_bits = [1 << b for b in range(n_mp.bit_length() - 1)]
    rows, part = memory_keys.shape
    share, blocks = part // 2, 2
    block = share // blocks
    core = lax.axis_index("seq") & 1

    def packed(keys, values):
        both = [lax.dynamic_slice_in_dim(array, core * share, share, axis=1) for array in (keys, values)]
        return jnp.concatenate([b[:, n * block : (n + 1) * block] for n in range(blocks) for b in both], axis=1)

    other = [swap(array, "seq", core_bit) for array in (memory_keys, memory_values)]
    base = jnp.concatenate([packed(memory_keys, memory_values), packed(*other)])
    base, queries_out, grad_out = together(base, queries, output_grad)
    got = [swap(base, "seq", bits) for bits in z_bits]
    tokens = (queries, output_grad)
    tokens += tuple(swap(array, "seq", core_bit) for array in packing(n_mp, blocks, queries_out, grad_out))
    got = [base] + got
    first, second = (jnp.concatenate([g[:, n * 2 * block : (n + 1) * 2 * block] for g in got]) for n in (0, 1))

    def wider(held, got):
        return jnp.concatenate([held, got])

    first_got, second_got = together(swap(first, "seq", x_bit), swap(second, "mp", y_bits[0]))
    first, second = wider(first, first_got), wider(second, second_got)
    for bits in y_bits[:-1]:
        first = wider(first, swap(first, "mp", bits))
    for bits in y_bits[1:]:
        second = wider(second, swap(second, "mp", bits))
    second_got, first_got = swap(second, "seq", x_bit), swap(first, "mp", y_bits[-1])

    half = n_mp // 2
    outputs, sent, (first_keep,) = attention(
        n_mp, blocks, [(0, 0, half, (0,), (0,))], tokens, [first], [f32], [], {}
    )
    first_keep, second = together(first_keep, second)
    of_first = (0, half, n_mp - half, (0,))
    *_, (first_give, second_give) = attention(
        n_mp,
        blocks,
        [(*of_first, (0,)), (1, 0, n_mp, (1, 2), (None, 1))],
        tokens,
        [first_got, second, second_got],
        [bf16, bf16],
        None,
        {},
    )
    outputs, sent, (second_keep,) = attention(
        n_mp, blocks, [(1, 0, n_mp, (0, 1), (0, None))], tokens, [second, second_got], [f32], outputs, sent
    )
    first_terms, second_terms = swap(first_give, "mp", y_bits[-1]), swap(second_give, "seq", x_bit)
    first, second, sent[1], first_got = together(
        first_keep + first_terms.astype(f32), second_keep + second_terms.astype(f32), sent[1], first_got
    )
    outputs, sent, _ = attention(n_mp, blocks, [(*of_first, ())], tokens, [first_got], [], outputs, sent)

    def fold(total, axis, bits):
        middle = total.shape[0] // 2
        return total[:middle] + swap(total[middle:].astype(bf16), axis, bits).astype(f32)

    for bits in y_bits[-2::-1]:
        first = fold(first, "mp", bits)
    for bits in y_bits[:0:-1]:
        second = fold(second, "mp", bits)
    first, second = fold(first, "seq", x_bit), fold(second, "mp", y_bits[0])
    returned = [swap(sent[block], "seq", core_bit) for block in range(blocks)]
    first, second, returned[1] = together(first, second, returned[1])
    total = jnp.concatenate([first, second], axis=1)
    outputs = placing(n_mp, returned, *outputs)
    count, give = 2 * rows, total.astype(bf16)
    got = [swap(give[n * count : (n + 1) * count], "seq", bits) for n, bits in enumerate(z_bits, 1)]
    got, outputs = together(got, outputs)
    total = (total[:count] + sum(g.astype(f32) for g in got)).astype(bf16)
    mine, other = total[:rows], swap(total[rows:], "seq", core_bit)

    return (*outputs, *joining(blocks, mine, other))


def solution(mesh):
    body = functools.partial(shards, mesh.shape["seq"], mesh.shape["mp"])
    return jax.shard_map(
        body,
        mesh=mesh,
        in_specs=(P(("seq", "mp"), None), P("seq", "mp"), P("seq", "mp"), P(("seq", "mp"), None)),
        out_specs=(P(("seq", "mp"), None), P(("seq", "mp"), None), P("seq", "mp"), P("seq", "mp")),
        check_vma=False,
    )
```
